32 devices in a mesh: wide: 8 (over y, x, core), narrow: 4 (over z).
Axes of the slice: x: 2, y: 2, z: 4, core: 2. Of those that a mesh axis runs over, the one named last changes fastest.
Arguments:
- amplitudes: bfloat16 [2048, 1024], P('narrow'), may hold values from -6 to 6
- integrals: bfloat16 [64, 128, 128], P('wide', 'narrow'), may hold values from -0.5 to 0.5
- in_tile: int32 [64], P('wide'), may hold values from 0 to 7
- counts: int32 [8], P('wide'), may hold values from 1 to 8, as said below
- out_tile: int32 [64], P('wide'), may hold values from 0 to 15, as said below
- owner_map: int32 [16], replicated, may hold values from 0 to 15, as said below
Outputs:
- residual: float32 [2048, 2048], P('narrow', 'wide')
The draws below stay inside these ranges and needn't reach their ends.
Inputs may be any that keep to these rules, and one draw needn't show every extreme that they name: `counts`: some home device has exactly 8 live tasks in every draw. `out_tile`: call device owner_map[t] // 2 the owner of tile t. The 8 slots of one home device have tiles of pairwise different owners, and the live tasks of all homes give one owner at most 4 tasks; some owner receives exactly 4 in every draw. `owner_map`: A permutation of the residual tiles.
All inputs are finite; a program needn't handle non-finite values.
Results may differ from the reference program's by a relative error of at most 0.0029.
Values may be sent and summed in bfloat16 or wider, within the bound.
No kernel may reach another device: no remote copies, remote signals or barrier semaphores. Data moves between devices by JAX's collectives and lax.ppermute only.
A program may use at most 64 MiB of HBM per device.

```python
import jax
import jax.numpy as jnp
from jax import lax

TILE = 128
KT = 8
OWN = 2
HOLD = 8
RECV = 4
ROWS = 2048
TASKS = 64
NOUT = 16


def plan_draw(key):
    homes = TASKS // HOLD
    half = RECV
    owner_perm = jax.random.permutation(jax.random.fold_in(key, 101), NOUT).astype(jnp.int32)
    inverse = jnp.zeros((NOUT,), jnp.int32).at[owner_perm].set(jnp.arange(NOUT, dtype=jnp.int32))
    order = jax.random.permutation(jax.random.fold_in(key, 102), homes).astype(jnp.int32)
    first = order[:homes // 2]
    second = order[homes // 2:]
    spread = jax.random.randint(jax.random.fold_in(key, 103), (homes // 2,), 0, half - 1).astype(jnp.int32)
    first_counts = (half + spread).at[0].set(HOLD)
    second_counts = (half - 1 - spread).at[0].set(1)
    live_counts = jnp.zeros((homes,), jnp.int32).at[first].set(first_counts).at[second].set(second_counts)
    starts = jnp.cumsum(live_counts) - live_counts
    slot_ids = jnp.arange(HOLD, dtype=jnp.int32)[None, :]
    target = (starts[:, None] + slot_ids) % homes
    local_slot = jax.random.randint(jax.random.fold_in(key, 105), (homes, HOLD), 0, OWN).astype(jnp.int32)
    out_ids = inverse[target * OWN + local_slot].reshape(TASKS)
    return (live_counts, out_ids, owner_perm)


def draw_counts(key, part):
    return plan_draw(key)[0]


def draw_out_tile(key, part):
    return plan_draw(key)[1]


def draw_owner_map(key, part):
    return plan_draw(key)[2]


def with_ends(drawn, key, least, high):
    shape = drawn.shape
    spot = [jax.random.randint(jax.random.fold_in(key, axis), (), 0, shape[axis]) for axis in range(len(shape))]
    drawn = drawn.at[tuple(spot)].set(least)
    longest = shape.index(max(shape))
    spot[longest] = (spot[longest] + 1) % shape[longest]
    return drawn.at[tuple(spot)].set(high)


def levels(key, dims, cuts, smallest, top_value):
    def one(axis_at, blocks):
        steps = jax.random.uniform(jax.random.fold_in(jax.random.fold_in(key, 6), axis_at), (blocks,), jnp.float32, smallest / len(cuts), top_value / len(cuts))
        return jnp.repeat(jnp.exp(steps), dims[axis_at] // blocks).reshape((-1,) + (1,) * (len(dims) - axis_at - 1))

    gain = one(*cuts[0])
    for cut in cuts[1:]:
        gain = gain * one(*cut)
    return gain


def centred(key, shape, scale, reach, cuts=(), kind=jnp.bfloat16):
    array = jax.random.normal(key, shape, jnp.float32) * scale
    if len(cuts) > 0:
        array = levels(key, shape, cuts, -0.22, 0.18) * array
    return jnp.clip(array, min=-reach, max=reach).astype(kind)


def setup_inputs(seed: int = 0) -> dict:
    key_of = jax.random.split(jax.random.key(seed), 7)
    return {
        "amplitudes": centred(key_of[0], (ROWS, KT * TILE), 1.0, 6.0, ((0, 4),)),
        "integrals": centred(key_of[1], (TASKS, TILE, TILE), TILE ** -0.5, 0.5, ((0, 8), (1, 4))),
        "in_tile": with_ends(jax.random.randint(key_of[2], (TASKS,), 0, KT), jax.random.fold_in(key_of[2], 1), 0, KT - 1).astype(jnp.int32),
        "counts": draw_counts(jax.random.fold_in(key_of[6], 71), 0),
        "out_tile": draw_out_tile(jax.random.fold_in(key_of[6], 71), 0),
        "owner_map": draw_owner_map(jax.random.fold_in(key_of[6], 71), 0),
    }


def reference(amplitudes, integrals, in_tile, counts, out_tile, owner_map):
    amp_blocks = amplitudes.reshape(ROWS, KT, TILE)

    def add_task(running, task_index):
        is_live = (task_index % HOLD) < counts[task_index // HOLD]

        def compute(_):
            columns = lax.dynamic_index_in_dim(amp_blocks, in_tile[task_index].astype(jnp.int32), 1, keepdims=False)
            integral_tile = lax.dynamic_index_in_dim(integrals, task_index, 0, keepdims=False)
            product = jnp.dot(columns, integral_tile, preferred_element_type=jnp.float32).astype(jnp.bfloat16)
            product = lax.optimization_barrier(product)
            return product.astype(jnp.float32)

        def skipped(_):
            return jnp.zeros((ROWS, TILE), jnp.float32)

        product = lax.cond(is_live, compute, skipped, 0)
        place_at = owner_map[out_tile[task_index]].astype(jnp.int32)
        current = lax.dynamic_index_in_dim(running, place_at, 0, keepdims=False)
        running = lax.dynamic_update_index_in_dim(running, current + product, place_at, 0)
        return running, 0

    start_sum = jnp.zeros((NOUT, ROWS, TILE), jnp.float32)
    running, _ = lax.scan(add_task, start_sum, jnp.arange(TASKS, dtype=jnp.int32))
    return jnp.transpose(running, (1, 0, 2)).reshape(ROWS, NOUT * TILE)
```

```python
import functools

import jax
import jax.numpy as jnp
from jax import lax
from jax.experimental import pallas as pl
from jax.experimental.pallas import tpu as pltpu
from jax.sharding import PartitionSpec as P

META = 16


def pack_kernel(own_count, in_tile, counts, out_tile, owner_map, rows_ref, out_ref, slab, sems):
    slot_count, row_count, _ = rows_ref.shape
    depth_count = out_ref.shape[1]
    slab[...] = jnp.zeros_like(slab)
    upper = lax.broadcasted_iota(jnp.int32, (META, slab.shape[2]), 0) < META // 2

    def place(h, _):
        spot = owner_map[out_tile[h]]
        owner = lax.div(spot, own_count)
        code = jnp.where(h < counts[0], lax.rem(spot, own_count) + 1, 0)
        slab[owner, :row_count] = rows_ref[h]
        slab[owner, row_count:] = jnp.where(
            upper, code.astype(jnp.float32), in_tile[h].astype(jnp.float32)
        ).astype(slab.dtype)
        return 0

    lax.fori_loop(0, slot_count, place, 0, unroll=slot_count <= 8)
    copies = [
        pltpu.make_async_copy(slab, out_ref.at[:, z], sems.at[z]) for z in range(depth_count)
    ]
    for copy in copies:
        copy.start()
    for copy in copies:
        copy.wait()


def ladder_kernel(rows, amp_ref, got_ref, out_ref, column, place, source):
    wide_count, depth_count, _, width = got_ref.shape
    padded = got_ref.shape[2] - META

    def list_live(w, found):
        meta = got_ref[w, 0, padded:].astype(jnp.float32)
        code = jnp.max(meta[: META // 2]).astype(jnp.int32)
        tile = jnp.max(meta[META // 2 :]).astype(jnp.int32)

        @pl.when(code > 0)
        def _():
            source[found] = w
            column[found] = tile
            place[found] = code - 1

        return found + (code > 0).astype(jnp.int32)

    live = lax.fori_loop(0, wide_count, list_live, jnp.int32(0), unroll=wide_count <= 8)
    out_ref[...] = jnp.zeros_like(out_ref)

    def add_task(u, _):
        if rows == padded:
            tile = got_ref[source[u], :, :padded].reshape(depth_count * rows, width)
        else:
            tile = got_ref[source[u], :, :padded].astype(jnp.float32)[:, :rows]
            tile = tile.reshape(depth_count * rows, width).astype(got_ref.dtype)
        columns = amp_ref[:, pl.ds(pl.multiple_of(column[u] * width, width), width)]
        spot = pl.ds(pl.multiple_of(place[u] * width, width), width)
        out_ref[:, spot] += jnp.dot(columns, tile, preferred_element_type=jnp.float32)
        return 0

    lax.fori_loop(0, live, add_task, 0)


def shards(amplitudes, integrals, in_tile, counts, out_tile, owner_map):
    slot_count, rows, width = integrals.shape
    wide_count = lax.axis_size("wide")
    depth_count = lax.axis_size("narrow")
    own_count = owner_map.shape[0] // wide_count
    padded = -(-rows // META) * META
    if padded != rows:
        integrals = jnp.pad(integrals, ((0, 0), (0, padded - rows), (0, 0)))
    length = padded + META
    smem = pl.BlockSpec(memory_space=pltpu.SMEM)
    vmem = pl.BlockSpec(memory_space=pltpu.VMEM)
    send = pl.pallas_call(
        functools.partial(pack_kernel, own_count),
        out_shape=jax.ShapeDtypeStruct((wide_count, depth_count, length, width), integrals.dtype),
        in_specs=[smem] * 4 + [vmem],
        out_specs=pl.BlockSpec(memory_space=pl.ANY),
        scratch_shapes=[
            pltpu.VMEM((wide_count, length, width), integrals.dtype),
            pltpu.SemaphoreType.DMA((depth_count,)),
        ],
        name="pack",
    )(in_tile, counts, out_tile, owner_map, integrals)
    got = lax.all_to_all(
        send.reshape(wide_count * depth_count, length, width),
        ("wide", "narrow"),
        split_axis=0,
        concat_axis=0,
        tiled=True,
    ).reshape(wide_count, depth_count, length, width)
    return pl.pallas_call(
        functools.partial(ladder_kernel, rows),
        out_shape=jax.ShapeDtypeStruct((amplitudes.shape[0], own_count * width), jnp.float32),
        in_specs=[vmem, vmem],
        out_specs=vmem,
        scratch_shapes=[pltpu.SMEM((wide_count,), jnp.int32)] * 3,
        compiler_params=pltpu.CompilerParams(vmem_limit_bytes=32 * 2**20),
        name="ladder",
    )(amplitudes, got)


def solution(mesh):
    return jax.shard_map(
        shards,
        mesh=mesh,
        in_specs=(
            P("narrow", None),
            P("wide", "narrow", None),
            P("wide"),
            P("wide"),
            P("wide"),
            P(),
        ),
        out_specs=P("narrow", "wide"),
        check_vma=False,
    )
```

```python
import functools

import jax
import jax.numpy as jnp
from jax import lax
from jax.experimental import pallas as pl
from jax.experimental.pallas import tpu as pltpu
from jax.sharding import PartitionSpec as P

META = 16


def pack_kernel(own_count, in_tile, counts, out_tile, owner_map, rows_ref, *outs_and_slab):
    *out_refs, slab = outs_and_slab
    slot_count, row_count, width = rows_ref.shape
    wide_count = len(out_refs)
    me = lax.axis_index("wide")
    slab[...] = jnp.zeros_like(slab)
    upper = lax.broadcasted_iota(jnp.int32, (META, width), 0) < META // 2

    def place(h, _):
        spot = owner_map[out_tile[h]]
        owner = lax.div(spot, own_count)
        step = lax.rem(owner - me + wide_count, wide_count)
        code = jnp.where(h < counts[0], lax.rem(spot, own_count) + 1, 0)
        slab[step, :row_count] = rows_ref[h]
        slab[step, row_count:] = jnp.where(
            upper, code.astype(jnp.float32), in_tile[h].astype(jnp.float32)
        ).astype(slab.dtype)
        return 0

    lax.fori_loop(0, slot_count, place, 0, unroll=slot_count <= 8)
    for step, out_ref in enumerate(out_refs):
        out_ref[...] = slab[step]


def compact_kernel(*refs):
    *got_refs, tiles_ref, column, place = refs
    recv_count, padded, _ = tiles_ref.shape
    tiles_ref[...] = jnp.zeros_like(tiles_ref)
    for u in range(recv_count):
        column[u] = 0
        place[u] = -1
    found = jnp.int32(0)
    for got_ref in got_refs:
        meta = got_ref[padded:].astype(jnp.float32)
        code = jnp.max(meta[: META // 2]).astype(jnp.int32)
        tile = jnp.max(meta[META // 2 :]).astype(jnp.int32)

        @pl.when((code > 0) & (found < recv_count))
        def _():
            tiles_ref[found] = got_ref[:padded]
            column[found] = tile
            place[found] = code - 1

        found += (code > 0).astype(jnp.int32)


def ladder_kernel(rows, column, place, amp_ref, *refs):
    *got_refs, out_ref, tiles = refs
    recv_count, padded, width = got_refs[0].shape
    depth_count = len(got_refs)
    me = lax.axis_index("narrow")
    for step, got_ref in enumerate(got_refs):
        depth = lax.rem(me - step + depth_count, depth_count)
        spot = pl.ds(pl.multiple_of(depth * rows, rows), rows)
        tiles[:, spot] = got_ref[...].astype(tiles.dtype)[:, :rows]
    out_ref[...] = jnp.zeros_like(out_ref)

    def add_task(u, _):
        @pl.when(place[u] >= 0)
        def _():
            columns = amp_ref[:, pl.ds(pl.multiple_of(column[u] * width, width), width)]
            spot = pl.ds(pl.multiple_of(place[u] * width, width), width)
            out_ref[:, spot] += jnp.dot(
                columns, tiles[u].astype(amp_ref.dtype), preferred_element_type=jnp.float32
            )

        return 0

    lax.fori_loop(0, recv_count, add_task, 0)


def shift(value, axis, step):
    count = lax.axis_size(axis)
    return lax.ppermute(value, axis, [(d, (d + step) % count) for d in range(count)])


def shards(amplitudes, integrals, in_tile, counts, out_tile, owner_map):
    slot_count, rows, width = integrals.shape
    wide_count = lax.axis_size("wide")
    depth_count = lax.axis_size("narrow")
    own_count = owner_map.shape[0] // wide_count
    recv_count = slot_count // 2
    padded = -(-rows // META) * META
    if padded != rows:
        integrals = jnp.pad(integrals, ((0, 0), (0, padded - rows), (0, 0)))
    kind = integrals.dtype
    smem = pl.BlockSpec(memory_space=pltpu.SMEM)
    vmem = pl.BlockSpec(memory_space=pltpu.VMEM)
    sent = pl.pallas_call(
        functools.partial(pack_kernel, own_count),
        out_shape=[jax.ShapeDtypeStruct((padded + META, width), kind)] * wide_count,
        in_specs=[smem] * 4 + [vmem],
        out_specs=[vmem] * wide_count,
        scratch_shapes=[pltpu.VMEM((wide_count, padded + META, width), kind)],
        name="pack",
    )(in_tile, counts, out_tile, owner_map, integrals)
    got = [sent[0]] + [shift(sent[step], "wide", step) for step in range(1, wide_count)]
    tiles, column, place = pl.pallas_call(
        compact_kernel,
        out_shape=[
            jax.ShapeDtypeStruct((recv_count, padded, width), kind),
            jax.ShapeDtypeStruct((recv_count,), jnp.int32),
            jax.ShapeDtypeStruct((recv_count,), jnp.int32),
        ],
        in_specs=[vmem] * wide_count,
        out_specs=[vmem, smem, smem],
        name="compact",
    )(*got)
    parts = [tiles] + [shift(tiles, "narrow", step) for step in range(1, depth_count)]
    whole_kind = kind if rows % META == 0 else jnp.float32
    return pl.pallas_call(
        functools.partial(ladder_kernel, rows),
        out_shape=jax.ShapeDtypeStruct((amplitudes.shape[0], own_count * width), jnp.float32),
        in_specs=[smem, smem, vmem] + [vmem] * depth_count,
        out_specs=vmem,
        scratch_shapes=[pltpu.VMEM((recv_count, depth_count * rows, width), whole_kind)],
        compiler_params=pltpu.CompilerParams(vmem_limit_bytes=32 * 2**20),
        name="ladder",
    )(column, place, amplitudes, *parts)


def solution(mesh):
    return jax.shard_map(
        shards,
        mesh=mesh,
        in_specs=(
            P("narrow", None),
            P("wide", "narrow", None),
            P("wide"),
            P("wide"),
            P("wide"),
            P(),
        ),
        out_specs=P("narrow", "wide"),
        check_vma=False,
    )
```

```python
import functools

import jax
import jax.numpy as jnp
from jax import lax
from jax.experimental import pallas as pl
from jax.experimental.pallas import tpu as pltpu
from jax.sharding import PartitionSpec as P

META = 8
GROUP = 4


def pack_kernel(own_count, hbm_in, hbm_counts, hbm_out, hbm_map, hbm_rows, send_ref, *scratch):
    in_tile, counts, out_tile, owner_map, rows, sems = scratch
    pairs = [
        (hbm_out, out_tile),
        (hbm_map, owner_map),
        (hbm_counts, counts),
        (hbm_in, in_tile),
        (hbm_rows, rows),
    ]
    copies = [
        pltpu.make_async_copy(source, target, sems.at[i])
        for i, (source, target) in enumerate(pairs)
    ]
    for copy in copies:
        copy.start()
    slot_count, row_count, width = rows.shape
    wide_count, depth_count = send_ref.shape[:2]
    if slot_count != wide_count:
        send_ref[...] = jnp.zeros_like(send_ref)
    for copy in copies:
        copy.wait()

    def place(h, _):
        spot = owner_map[out_tile[h]]
        owner = lax.div(spot, own_count)
        label = in_tile[h] * own_count + lax.rem(spot, own_count) + 1
        label = jnp.where(h < counts[0], label, 0).astype(jnp.float32)
        block = rows[h].astype(jnp.float32)
        meta = jnp.full((META, width), label, jnp.float32)
        message = jnp.concatenate([block, meta], axis=0).astype(send_ref.dtype)
        for z in range(depth_count):
            send_ref[owner, z] = message
        return 0

    lax.fori_loop(0, slot_count, place, 0, unroll=slot_count <= 8)


def ladder_kernel(rows, own_count, amp_ref, got_ref, out_hbm, out, picked, tiles, column, sems):
    wide_count, depth_count, _, width = got_ref.shape
    padded = got_ref.shape[2] - META
    recv_count = column.shape[0]
    tiles[...] = jnp.zeros_like(tiles)
    for u in range(recv_count):
        column[u] = 0

    def list_live(w, found):
        meta = got_ref[w, 0].astype(jnp.float32)[padded:]
        label = jnp.max(meta).astype(jnp.int32)

        @pl.when((label > 0) & (found < recv_count))
        def _():
            column[found] = lax.div(label - 1, own_count)
            spot = pl.multiple_of(lax.rem(label - 1, own_count) * width, width)
            if rows % 16 == 0:
                tile = got_ref[w][:, :rows]
            else:
                tile = got_ref[w].astype(jnp.float32)[:, :rows]
            tile = tile.reshape(depth_count * rows, width).astype(tiles.dtype)
            at = pl.multiple_of(found * width, width)
            tiles[pl.ds(at, width), pl.ds(spot, width)] = tile

        return found + (label > 0).astype(jnp.int32)

    lax.fori_loop(0, wide_count, list_live, jnp.int32(0), unroll=wide_count <= 8)
    row_count = amp_ref.shape[0]
    chunk_count = sems.shape[0]
    chunk = row_count // chunk_count
    copies = []
    for c in range(chunk_count):
        part = pl.ds(c * chunk, chunk)
        total = None
        for first in range(0, recv_count, GROUP):
            size = min(GROUP, recv_count - first)
            for u in range(size):
                at = pl.multiple_of(column[first + u] * width, width)
                picked[:, u * width : (u + 1) * width] = amp_ref[part, pl.ds(at, width)]
            term = jnp.dot(
                picked[:, : size * width],
                tiles[first * width : (first + size) * width],
                preferred_element_type=jnp.float32,
            )
            total = term if total is None else total + term
        out[part] = total
        copy = pltpu.make_async_copy(out.at[part], out_hbm.at[part], sems.at[c])
        copy.start()
        copies.append(copy)
    for copy in copies:
        copy.wait()


def shards(amplitudes, integrals, in_tile, counts, out_tile, owner_map):
    slot_count, rows, width = integrals.shape
    row_count = amplitudes.shape[0]
    wide_count = lax.axis_size("wide")
    depth_count = lax.axis_size("narrow")
    own_count = owner_map.shape[0] // wide_count
    recv_count = slot_count // 2
    kind = integrals.dtype
    whole = pl.BlockSpec(memory_space=pl.ANY)
    vmem = pl.BlockSpec(memory_space=pltpu.VMEM)
    send = pl.pallas_call(
        functools.partial(pack_kernel, own_count),
        out_shape=jax.ShapeDtypeStruct((wide_count, depth_count, rows + META, width), kind),
        in_specs=[whole] * 5,
        out_specs=vmem,
        scratch_shapes=[
            pltpu.SMEM(in_tile.shape, jnp.int32),
            pltpu.SMEM(counts.shape, jnp.int32),
            pltpu.SMEM(out_tile.shape, jnp.int32),
            pltpu.SMEM(owner_map.shape, jnp.int32),
            pltpu.VMEM(integrals.shape, kind),
            pltpu.SemaphoreType.DMA((5,)),
        ],
        compiler_params=pltpu.CompilerParams(vmem_limit_bytes=40 * 2**20),
        name="pack",
    )(in_tile, counts, out_tile, owner_map, integrals)
    got = lax.all_to_all(
        send.reshape(wide_count * depth_count, rows + META, width),
        ("wide", "narrow"),
        split_axis=0,
        concat_axis=0,
        tiled=True,
    ).reshape(wide_count, depth_count, rows + META, width)
    chunk_count = 4 if row_count % 64 == 0 else 1
    return pl.pallas_call(
        functools.partial(ladder_kernel, rows, own_count),
        out_shape=jax.ShapeDtypeStruct((row_count, own_count * width), jnp.float32),
        in_specs=[vmem, vmem],
        out_specs=whole,
        scratch_shapes=[
            pltpu.VMEM((row_count, own_count * width), jnp.float32),
            pltpu.VMEM((row_count // chunk_count, min(GROUP, recv_count) * width), kind),
            pltpu.VMEM((recv_count * width, own_count * width), kind),
            pltpu.SMEM((recv_count,), jnp.int32),
            pltpu.SemaphoreType.DMA((chunk_count,)),
        ],
        compiler_params=pltpu.CompilerParams(vmem_limit_bytes=32 * 2**20),
        name="ladder",
    )(amplitudes, got)


def solution(mesh):
    return jax.shard_map(
        shards,
        mesh=mesh,
        in_specs=(
            P("narrow", None),
            P("wide", "narrow", None),
            P("wide"),
            P("wide"),
            P("wide"),
            P(),
        ),
        out_specs=P("narrow", "wide"),
        check_vma=False,
    )
```

```python
import functools

import jax
import jax.numpy as jnp
from jax import lax
from jax.experimental import pallas as pl
from jax.experimental.pallas import tpu as pltpu
from jax.sharding import PartitionSpec as P

GROUP = 4


def pack_kernel(
    own_count,
    in_tile,
    out_tile,
    owner_map,
    counts_ref,
    rows_ref,
    amp_hbm,
    send_ref,
    label_ref,
    amp_ref,
    sem,
):
    fetch = pltpu.make_async_copy(amp_hbm, amp_ref, sem)
    fetch.start()
    slot_count = rows_ref.shape[0]
    wide_count, depth_count, _, width = send_ref.shape
    if slot_count != wide_count:
        send_ref[...] = jnp.zeros_like(send_ref)
    count = jnp.broadcast_to(counts_ref[...].reshape(1, 1), (wide_count, width))
    owners = lax.broadcasted_iota(jnp.int32, (wide_count, width), 0)

    def place(h, labels):
        spot = owner_map[out_tile[h]]
        owner = lax.div(spot, own_count)
        label = in_tile[h] * own_count + lax.rem(spot, own_count) + 1
        block = rows_ref[h]
        for z in range(depth_count):
            send_ref[owner, z] = block
        return jnp.where((owners == owner) & (h < count), label, labels)

    labels = jnp.zeros((wide_count, width), jnp.int32)
    labels = lax.fori_loop(0, slot_count, place, labels, unroll=slot_count <= 8)
    label_ref[...] = labels.astype(jnp.float32).astype(label_ref.dtype)
    fetch.wait()


def ladder_kernel(rows, own_count, recv_count, label_ref, amp_ref, got_ref, out_ref, tiles, column, seen):
    wide_count, depth_count, _, width = got_ref.shape
    me = lax.axis_index("wide")
    mine = lax.broadcasted_iota(jnp.int32, (wide_count, width), 0) == me
    tiles[...] = jnp.zeros_like(tiles)
    for u in range(recv_count):
        column[u] = 0

    def read_label(w):
        home = label_ref[pl.ds(pl.multiple_of(w * wide_count, wide_count), wide_count)]
        return jnp.max(jnp.where(mine, home.astype(jnp.float32), 0.0)).astype(jnp.int32)

    def keep(w, label, found):
        live = jnp.minimum(label, 1)
        at = jnp.minimum(found, recv_count)
        code = jnp.maximum(label - 1, 0)
        column[at] = lax.div(code, own_count)
        spot = lax.rem(code, own_count)
        if rows % 16 == 0:
            tile = got_ref[w]
        else:
            tile = got_ref[w].astype(jnp.float32)
        tile = tile.reshape(depth_count * rows, width).astype(tiles.dtype)
        at = pl.multiple_of(at * width, width)
        for q in range(own_count):
            kept = jnp.where((live > 0) & (spot == q), tile, jnp.zeros_like(tile))
            tiles[pl.ds(at, width), q * width : (q + 1) * width] = kept
        return found + live

    if wide_count <= 8:
        labels = [read_label(w) for w in range(wide_count)]
        found = jnp.int32(0)
        for w in range(wide_count):
            found = keep(w, labels[w], found)
    else:

        def note(w, _):
            seen[w] = read_label(w)
            return 0

        lax.fori_loop(0, wide_count, note, 0)
        lax.fori_loop(0, wide_count, lambda w, found: keep(w, seen[w], found), jnp.int32(0))
    total = None
    for first in range(0, recv_count, GROUP):
        last = min(first + GROUP, recv_count)
        spots = [pl.multiple_of(column[u] * width, width) for u in range(first, last)]
        picked = jnp.concatenate([amp_ref[:, pl.ds(spot, width)] for spot in spots], axis=1)
        term = jnp.dot(
            picked, tiles[first * width : last * width], preferred_element_type=jnp.float32
        )
        total = term if total is None else total + term
    out_ref[...] = total


def shards(amplitudes, integrals, in_tile, counts, out_tile, owner_map):
    slot_count, rows, width = integrals.shape
    row_count = amplitudes.shape[0]
    wide_count = lax.axis_size("wide")
    depth_count = lax.axis_size("narrow")
    own_count = owner_map.shape[0] // wide_count
    recv_count = slot_count // 2
    kind = integrals.dtype
    smem = pl.BlockSpec(memory_space=pltpu.SMEM)
    vmem = pl.BlockSpec(memory_space=pltpu.VMEM)
    send, labels, near = pl.pallas_call(
        functools.partial(pack_kernel, own_count),
        out_shape=[
            jax.ShapeDtypeStruct((wide_count, depth_count, rows, width), kind),
            jax.ShapeDtypeStruct((wide_count, width), kind),
            jax.ShapeDtypeStruct(amplitudes.shape, amplitudes.dtype),
        ],
        in_specs=[smem] * 3 + [vmem] * 2 + [pl.BlockSpec(memory_space=pl.ANY)],
        out_specs=[vmem] * 3,
        scratch_shapes=[pltpu.SemaphoreType.DMA],
        name="pack",
    )(in_tile, out_tile, owner_map, counts, integrals, amplitudes)
    labels = lax.all_gather(labels, "wide", axis=0, tiled=True)
    got = lax.all_to_all(
        send.reshape(wide_count * depth_count, rows, width),
        ("wide", "narrow"),
        split_axis=0,
        concat_axis=0,
        tiled=True,
    ).reshape(wide_count, depth_count, rows, width)
    return pl.pallas_call(
        functools.partial(ladder_kernel, rows, own_count, recv_count),
        out_shape=jax.ShapeDtypeStruct((row_count, own_count * width), jnp.float32),
        in_specs=[vmem] * 3,
        out_specs=vmem,
        scratch_shapes=[
            pltpu.VMEM(((recv_count + 1) * width, own_count * width), kind),
            pltpu.SMEM((recv_count + 1,), jnp.int32),
            pltpu.SMEM((wide_count,), jnp.int32),
        ],
        compiler_params=pltpu.CompilerParams(vmem_limit_bytes=32 * 2**20),
        name="ladder",
    )(labels, near, got)


def solution(mesh):
    return jax.shard_map(
        shards,
        mesh=mesh,
        in_specs=(
            P("narrow", None),
            P("wide", "narrow", None),
            P("wide"),
            P("wide"),
            P("wide"),
            P(),
        ),
        out_specs=P("narrow", "wide"),
        check_vma=False,
    )
```

```python
import functools

import jax
import jax.numpy as jnp
from jax import lax
from jax.experimental import pallas as pl
from jax.experimental.pallas import tpu as pltpu
from jax.sharding import PartitionSpec as P

META = 8
GROUP = 4


def pack_kernel(
    own_count, in_tile, counts, out_tile, owner_map, rows_ref, far_ref, send_ref
):
    slot_count, _, width = rows_ref.shape
    wide_count, near_count = send_ref.shape[:2]
    if slot_count != wide_count:
        send_ref[...] = jnp.zeros_like(send_ref)
    upper = lax.axis_index("narrow") >= near_count

    def place(h, _):
        spot = owner_map[out_tile[h]]
        owner = lax.div(spot, own_count)
        label = in_tile[h] * own_count + lax.rem(spot, own_count) + 1
        label = jnp.where(h < counts[0], label, 0).astype(jnp.float32)
        mine = rows_ref[h].astype(jnp.float32)
        far = far_ref[h].astype(jnp.float32)
        message = [
            jnp.where(upper, far, mine),
            jnp.where(upper, mine, far),
            jnp.full((META, width), label, jnp.float32),
        ]
        message = jnp.concatenate(message, axis=0).astype(send_ref.dtype)
        for z in range(near_count):
            send_ref[owner, z] = message
        return 0

    lax.fori_loop(0, slot_count, place, 0, unroll=slot_count <= 8)


def ladder_kernel(
    rows, own_count, recv_count, amp_hbm, got_ref, out_ref, amp_ref, tiles, column, seen, sem
):
    fetch = pltpu.make_async_copy(amp_hbm, amp_ref, sem)
    fetch.start()
    wide_count, near_count, _, width = got_ref.shape
    tiles[...] = jnp.zeros_like(tiles)
    for u in range(recv_count):
        column[u] = 0

    def read_label(w):
        meta = got_ref[w, 0].astype(jnp.float32)[2 * rows :]
        return jnp.max(meta).astype(jnp.int32)

    def keep(w, label, found):
        live = jnp.minimum(label, 1)
        at = jnp.minimum(found, recv_count)
        code = jnp.maximum(label - 1, 0)
        column[at] = lax.div(code, own_count)
        spot = lax.rem(code, own_count)
        message = got_ref[w]
        if rows % 16 != 0:
            message = message.astype(jnp.float32)
        halves = [message[:, :rows], message[:, rows : 2 * rows]]
        halves = [half.reshape(near_count * rows, width) for half in halves]
        tile = jnp.concatenate(halves, axis=0).astype(tiles.dtype)
        at = pl.multiple_of(at * width, width)
        for q in range(own_count):
            kept = jnp.where((live > 0) & (spot == q), tile, jnp.zeros_like(tile))
            tiles[pl.ds(at, width), q * width : (q + 1) * width] = kept
        return found + live

    if wide_count <= 8:
        labels = [read_label(w) for w in range(wide_count)]
        found = jnp.int32(0)
        for w in range(wide_count):
            found = keep(w, labels[w], found)
    else:

        def note(w, _):
            seen[w] = read_label(w)
            return 0

        lax.fori_loop(0, wide_count, note, 0)
        lax.fori_loop(0, wide_count, lambda w, found: keep(w, seen[w], found), jnp.int32(0))
    fetch.wait()
    total = None
    for first in range(0, recv_count, GROUP):
        last = min(first + GROUP, recv_count)
        spots = [pl.multiple_of(column[u] * width, width) for u in range(first, last)]
        picked = jnp.concatenate([amp_ref[:, pl.ds(spot, width)] for spot in spots], axis=1)
        term = jnp.dot(
            picked, tiles[first * width : last * width], preferred_element_type=jnp.float32
        )
        total = term if total is None else total + term
    out_ref[...] = total


def shards(amplitudes, integrals, in_tile, counts, out_tile, owner_map):
    slot_count, rows, width = integrals.shape
    row_count = amplitudes.shape[0]
    wide_count = lax.axis_size("wide")
    depth_count = lax.axis_size("narrow")
    near_count = depth_count // 2
    own_count = owner_map.shape[0] // wide_count
    recv_count = slot_count // 2
    kind = integrals.dtype
    length = 2 * rows + META
    smem = pl.BlockSpec(memory_space=pltpu.SMEM)
    vmem = pl.BlockSpec(memory_space=pltpu.VMEM)
    across = [(z, (z + near_count) % depth_count) for z in range(depth_count)]
    far = lax.ppermute(integrals, "narrow", across)
    send = pl.pallas_call(
        functools.partial(pack_kernel, own_count),
        out_shape=jax.ShapeDtypeStruct((wide_count, near_count, length, width), kind),
        in_specs=[smem] * 4 + [vmem] * 2,
        out_specs=vmem,
        name="pack",
    )(in_tile, counts, out_tile, owner_map, integrals, far)
    groups = [
        [w * depth_count + half * near_count + z for w in range(wide_count) for z in range(near_count)]
        for half in range(2)
    ]
    got = lax.all_to_all(
        send.reshape(wide_count * near_count, length, width),
        ("wide", "narrow"),
        split_axis=0,
        concat_axis=0,
        tiled=True,
        axis_index_groups=groups,
    ).reshape(wide_count, near_count, length, width)
    return pl.pallas_call(
        functools.partial(ladder_kernel, rows, own_count, recv_count),
        out_shape=jax.ShapeDtypeStruct((row_count, own_count * width), jnp.float32),
        in_specs=[pl.BlockSpec(memory_space=pl.ANY), vmem],
        out_specs=vmem,
        scratch_shapes=[
            pltpu.VMEM(amplitudes.shape, amplitudes.dtype),
            pltpu.VMEM(((recv_count + 1) * width, own_count * width), kind),
            pltpu.SMEM((recv_count + 1,), jnp.int32),
            pltpu.SMEM((wide_count,), jnp.int32),
            pltpu.SemaphoreType.DMA,
        ],
        name="ladder",
    )(amplitudes, got)


def solution(mesh):
    return jax.shard_map(
        shards,
        mesh=mesh,
        in_specs=(
            P("narrow", None),
            P("wide", "narrow", None),
            P("wide"),
            P("wide"),
            P("wide"),
            P(),
        ),
        out_specs=P("narrow", "wide"),
        check_vma=False,
    )
```

```python
import functools

import jax
import jax.numpy as jnp
from jax import lax
from jax.experimental import pallas as pl
from jax.experimental.pallas import tpu as pltpu
from jax.sharding import PartitionSpec as P

PAIR = 2
GROUP = 4
UNROLL = 8


def each(count, body, start):
    if count > UNROLL:
        return lax.fori_loop(0, count, body, start)
    for i in range(count):
        start = body(i, start)
    return start


def message_at(index, length):
    start = index * length
    if not isinstance(index, int):
        start = pl.multiple_of(start, length)
    return start


def pack_kernel(own_count, depth_count, in_tile, counts, out_tile, owner_map, rows_ref, send_ref, slot, code):
    slot_count, rows, width = rows_ref.shape
    wide_count = slot.shape[0]
    length = send_ref.shape[0] // (wide_count * depth_count)
    for owner in range(wide_count):
        slot[owner] = 0
        code[owner] = 0

    def route(h, _):
        spot = owner_map[out_tile[h]]
        owner = lax.div(spot, own_count)
        label = in_tile[h] * own_count + lax.rem(spot, own_count) + 1
        slot[owner] = h
        code[owner] = jnp.where(h < counts[0], label, 0)
        return 0

    each(slot_count, route, 0)

    def write(owner, _):
        block = rows_ref[slot[owner]]
        label = jnp.full((length - rows, width), code[owner].astype(jnp.float32), jnp.float32)
        if length % 16 == 0:
            message = jnp.concatenate([block.astype(jnp.float32), label], axis=0)
            pieces = [(0, message.astype(send_ref.dtype))]
        else:
            pieces = [(0, block), (rows, label.astype(send_ref.dtype))]
        for z in range(depth_count):
            start = message_at(owner * depth_count + z, length)
            for offset, piece in pieces:
                send_ref[pl.ds(start + offset, piece.shape[0])] = piece
        return 0

    each(wide_count, write, 0)


def ladder_kernel(
    rows, depth_count, own_count, recv_count, amp_ref, got_ref, out_ref, tiles, column, seen
):
    wide_count = seen.shape[0]
    width = got_ref.shape[1]
    length = got_ref.shape[0] // (wide_count * depth_count)
    tiles[...] = jnp.zeros_like(tiles)
    for u in range(recv_count):
        column[u] = 0

    def message(w, z):
        start = message_at(w * depth_count + z, length)
        if length % 16 == 0:
            return got_ref[pl.ds(start, length)].astype(jnp.float32)[:rows]
        return got_ref[pl.ds(start, rows)]

    def read_label(w):
        start = message_at(w * depth_count, length)
        if length % 16 == 0:
            label = got_ref[pl.ds(start, length)].astype(jnp.float32)[rows:]
        else:
            label = got_ref[pl.ds(start + rows, length - rows)].astype(jnp.float32)
        return jnp.max(label).astype(jnp.int32)

    def keep(w, label, found):
        live = jnp.minimum(label, 1)
        at = jnp.minimum(found, recv_count)
        place = jnp.maximum(label - 1, 0)
        column[at] = lax.div(place, own_count)
        spot = lax.rem(place, own_count)
        tile = jnp.concatenate([message(w, z) for z in range(depth_count)], axis=0)
        tile = tile.astype(tiles.dtype)
        at = pl.multiple_of(at * width, width)
        for q in range(own_count):
            kept = jnp.where((live > 0) & (spot == q), tile, jnp.zeros_like(tile))
            tiles[pl.ds(at, width), q * width : (q + 1) * width] = kept
        return found + live

    if wide_count <= UNROLL:
        labels = [read_label(w) for w in range(wide_count)]
        found = jnp.int32(0)
        for w in range(wide_count):
            found = keep(w, labels[w], found)
    else:

        def note(w, _):
            seen[w] = read_label(w)
            return 0

        lax.fori_loop(0, wide_count, note, 0)
        lax.fori_loop(0, wide_count, lambda w, found: keep(w, seen[w], found), jnp.int32(0))
    total = None
    for first in range(0, recv_count, GROUP):
        last = min(first + GROUP, recv_count)
        spots = [pl.multiple_of(column[u] * width, width) for u in range(first, last)]
        picked = jnp.concatenate([amp_ref[:, pl.ds(spot, width)] for spot in spots], axis=1)
        term = jnp.dot(
            picked, tiles[first * width : last * width], preferred_element_type=jnp.float32
        )
        total = term if total is None else total + term
    out_ref[...] = total


def shards(amplitudes, integrals, in_tile, counts, out_tile, owner_map):
    slot_count, rows, width = integrals.shape
    row_count = amplitudes.shape[0]
    wide_count = lax.axis_size("wide")
    depth_count = lax.axis_size("narrow")
    own_count = owner_map.shape[0] // wide_count
    recv_count = slot_count // 2
    kind = integrals.dtype
    message_count = wide_count * depth_count
    length = rows + PAIR
    if wide_count > UNROLL or rows % PAIR != 0 or message_count * length % 16 != 0:
        length = -(-length // 16) * 16
    smem = pl.BlockSpec(memory_space=pltpu.SMEM)
    vmem = pl.BlockSpec(memory_space=pltpu.VMEM)
    send = pl.pallas_call(
        functools.partial(pack_kernel, own_count, depth_count),
        out_shape=jax.ShapeDtypeStruct((message_count * length, width), kind),
        in_specs=[smem] * 4 + [vmem],
        out_specs=vmem,
        scratch_shapes=[pltpu.SMEM((wide_count,), jnp.int32)] * 2,
        name="pack",
    )(in_tile, counts, out_tile, owner_map, integrals)
    got = lax.all_to_all(
        send.reshape(message_count, length // PAIR, PAIR, width),
        ("wide", "narrow"),
        split_axis=0,
        concat_axis=0,
        tiled=True,
    ).reshape(message_count * length, width)
    return pl.pallas_call(
        functools.partial(ladder_kernel, rows, depth_count, own_count, recv_count),
        out_shape=jax.ShapeDtypeStruct((row_count, own_count * width), jnp.float32),
        in_specs=[vmem] * 2,
        out_specs=vmem,
        scratch_shapes=[
            pltpu.VMEM(((recv_count + 1) * width, own_count * width), kind),
            pltpu.SMEM((recv_count + 1,), jnp.int32),
            pltpu.SMEM((wide_count,), jnp.int32),
        ],
        compiler_params=pltpu.CompilerParams(vmem_limit_bytes=32 * 2**20),
        name="ladder",
    )(amplitudes, got)


def solution(mesh):
    return jax.shard_map(
        shards,
        mesh=mesh,
        in_specs=(
            P("narrow", None),
            P("wide", "narrow", None),
            P("wide"),
            P("wide"),
            P("wide"),
            P(),
        ),
        out_specs=P("narrow", "wide"),
        check_vma=False,
    )
```

```python
import functools

import jax
import jax.numpy as jnp
from jax import lax
from jax.experimental import pallas as pl
from jax.experimental.pallas import tpu as pltpu
from jax.sharding import PartitionSpec as P

PAIR = 2
GROUP = 4
UNROLL = 8


def each(count, body, start):
    if count > UNROLL:
        return lax.fori_loop(0, count, body, start)
    for i in range(count):
        start = body(i, start)
    return start


def message_at(index, length):
    start = index * length
    if not isinstance(index, int):
        start = pl.multiple_of(start, length)
    return start


def pack_kernel(own_count, depth_count, *refs):
    sources, send_ref, targets, (slot, code, sems) = refs[:5], refs[5], refs[6:11], refs[11:]
    in_tile, counts, out_tile, owner_map, rows_ref = targets
    copies = [
        pltpu.make_async_copy(source, target, sems.at[i])
        for i, (source, target) in enumerate(zip(sources, targets))
    ]
    for copy in copies:
        copy.start()
    slot_count, rows, width = rows_ref.shape
    wide_count = slot.shape[0]
    length = send_ref.shape[0] // (wide_count * depth_count)
    for owner in range(wide_count):
        slot[owner] = 0
        code[owner] = 0
    for copy in copies:
        copy.wait()

    def route(h, _):
        spot = owner_map[out_tile[h]]
        owner = lax.div(spot, own_count)
        label = in_tile[h] * own_count + lax.rem(spot, own_count) + 1
        slot[owner] = h
        code[owner] = jnp.where(h < counts[0], label, 0)
        return 0

    each(slot_count, route, 0)

    def write(owner, _):
        block = rows_ref[slot[owner]]
        label = jnp.full((length - rows, width), code[owner].astype(jnp.float32), jnp.float32)
        if length % 16 == 0:
            message = jnp.concatenate([block.astype(jnp.float32), label], axis=0)
            pieces = [(0, message.astype(send_ref.dtype))]
        else:
            pieces = [(0, block), (rows, label.astype(send_ref.dtype))]
        for z in range(depth_count):
            start = message_at(owner * depth_count + z, length)
            for offset, piece in pieces:
                send_ref[pl.ds(start + offset, piece.shape[0])] = piece
        return 0

    each(wide_count, write, 0)


def ladder_kernel(
    rows, depth_count, own_count, recv_count, amp_ref, got_ref, out_ref, tiles, column, seen
):
    wide_count = seen.shape[0]
    width = got_ref.shape[1]
    length = got_ref.shape[0] // (wide_count * depth_count)
    tiles[...] = jnp.zeros_like(tiles)
    for u in range(recv_count):
        column[u] = 0

    def message(w, z):
        start = message_at(w * depth_count + z, length)
        if length % 16 == 0:
            return got_ref[pl.ds(start, length)].astype(jnp.float32)[:rows]
        return got_ref[pl.ds(start, rows)]

    def read_label(w):
        start = message_at(w * depth_count, length)
        if length % 16 == 0:
            label = got_ref[pl.ds(start, length)].astype(jnp.float32)[rows:]
        else:
            label = got_ref[pl.ds(start + rows, length - rows)].astype(jnp.float32)
        return jnp.max(label).astype(jnp.int32)

    def keep(w, label, found):
        live = jnp.minimum(label, 1)
        at = jnp.minimum(found, recv_count)
        place = jnp.maximum(label - 1, 0)
        column[at] = lax.div(place, own_count)
        spot = lax.rem(place, own_count)
        tile = jnp.concatenate([message(w, z) for z in range(depth_count)], axis=0)
        tile = tile.astype(tiles.dtype)
        at = pl.multiple_of(at * width, width)
        for q in range(own_count):
            kept = jnp.where((live > 0) & (spot == q), tile, jnp.zeros_like(tile))
            tiles[pl.ds(at, width), q * width : (q + 1) * width] = kept
        return found + live

    if wide_count <= UNROLL:
        labels = [read_label(w) for w in range(wide_count)]
        found = jnp.int32(0)
        for w in range(wide_count):
            found = keep(w, labels[w], found)
    else:

        def note(w, _):
            seen[w] = read_label(w)
            return 0

        lax.fori_loop(0, wide_count, note, 0)
        lax.fori_loop(0, wide_count, lambda w, found: keep(w, seen[w], found), jnp.int32(0))
    total = None
    for first in range(0, recv_count, GROUP):
        last = min(first + GROUP, recv_count)
        spots = [pl.multiple_of(column[u] * width, width) for u in range(first, last)]
        picked = jnp.concatenate([amp_ref[:, pl.ds(spot, width)] for spot in spots], axis=1)
        term = jnp.dot(
            picked, tiles[first * width : last * width], preferred_element_type=jnp.float32
        )
        total = term if total is None else total + term
    out_ref[...] = total


def shards(amplitudes, integrals, in_tile, counts, out_tile, owner_map):
    slot_count, rows, width = integrals.shape
    row_count = amplitudes.shape[0]
    wide_count = lax.axis_size("wide")
    depth_count = lax.axis_size("narrow")
    own_count = owner_map.shape[0] // wide_count
    recv_count = slot_count // 2
    kind = integrals.dtype
    message_count = wide_count * depth_count
    length = rows + PAIR
    if wide_count > UNROLL or rows % PAIR != 0 or message_count * length % 16 != 0:
        length = -(-length // 16) * 16
    hbm = pl.BlockSpec(memory_space=pltpu.HBM)
    vmem = pl.BlockSpec(memory_space=pltpu.VMEM)
    given = [in_tile, counts, out_tile, owner_map, integrals]
    given = [
        value if value.size == 1 else pltpu.with_memory_space_constraint(value, pltpu.HBM)
        for value in given
    ]
    send = pl.pallas_call(
        functools.partial(pack_kernel, own_count, depth_count),
        out_shape=jax.ShapeDtypeStruct((message_count * length, width), kind),
        in_specs=[hbm] * len(given),
        out_specs=vmem,
        scratch_shapes=[pltpu.SMEM(value.shape, value.dtype) for value in given[:-1]]
        + [pltpu.VMEM(integrals.shape, kind)]
        + [pltpu.SMEM((wide_count,), jnp.int32)] * 2
        + [pltpu.SemaphoreType.DMA((len(given),))],
        compiler_params=pltpu.CompilerParams(vmem_limit_bytes=32 * 2**20),
        cost_estimate=pl.CostEstimate(flops=2**30, bytes_accessed=2**20, transcendentals=0),
        name="pack",
    )(*given)
    got = lax.all_to_all(
        send.reshape(message_count, length // PAIR, PAIR, width),
        ("wide", "narrow"),
        split_axis=0,
        concat_axis=0,
        tiled=True,
    ).reshape(message_count * length, width)
    return pl.pallas_call(
        functools.partial(ladder_kernel, rows, depth_count, own_count, recv_count),
        out_shape=jax.ShapeDtypeStruct((row_count, own_count * width), jnp.float32),
        in_specs=[vmem] * 2,
        out_specs=vmem,
        scratch_shapes=[
            pltpu.VMEM(((recv_count + 1) * width, own_count * width), kind),
            pltpu.SMEM((recv_count + 1,), jnp.int32),
            pltpu.SMEM((wide_count,), jnp.int32),
        ],
        compiler_params=pltpu.CompilerParams(vmem_limit_bytes=32 * 2**20),
        name="ladder",
    )(amplitudes, got)


def solution(mesh):
    return jax.shard_map(
        shards,
        mesh=mesh,
        in_specs=(
            P("narrow", None),
            P("wide", "narrow", None),
            P("wide"),
            P("wide"),
            P("wide"),
            P(),
        ),
        out_specs=P("narrow", "wide"),
        check_vma=False,
    )
```

```python
import functools

import jax
import jax.numpy as jnp
from jax import lax
from jax.experimental import pallas as pl
from jax.experimental.pallas import tpu as pltpu
from jax.sharding import PartitionSpec as P

PAIR = 2
GROUP = 4
UNROLL = 8


def each(count, body, start):
    if count > UNROLL:
        return lax.fori_loop(0, count, body, start)
    for i in range(count):
        start = body(i, start)
    return start


def message_at(index, length):
    start = index * length
    if not isinstance(index, int):
        start = pl.multiple_of(start, length)
    return start


def pack_kernel(own_count, depth_count, *refs):
    sources, send_ref, targets, (slot, code, sems) = refs[:5], refs[5], refs[6:11], refs[11:]
    in_tile, counts, out_tile, owner_map, rows_ref = targets
    copies = [
        pltpu.make_async_copy(source, target, sems.at[i])
        for i, (source, target) in enumerate(zip(sources, targets))
    ]
    for copy in copies:
        copy.start()
    slot_count, rows, width = rows_ref.shape
    wide_count = slot.shape[0]
    length = send_ref.shape[0] // (wide_count * depth_count)
    for owner in range(wide_count):
        slot[owner] = 0
        code[owner] = 0
    for copy in copies:
        copy.wait()

    def route(h, _):
        spot = owner_map[out_tile[h]]
        owner = lax.div(spot, own_count)
        label = in_tile[h] * own_count + lax.rem(spot, own_count) + 1
        slot[owner] = h
        code[owner] = jnp.where(h < counts[0], label, 0)
        return 0

    each(slot_count, route, 0)

    def write(owner, _):
        block = rows_ref[slot[owner]]
        label = jnp.full((length - rows, width), code[owner].astype(jnp.float32), jnp.float32)
        if length % 16 == 0:
            message = jnp.concatenate([block.astype(jnp.float32), label], axis=0)
            pieces = [(0, message.astype(send_ref.dtype))]
        else:
            pieces = [(0, block), (rows, label.astype(send_ref.dtype))]
        for z in range(depth_count):
            start = message_at(owner * depth_count + z, length)
            for offset, piece in pieces:
                send_ref[pl.ds(start + offset, piece.shape[0])] = piece
        return 0

    each(wide_count, write, 0)


def fetch_kernel(source, target, sem):
    copy = pltpu.make_async_copy(source, target, sem)
    copy.start()
    copy.wait()


def ladder_kernel(
    rows, depth_count, own_count, recv_count, amp_ref, got_ref, out_ref, tiles, column, seen
):
    wide_count = seen.shape[0]
    width = got_ref.shape[1]
    length = got_ref.shape[0] // (wide_count * depth_count)
    tiles[...] = jnp.zeros_like(tiles)
    for u in range(recv_count):
        column[u] = 0

    def message(w, z):
        start = message_at(w * depth_count + z, length)
        if length % 16 == 0:
            return got_ref[pl.ds(start, length)].astype(jnp.float32)[:rows]
        return got_ref[pl.ds(start, rows)]

    def read_label(w):
        start = message_at(w * depth_count, length)
        if length % 16 == 0:
            label = got_ref[pl.ds(start, length)].astype(jnp.float32)[rows:]
        else:
            label = got_ref[pl.ds(start + rows, length - rows)].astype(jnp.float32)
        return jnp.max(label).astype(jnp.int32)

    def keep(w, label, found):
        live = jnp.minimum(label, 1)
        at = jnp.minimum(found, recv_count)
        place = jnp.maximum(label - 1, 0)
        column[at] = lax.div(place, own_count)
        spot = lax.rem(place, own_count)
        tile = jnp.concatenate([message(w, z) for z in range(depth_count)], axis=0)
        tile = tile.astype(tiles.dtype)
        at = pl.multiple_of(at * width, width)
        for q in range(own_count):
            kept = jnp.where((live > 0) & (spot == q), tile, jnp.zeros_like(tile))
            tiles[pl.ds(at, width), q * width : (q + 1) * width] = kept
        return found + live

    if wide_count <= UNROLL:
        labels = [read_label(w) for w in range(wide_count)]
        found = jnp.int32(0)
        for w in range(wide_count):
            found = keep(w, labels[w], found)
    else:

        def note(w, _):
            seen[w] = read_label(w)
            return 0

        lax.fori_loop(0, wide_count, note, 0)
        lax.fori_loop(0, wide_count, lambda w, found: keep(w, seen[w], found), jnp.int32(0))
    total = None
    for first in range(0, recv_count, GROUP):
        last = min(first + GROUP, recv_count)
        spots = [pl.multiple_of(column[u] * width, width) for u in range(first, last)]
        picked = jnp.concatenate([amp_ref[:, pl.ds(spot, width)] for spot in spots], axis=1)
        term = jnp.dot(
            picked, tiles[first * width : last * width], preferred_element_type=jnp.float32
        )
        total = term if total is None else total + term
    out_ref[...] = total


def shards(amplitudes, integrals, in_tile, counts, out_tile, owner_map):
    slot_count, rows, width = integrals.shape
    row_count = amplitudes.shape[0]
    wide_count = lax.axis_size("wide")
    depth_count = lax.axis_size("narrow")
    own_count = owner_map.shape[0] // wide_count
    recv_count = slot_count // 2
    kind = integrals.dtype
    message_count = wide_count * depth_count
    length = rows + PAIR
    if wide_count > UNROLL or rows % PAIR != 0 or message_count * length % 16 != 0:
        length = -(-length // 16) * 16
    hbm = pl.BlockSpec(memory_space=pltpu.HBM)
    vmem = pl.BlockSpec(memory_space=pltpu.VMEM)
    given = [in_tile, counts, out_tile, owner_map, integrals]
    given = [
        value if value.size == 1 else pltpu.with_memory_space_constraint(value, pltpu.HBM)
        for value in given
    ]
    send = pl.pallas_call(
        functools.partial(pack_kernel, own_count, depth_count),
        out_shape=jax.ShapeDtypeStruct((message_count * length, width), kind),
        in_specs=[hbm] * len(given),
        out_specs=vmem,
        scratch_shapes=[pltpu.SMEM(value.shape, value.dtype) for value in given[:-1]]
        + [pltpu.VMEM(integrals.shape, kind)]
        + [pltpu.SMEM((wide_count,), jnp.int32)] * 2
        + [pltpu.SemaphoreType.DMA((len(given),))],
        compiler_params=pltpu.CompilerParams(vmem_limit_bytes=32 * 2**20),
        name="pack",
    )(*given)
    got = lax.all_to_all(
        send.reshape(message_count, length // PAIR, PAIR, width),
        ("wide", "narrow"),
        split_axis=0,
        concat_axis=0,
        tiled=True,
    ).reshape(message_count * length, width)
    near = pl.pallas_call(
        fetch_kernel,
        out_shape=jax.ShapeDtypeStruct(amplitudes.shape, amplitudes.dtype),
        in_specs=[hbm],
        out_specs=vmem,
        scratch_shapes=[pltpu.SemaphoreType.DMA],
        compiler_params=pltpu.CompilerParams(vmem_limit_bytes=32 * 2**20),
        cost_estimate=pl.CostEstimate(flops=2**30, bytes_accessed=2**21, transcendentals=0),
        name="fetch",
    )(pltpu.with_memory_space_constraint(amplitudes, pltpu.HBM))
    return pl.pallas_call(
        functools.partial(ladder_kernel, rows, depth_count, own_count, recv_count),
        out_shape=jax.ShapeDtypeStruct((row_count, own_count * width), jnp.float32),
        in_specs=[vmem] * 2,
        out_specs=vmem,
        scratch_shapes=[
            pltpu.VMEM(((recv_count + 1) * width, own_count * width), kind),
            pltpu.SMEM((recv_count + 1,), jnp.int32),
            pltpu.SMEM((wide_count,), jnp.int32),
        ],
        compiler_params=pltpu.CompilerParams(vmem_limit_bytes=32 * 2**20),
        name="ladder",
    )(near, got)


def solution(mesh):
    return jax.shard_map(
        shards,
        mesh=mesh,
        in_specs=(
            P("narrow", None),
            P("wide", "narrow", None),
            P("wide"),
            P("wide"),
            P("wide"),
            P(),
        ),
        out_specs=P("narrow", "wide"),
        check_vma=False,
    )
```

```python
import functools

import jax
import jax.numpy as jnp
from jax import lax
from jax.experimental import pallas as pl
from jax.experimental.pallas import tpu as pltpu
from jax.sharding import PartitionSpec as P

PAIR = 2
GROUP = 4
UNROLL = 8


def each(count, body, start):
    if count > UNROLL:
        return lax.fori_loop(0, count, body, start)
    for i in range(count):
        start = body(i, start)
    return start


def message_at(index, count, length):
    start = (count - 1 - index) * length
    if not isinstance(index, int):
        start = pl.multiple_of(start, length)
    return start


def pack_kernel(own_count, depth_count, *refs):
    sources, send_ref, targets, (slot, code, sems) = refs[:5], refs[5], refs[6:11], refs[11:]
    in_tile, counts, out_tile, owner_map, rows_ref = targets
    copies = [
        pltpu.make_async_copy(source, target, sems.at[i])
        for i, (source, target) in enumerate(zip(sources, targets))
    ]
    for copy in copies:
        copy.start()
    slot_count, rows, width = rows_ref.shape
    wide_count = slot.shape[0]
    length = send_ref.shape[0] // (wide_count * depth_count)
    for owner in range(wide_count):
        slot[owner] = 0
        code[owner] = 0
    for copy in copies:
        copy.wait()

    def route(h, _):
        spot = owner_map[out_tile[h]]
        owner = lax.div(spot, own_count)
        label = in_tile[h] * own_count + lax.rem(spot, own_count) + 1
        slot[owner] = h
        code[owner] = jnp.where(h < counts[0], label, 0)
        return 0

    each(slot_count, route, 0)

    def write(owner, _):
        block = rows_ref[slot[owner]]
        label = jnp.full((length - rows, width), code[owner].astype(jnp.float32), jnp.float32)
        if length % 16 == 0:
            message = jnp.concatenate([block.astype(jnp.float32), label], axis=0)
            pieces = [(0, message.astype(send_ref.dtype))]
        else:
            pieces = [(0, block), (rows, label.astype(send_ref.dtype))]
        for z in range(depth_count):
            start = message_at(owner * depth_count + z, wide_count * depth_count, length)
            for offset, piece in pieces:
                send_ref[pl.ds(start + offset, piece.shape[0])] = piece
        return 0

    each(wide_count, write, 0)


def ladder_kernel(
    rows, depth_count, own_count, recv_count, amp_ref, got_ref, out_ref, tiles, column, seen
):
    wide_count = seen.shape[0]
    width = got_ref.shape[1]
    length = got_ref.shape[0] // (wide_count * depth_count)
    tiles[...] = jnp.zeros_like(tiles)
    for u in range(recv_count):
        column[u] = 0

    def message(w, z):
        start = message_at(w * depth_count + z, wide_count * depth_count, length)
        if length % 16 == 0:
            return got_ref[pl.ds(start, length)].astype(jnp.float32)[:rows]
        return got_ref[pl.ds(start, rows)]

    def read_label(w):
        start = message_at(w * depth_count, wide_count * depth_count, length)
        if length % 16 == 0:
            label = got_ref[pl.ds(start, length)].astype(jnp.float32)[rows:]
        else:
            label = got_ref[pl.ds(start + rows, length - rows)].astype(jnp.float32)
        return jnp.max(label).astype(jnp.int32)

    def keep(w, label, found):
        live = jnp.minimum(label, 1)
        at = jnp.minimum(found, recv_count)
        place = jnp.maximum(label - 1, 0)
        column[at] = lax.div(place, own_count)
        spot = lax.rem(place, own_count)
        tile = jnp.concatenate([message(w, z) for z in range(depth_count)], axis=0)
        tile = tile.astype(tiles.dtype)
        at = pl.multiple_of(at * width, width)
        for q in range(own_count):
            kept = jnp.where((live > 0) & (spot == q), tile, jnp.zeros_like(tile))
            tiles[pl.ds(at, width), q * width : (q + 1) * width] = kept
        return found + live

    if wide_count <= UNROLL:
        labels = [read_label(w) for w in range(wide_count)]
        found = jnp.int32(0)
        for w in range(wide_count):
            found = keep(w, labels[w], found)
    else:

        def note(w, _):
            seen[w] = read_label(w)
            return 0

        lax.fori_loop(0, wide_count, note, 0)
        lax.fori_loop(0, wide_count, lambda w, found: keep(w, seen[w], found), jnp.int32(0))
    total = None
    for first in range(0, recv_count, GROUP):
        last = min(first + GROUP, recv_count)
        spots = [pl.multiple_of(column[u] * width, width) for u in range(first, last)]
        picked = jnp.concatenate([amp_ref[:, pl.ds(spot, width)] for spot in spots], axis=1)
        term = jnp.dot(
            picked, tiles[first * width : last * width], preferred_element_type=jnp.float32
        )
        total = term if total is None else total + term
    out_ref[...] = total


def shards(amplitudes, integrals, in_tile, counts, out_tile, owner_map):
    slot_count, rows, width = integrals.shape
    row_count = amplitudes.shape[0]
    wide_count = lax.axis_size("wide")
    depth_count = lax.axis_size("narrow")
    own_count = owner_map.shape[0] // wide_count
    recv_count = slot_count // 2
    kind = integrals.dtype
    message_count = wide_count * depth_count
    length = rows + PAIR
    if wide_count > UNROLL or rows % PAIR != 0 or message_count * length % 16 != 0:
        length = -(-length // 16) * 16
    hbm = pl.BlockSpec(memory_space=pltpu.HBM)
    vmem = pl.BlockSpec(memory_space=pltpu.VMEM)
    given = [in_tile, counts, out_tile, owner_map, integrals]
    given = [
        value if value.size == 1 else pltpu.with_memory_space_constraint(value, pltpu.HBM)
        for value in given
    ]
    send = pl.pallas_call(
        functools.partial(pack_kernel, own_count, depth_count),
        out_shape=jax.ShapeDtypeStruct((message_count * length, width), kind),
        in_specs=[hbm] * len(given),
        out_specs=vmem,
        scratch_shapes=[pltpu.SMEM(value.shape, value.dtype) for value in given[:-1]]
        + [pltpu.VMEM(integrals.shape, kind)]
        + [pltpu.SMEM((wide_count,), jnp.int32)] * 2
        + [pltpu.SemaphoreType.DMA((len(given),))],
        compiler_params=pltpu.CompilerParams(vmem_limit_bytes=32 * 2**20),
        cost_estimate=pl.CostEstimate(flops=2**30, bytes_accessed=2**20, transcendentals=0),
        name="pack",
    )(*given)
    got = lax.all_to_all(
        send.reshape(message_count, length // PAIR, PAIR, width),
        ("wide", "narrow"),
        split_axis=0,
        concat_axis=0,
        tiled=True,
        axis_index_groups=[list(reversed(range(message_count)))],
    ).reshape(message_count * length, width)
    return pl.pallas_call(
        functools.partial(ladder_kernel, rows, depth_count, own_count, recv_count),
        out_shape=jax.ShapeDtypeStruct((row_count, own_count * width), jnp.float32),
        in_specs=[vmem] * 2,
        out_specs=vmem,
        scratch_shapes=[
            pltpu.VMEM(((recv_count + 1) * width, own_count * width), kind),
            pltpu.SMEM((recv_count + 1,), jnp.int32),
            pltpu.SMEM((wide_count,), jnp.int32),
        ],
        compiler_params=pltpu.CompilerParams(vmem_limit_bytes=32 * 2**20),
        name="ladder",
    )(amplitudes, got)


def solution(mesh):
    return jax.shard_map(
        shards,
        mesh=mesh,
        in_specs=(
            P("narrow", None),
            P("wide", "narrow", None),
            P("wide"),
            P("wide"),
            P("wide"),
            P(),
        ),
        out_specs=P("narrow", "wide"),
        check_vma=False,
    )
```

```python
import functools

import jax
import jax.numpy as jnp
from jax import lax
from jax.experimental import pallas as pl
from jax.experimental.pallas import tpu as pltpu
from jax.sharding import PartitionSpec as P

PAIR = 2
GROUP = 4
UNROLL = 8


def each(count, body, start):
    if count > UNROLL:
        return lax.fori_loop(0, count, body, start)
    for i in range(count):
        start = body(i, start)
    return start


def message_at(index, length):
    start = index * length
    if not isinstance(index, int):
        start = pl.multiple_of(start, length)
    return start


def pack_kernel(own_count, depth_count, *refs):
    sources, send_ref, targets, (slot, code, sems) = refs[:5], refs[5], refs[6:11], refs[11:]
    in_tile, counts, out_tile, owner_map, rows_ref = targets
    copies = [
        pltpu.make_async_copy(source, target, sems.at[i])
        for i, (source, target) in enumerate(zip(sources, targets))
    ]
    for copy in copies:
        copy.start()
    slot_count, rows, width = rows_ref.shape
    wide_count = slot.shape[0]
    length = send_ref.shape[0] // (wide_count * depth_count)
    for owner in range(wide_count):
        slot[owner] = 0
        code[owner] = 0
    for copy in copies:
        copy.wait()

    def route(h, _):
        spot = owner_map[out_tile[h]]
        owner = lax.div(spot, own_count)
        label = in_tile[h] * own_count + lax.rem(spot, own_count) + 1
        slot[owner] = h
        code[owner] = jnp.where(h < counts[0], label, 0)
        return 0

    each(slot_count, route, 0)

    def write(owner, _):
        block = rows_ref[slot[owner]]
        label = jnp.full((length - rows, width), code[owner].astype(jnp.float32), jnp.float32)
        if length % 16 == 0:
            message = jnp.concatenate([block.astype(jnp.float32), label], axis=0)
            pieces = [(0, message.astype(send_ref.dtype))]
        else:
            pieces = [(0, block), (rows, label.astype(send_ref.dtype))]
        for z in range(depth_count):
            start = message_at(z * wide_count + owner, length)
            for offset, piece in pieces:
                send_ref[pl.ds(start + offset, piece.shape[0])] = piece
        return 0

    each(wide_count, write, 0)


def ladder_kernel(
    rows, depth_count, own_count, recv_count, amp_ref, got_ref, out_ref, tiles, column, seen
):
    wide_count = seen.shape[0]
    width = got_ref.shape[1]
    length = got_ref.shape[0] // (wide_count * depth_count)
    tiles[...] = jnp.zeros_like(tiles)
    for u in range(recv_count):
        column[u] = 0

    def message(w, z):
        start = message_at(z * wide_count + w, length)
        if length % 16 == 0:
            return got_ref[pl.ds(start, length)].astype(jnp.float32)[:rows]
        return got_ref[pl.ds(start, rows)]

    def read_label(w):
        start = message_at(w, length)
        if length % 16 == 0:
            label = got_ref[pl.ds(start, length)].astype(jnp.float32)[rows:]
        else:
            label = got_ref[pl.ds(start + rows, length - rows)].astype(jnp.float32)
        return jnp.max(label).astype(jnp.int32)

    def keep(w, label, found):
        live = jnp.minimum(label, 1)
        at = jnp.minimum(found, recv_count)
        place = jnp.maximum(label - 1, 0)
        column[at] = lax.div(place, own_count)
        spot = lax.rem(place, own_count)
        tile = jnp.concatenate([message(w, z) for z in range(depth_count)], axis=0)
        tile = tile.astype(tiles.dtype)
        at = pl.multiple_of(at * width, width)
        for q in range(own_count):
            kept = jnp.where((live > 0) & (spot == q), tile, jnp.zeros_like(tile))
            tiles[pl.ds(at, width), q * width : (q + 1) * width] = kept
        return found + live

    if wide_count <= UNROLL:
        labels = [read_label(w) for w in range(wide_count)]
        found = jnp.int32(0)
        for w in range(wide_count):
            found = keep(w, labels[w], found)
    else:

        def note(w, _):
            seen[w] = read_label(w)
            return 0

        lax.fori_loop(0, wide_count, note, 0)
        lax.fori_loop(0, wide_count, lambda w, found: keep(w, seen[w], found), jnp.int32(0))
    total = None
    for first in range(0, recv_count, GROUP):
        last = min(first + GROUP, recv_count)
        spots = [pl.multiple_of(column[u] * width, width) for u in range(first, last)]
        picked = jnp.concatenate([amp_ref[:, pl.ds(spot, width)] for spot in spots], axis=1)
        term = jnp.dot(
            picked, tiles[first * width : last * width], preferred_element_type=jnp.float32
        )
        total = term if total is None else total + term
    out_ref[...] = total


def shards(amplitudes, integrals, in_tile, counts, out_tile, owner_map):
    slot_count, rows, width = integrals.shape
    row_count = amplitudes.shape[0]
    wide_count = lax.axis_size("wide")
    depth_count = lax.axis_size("narrow")
    own_count = owner_map.shape[0] // wide_count
    recv_count = slot_count // 2
    kind = integrals.dtype
    message_count = wide_count * depth_count
    length = rows + PAIR
    if wide_count > UNROLL or rows % PAIR != 0 or message_count * length % 16 != 0:
        length = -(-length // 16) * 16
    hbm = pl.BlockSpec(memory_space=pltpu.HBM)
    vmem = pl.BlockSpec(memory_space=pltpu.VMEM)
    given = [in_tile, counts, out_tile, owner_map, integrals]
    given = [
        value if value.size == 1 else pltpu.with_memory_space_constraint(value, pltpu.HBM)
        for value in given
    ]
    send = pl.pallas_call(
        functools.partial(pack_kernel, own_count, depth_count),
        out_shape=jax.ShapeDtypeStruct((message_count * length, width), kind),
        in_specs=[hbm] * len(given),
        out_specs=vmem,
        scratch_shapes=[pltpu.SMEM(value.shape, value.dtype) for value in given[:-1]]
        + [pltpu.VMEM(integrals.shape, kind)]
        + [pltpu.SMEM((wide_count,), jnp.int32)] * 2
        + [pltpu.SemaphoreType.DMA((len(given),))],
        compiler_params=pltpu.CompilerParams(vmem_limit_bytes=32 * 2**20),
        cost_estimate=pl.CostEstimate(flops=2**30, bytes_accessed=2**20, transcendentals=0),
        name="pack",
    )(*given)
    got = lax.all_to_all(
        send.reshape(message_count, length // PAIR, PAIR, width),
        ("narrow", "wide"),
        split_axis=0,
        concat_axis=0,
        tiled=True,
    ).reshape(message_count * length, width)
    return pl.pallas_call(
        functools.partial(ladder_kernel, rows, depth_count, own_count, recv_count),
        out_shape=jax.ShapeDtypeStruct((row_count, own_count * width), jnp.float32),
        in_specs=[vmem] * 2,
        out_specs=vmem,
        scratch_shapes=[
            pltpu.VMEM(((recv_count + 1) * width, own_count * width), kind),
            pltpu.SMEM((recv_count + 1,), jnp.int32),
            pltpu.SMEM((wide_count,), jnp.int32),
        ],
        compiler_params=pltpu.CompilerParams(vmem_limit_bytes=32 * 2**20),
        name="ladder",
    )(amplitudes, got)


def solution(mesh):
    return jax.shard_map(
        shards,
        mesh=mesh,
        in_specs=(
            P("narrow", None),
            P("wide", "narrow", None),
            P("wide"),
            P("wide"),
            P("wide"),
            P(),
        ),
        out_specs=P("narrow", "wide"),
        check_vma=False,
    )
```

```python
import functools

import jax
import jax.numpy as jnp
from jax import lax
from jax.experimental import pallas as pl
from jax.experimental.pallas import tpu as pltpu
from jax.sharding import PartitionSpec as P

PAIR = 2
GROUP = 4
UNROLL = 8


def each(count, body, start):
    if count > UNROLL:
        return lax.fori_loop(0, count, body, start)
    for i in range(count):
        start = body(i, start)
    return start


def message_at(index, length):
    start = index * length
    if not isinstance(index, int):
        start = pl.multiple_of(start, length)
    return start


def route_kernel(own_count, wide_count, *refs):
    sources, (order_ref, label_ref, near_ref), targets, sems = refs[:5], refs[5:8], refs[8:12], refs[12]
    in_tile, counts, out_tile, owner_map = targets
    copies = [
        pltpu.make_async_copy(source, target, sems.at[i])
        for i, (source, target) in enumerate(zip(sources, (*targets, near_ref)))
    ]
    for copy in copies:
        copy.start()
    for copy in copies[:4]:
        copy.wait()
    slot_count, rows, width = near_ref.shape
    column = lax.broadcasted_iota(jnp.int32, (1, slot_count * rows), 1)
    owners = lax.broadcasted_iota(jnp.int32, (wide_count, width), 0)

    def route(h, carry):
        owner_of, labels = carry
        spot = owner_map[out_tile[h]]
        owner = lax.div(spot, own_count)
        label = in_tile[h] * own_count + lax.rem(spot, own_count) + 1
        label = jnp.where(h < counts[0], label, 0)
        owner_of = jnp.where(lax.div(column, rows) == h, owner, owner_of)
        return owner_of, jnp.where(owners == owner, label, labels)

    start = (jnp.zeros_like(column), jnp.zeros((wide_count, width), jnp.int32))
    owner_of, labels = each(slot_count, route, start)
    label_ref[...] = labels.astype(jnp.float32).astype(label_ref.dtype)
    row = lax.broadcasted_iota(jnp.int32, (wide_count * rows, 1), 0)
    hit = row == owner_of * rows + lax.rem(column, rows)
    order_ref[...] = hit.astype(jnp.float32).astype(order_ref.dtype)
    copies[4].wait()


def pack_kernel(wide_count, near_count, order_ref, label_ref, near_ref, far_ref, send_ref, both, ordered):
    slot_count, rows, width = near_ref.shape
    length = send_ref.shape[0] // (wide_count * near_count)
    for side, ref in enumerate((near_ref, far_ref)):
        block = ref[...]
        if rows % 16 != 0:
            block = block.astype(jnp.float32)
        block = block.reshape(slot_count * rows, width).astype(both.dtype)
        both[:, side * width : (side + 1) * width] = block
    ordered[...] = jnp.dot(order_ref[...], both[...], preferred_element_type=jnp.float32)
    labels = label_ref[...].astype(jnp.float32)
    ids = lax.broadcasted_iota(jnp.int32, labels.shape, 0)

    def write(owner, _):
        spot = owner * rows
        if not isinstance(owner, int):
            spot = pl.multiple_of(spot, rows)
        near = ordered[pl.ds(spot, rows), :width]
        far = ordered[pl.ds(spot, rows), width:]
        label = jnp.sum(jnp.where(ids == owner, labels, 0.0), axis=0, keepdims=True)
        label = jnp.broadcast_to(label, (length - 2 * rows, width))
        if length % 16 == 0:
            pieces = [(0, jnp.concatenate([near, far, label], axis=0))]
        else:
            pieces = [(0, near), (rows, far), (2 * rows, label)]
        for z in range(near_count):
            start = message_at(owner * near_count + z, length)
            for offset, piece in pieces:
                send_ref[pl.ds(start + offset, piece.shape[0])] = piece.astype(send_ref.dtype)
        return 0

    each(wide_count, write, 0)


def ladder_kernel(
    rows, near_count, own_count, recv_count, amp_ref, got_ref, out_ref, tiles, column, seen
):
    wide_count = seen.shape[0]
    width = got_ref.shape[1]
    length = got_ref.shape[0] // (wide_count * near_count)
    upper = lax.axis_index("narrow") >= near_count
    tiles[...] = jnp.zeros_like(tiles)
    for u in range(recv_count):
        column[u] = 0

    def message(w, z):
        start = message_at(w * near_count + z, length)
        if length % 16 == 0:
            block = got_ref[pl.ds(start, length)].astype(jnp.float32)
            return block[:rows], block[rows : 2 * rows]
        return got_ref[pl.ds(start, rows)], got_ref[pl.ds(start + rows, rows)]

    def read_label(w):
        start = message_at(w * near_count, length)
        if length % 16 == 0:
            label = got_ref[pl.ds(start, length)].astype(jnp.float32)[2 * rows :]
        else:
            label = got_ref[pl.ds(start + 2 * rows, length - 2 * rows)].astype(jnp.float32)
        return jnp.max(label).astype(jnp.int32)

    def keep(w, label, found):
        live = jnp.minimum(label, 1)
        at = jnp.minimum(found, recv_count)
        place = jnp.maximum(label - 1, 0)
        column[at] = lax.div(place, own_count)
        spot = lax.rem(place, own_count)
        parts = [message(w, z) for z in range(near_count)]
        near = jnp.concatenate([part[0] for part in parts], axis=0).astype(tiles.dtype)
        far = jnp.concatenate([part[1] for part in parts], axis=0).astype(tiles.dtype)
        halves = [jnp.where(upper, far, near), jnp.where(upper, near, far)]
        tile = jnp.concatenate(halves, axis=0)
        at = pl.multiple_of(at * width, width)
        for q in range(own_count):
            kept = jnp.where((live > 0) & (spot == q), tile, jnp.zeros_like(tile))
            tiles[pl.ds(at, width), q * width : (q + 1) * width] = kept
        return found + live

    if wide_count <= UNROLL:
        labels = [read_label(w) for w in range(wide_count)]
        found = jnp.int32(0)
        for w in range(wide_count):
            found = keep(w, labels[w], found)
    else:

        def note(w, _):
            seen[w] = read_label(w)
            return 0

        lax.fori_loop(0, wide_count, note, 0)
        lax.fori_loop(0, wide_count, lambda w, found: keep(w, seen[w], found), jnp.int32(0))
    total = None
    for first in range(0, recv_count, GROUP):
        last = min(first + GROUP, recv_count)
        spots = [pl.multiple_of(column[u] * width, width) for u in range(first, last)]
        picked = jnp.concatenate([amp_ref[:, pl.ds(spot, width)] for spot in spots], axis=1)
        term = jnp.dot(
            picked, tiles[first * width : last * width], preferred_element_type=jnp.float32
        )
        total = term if total is None else total + term
    out_ref[...] = total


def shards(amplitudes, integrals, in_tile, counts, out_tile, owner_map):
    slot_count, rows, width = integrals.shape
    row_count = amplitudes.shape[0]
    wide_count = lax.axis_size("wide")
    depth_count = lax.axis_size("narrow")
    own_count = owner_map.shape[0] // wide_count
    recv_count = slot_count // 2
    near_count = depth_count // 2
    kind = integrals.dtype
    message_count = wide_count * near_count
    length = 2 * rows + PAIR
    if wide_count > UNROLL or length % PAIR != 0 or message_count * length % 16 != 0:
        length = -(-length // 16) * 16
    hbm = pl.BlockSpec(memory_space=pltpu.HBM)
    vmem = pl.BlockSpec(memory_space=pltpu.VMEM)
    limit = pltpu.CompilerParams(vmem_limit_bytes=32 * 2**20)
    across = [(z, (z + near_count) % depth_count) for z in range(depth_count)]
    far = lax.ppermute(integrals, "narrow", across)
    given = [in_tile, counts, out_tile, owner_map, integrals]
    given = [
        value if value.size == 1 else pltpu.with_memory_space_constraint(value, pltpu.HBM)
        for value in given
    ]
    ordered, sent = wide_count * rows, slot_count * rows
    order, labels, near = pl.pallas_call(
        functools.partial(route_kernel, own_count, wide_count),
        out_shape=[
            jax.ShapeDtypeStruct((ordered, sent), kind),
            jax.ShapeDtypeStruct((wide_count, width), kind),
            jax.ShapeDtypeStruct(integrals.shape, kind),
        ],
        in_specs=[hbm] * len(given),
        out_specs=[vmem] * 3,
        scratch_shapes=[pltpu.SMEM(value.shape, value.dtype) for value in given[:-1]]
        + [pltpu.SemaphoreType.DMA((len(given),))],
        compiler_params=limit,
        cost_estimate=pl.CostEstimate(flops=2**30, bytes_accessed=2**20, transcendentals=0),
        name="route",
    )(*given)
    send = pl.pallas_call(
        functools.partial(pack_kernel, wide_count, near_count),
        out_shape=jax.ShapeDtypeStruct((message_count * length, width), kind),
        in_specs=[vmem] * 4,
        out_specs=vmem,
        scratch_shapes=[
            pltpu.VMEM((sent, 2 * width), kind),
            pltpu.VMEM((ordered, 2 * width), jnp.float32),
        ],
        compiler_params=limit,
        name="pack",
    )(order, labels, near, far)
    groups = [
        [w * depth_count + half * near_count + z for w in range(wide_count) for z in range(near_count)]
        for half in range(2)
    ]
    got = lax.all_to_all(
        send.reshape(message_count, length // PAIR, PAIR, width),
        ("wide", "narrow"),
        split_axis=0,
        concat_axis=0,
        tiled=True,
        axis_index_groups=groups,
    ).reshape(message_count * length, width)
    return pl.pallas_call(
        functools.partial(ladder_kernel, rows, near_count, own_count, recv_count),
        out_shape=jax.ShapeDtypeStruct((row_count, own_count * width), jnp.float32),
        in_specs=[vmem] * 2,
        out_specs=vmem,
        scratch_shapes=[
            pltpu.VMEM(((recv_count + 1) * width, own_count * width), kind),
            pltpu.SMEM((recv_count + 1,), jnp.int32),
            pltpu.SMEM((wide_count,), jnp.int32),
        ],
        compiler_params=limit,
        name="ladder",
    )(amplitudes, got)


def solution(mesh):
    return jax.shard_map(
        shards,
        mesh=mesh,
        in_specs=(
            P("narrow", None),
            P("wide", "narrow", None),
            P("wide"),
            P("wide"),
            P("wide"),
            P(),
        ),
        out_specs=P("narrow", "wide"),
        check_vma=False,
    )
```

```python
import functools

import jax
import jax.numpy as jnp
from jax import lax
from jax.experimental import pallas as pl
from jax.experimental.pallas import tpu as pltpu
from jax.sharding import PartitionSpec as P

PAIR = 2
GROUP = 4
PARTS = 2
UNROLL = 8


def each(count, body, start):
    if count > UNROLL:
        return lax.fori_loop(0, count, body, start)
    for i in range(count):
        start = body(i, start)
    return start


def message_at(index, length):
    start = index * length
    if not isinstance(index, int):
        start = pl.multiple_of(start, length)
    return start


def route_kernel(own_count, wide_count, *refs):
    sources, (order_ref, label_ref, near_ref), targets, sems = refs[:5], refs[5:8], refs[8:12], refs[12]
    in_tile, counts, out_tile, owner_map = targets
    copies = [
        pltpu.make_async_copy(source, target, sems.at[i])
        for i, (source, target) in enumerate(zip(sources, (*targets, near_ref)))
    ]
    for copy in copies:
        copy.start()
    for copy in copies[:4]:
        copy.wait()
    slot_count, rows, width = near_ref.shape
    column = lax.broadcasted_iota(jnp.int32, (1, slot_count * rows), 1)
    owners = lax.broadcasted_iota(jnp.int32, (wide_count, width), 0)

    def route(h, carry):
        owner_of, labels = carry
        spot = owner_map[out_tile[h]]
        owner = lax.div(spot, own_count)
        label = in_tile[h] * own_count + lax.rem(spot, own_count) + 1
        label = jnp.where(h < counts[0], label, 0)
        owner_of = jnp.where(lax.div(column, rows) == h, owner, owner_of)
        return owner_of, jnp.where(owners == owner, label, labels)

    start = (jnp.zeros_like(column), jnp.zeros((wide_count, width), jnp.int32))
    owner_of, labels = each(slot_count, route, start)
    label_ref[...] = labels.astype(jnp.float32).astype(label_ref.dtype)
    row = lax.broadcasted_iota(jnp.int32, (wide_count * rows, 1), 0)
    hit = row == owner_of * rows + lax.rem(column, rows)
    order_ref[...] = hit.astype(jnp.float32).astype(order_ref.dtype)
    copies[4].wait()


def pack_kernel(wide_count, near_count, order_ref, label_ref, near_ref, far_ref, send_ref, both, ordered):
    slot_count, rows, width = near_ref.shape
    length = send_ref.shape[0] // (wide_count * near_count)
    for side, ref in enumerate((near_ref, far_ref)):
        block = ref[...]
        if rows % 16 != 0:
            block = block.astype(jnp.float32)
        block = block.reshape(slot_count * rows, width).astype(both.dtype)
        both[:, side * width : (side + 1) * width] = block
    ordered[...] = jnp.dot(order_ref[...], both[...], preferred_element_type=jnp.float32)
    labels = label_ref[...].astype(jnp.float32)
    ids = lax.broadcasted_iota(jnp.int32, labels.shape, 0)

    def write(owner, _):
        spot = owner * rows
        if not isinstance(owner, int):
            spot = pl.multiple_of(spot, rows)
        near = ordered[pl.ds(spot, rows), :width]
        far = ordered[pl.ds(spot, rows), width:]
        label = jnp.sum(jnp.where(ids == owner, labels, 0.0), axis=0, keepdims=True)
        label = jnp.broadcast_to(label, (length - 2 * rows, width))
        if length % 16 == 0:
            pieces = [(0, jnp.concatenate([near, far, label], axis=0))]
        else:
            pieces = [(0, near), (rows, far), (2 * rows, label)]
        for z in range(near_count):
            start = message_at(owner * near_count + z, length)
            for offset, piece in pieces:
                send_ref[pl.ds(start + offset, piece.shape[0])] = piece.astype(send_ref.dtype)
        return 0

    each(wide_count, write, 0)


def ladder_kernel(
    rows, near_count, own_count, recv_count, amp_ref, got_ref, out_hbm, out_ref, tiles, column, seen, sems
):
    wide_count = seen.shape[0]
    width = got_ref.shape[1]
    length = got_ref.shape[0] // (wide_count * near_count)
    upper = lax.axis_index("narrow") >= near_count
    tiles[...] = jnp.zeros_like(tiles)
    for u in range(recv_count):
        column[u] = 0

    def message(w, z):
        start = message_at(w * near_count + z, length)
        if length % 16 == 0:
            block = got_ref[pl.ds(start, length)].astype(jnp.float32)
            return block[:rows], block[rows : 2 * rows]
        return got_ref[pl.ds(start, rows)], got_ref[pl.ds(start + rows, rows)]

    def read_label(w):
        start = message_at(w * near_count, length)
        if length % 16 == 0:
            label = got_ref[pl.ds(start, length)].astype(jnp.float32)[2 * rows :]
        else:
            label = got_ref[pl.ds(start + 2 * rows, length - 2 * rows)].astype(jnp.float32)
        return jnp.max(label).astype(jnp.int32)

    def keep(w, label, found):
        live = jnp.minimum(label, 1)
        at = jnp.minimum(found, recv_count)
        place = jnp.maximum(label - 1, 0)
        column[at] = lax.div(place, own_count)
        spot = lax.rem(place, own_count)
        parts = [message(w, z) for z in range(near_count)]
        near = jnp.concatenate([part[0] for part in parts], axis=0).astype(tiles.dtype)
        far = jnp.concatenate([part[1] for part in parts], axis=0).astype(tiles.dtype)
        halves = [jnp.where(upper, far, near), jnp.where(upper, near, far)]
        tile = jnp.concatenate(halves, axis=0)
        at = pl.multiple_of(at * width, width)
        for q in range(own_count):
            kept = jnp.where((live > 0) & (spot == q), tile, jnp.zeros_like(tile))
            tiles[pl.ds(at, width), q * width : (q + 1) * width] = kept
        return found + live

    if wide_count <= UNROLL:
        labels = [read_label(w) for w in range(wide_count)]
        found = jnp.int32(0)
        for w in range(wide_count):
            found = keep(w, labels[w], found)
    else:

        def note(w, _):
            seen[w] = read_label(w)
            return 0

        lax.fori_loop(0, wide_count, note, 0)
        lax.fori_loop(0, wide_count, lambda w, found: keep(w, seen[w], found), jnp.int32(0))
    row_count = amp_ref.shape[0]
    chunk = row_count // PARTS
    copies = []
    for part in range(PARTS):
        at = slice(part * chunk, (part + 1) * chunk)
        total = None
        for first in range(0, recv_count, GROUP):
            last = min(first + GROUP, recv_count)
            spots = [pl.multiple_of(column[u] * width, width) for u in range(first, last)]
            picked = [amp_ref[at, pl.ds(spot, width)] for spot in spots]
            term = jnp.dot(
                jnp.concatenate(picked, axis=1),
                tiles[first * width : last * width],
                preferred_element_type=jnp.float32,
            )
            total = term if total is None else total + term
        out_ref[at] = total
        copies.append(pltpu.make_async_copy(out_ref.at[at], out_hbm.at[at], sems.at[part]))
        copies[-1].start()
    for copy in copies:
        copy.wait()


def shards(amplitudes, integrals, in_tile, counts, out_tile, owner_map):
    slot_count, rows, width = integrals.shape
    row_count = amplitudes.shape[0]
    wide_count = lax.axis_size("wide")
    depth_count = lax.axis_size("narrow")
    own_count = owner_map.shape[0] // wide_count
    recv_count = slot_count // 2
    near_count = depth_count // 2
    kind = integrals.dtype
    message_count = wide_count * near_count
    length = 2 * rows + PAIR
    if wide_count > UNROLL or length % PAIR != 0 or message_count * length % 16 != 0:
        length = -(-length // 16) * 16
    hbm = pl.BlockSpec(memory_space=pltpu.HBM)
    vmem = pl.BlockSpec(memory_space=pltpu.VMEM)
    limit = pltpu.CompilerParams(vmem_limit_bytes=32 * 2**20)
    across = [(z, (z + near_count) % depth_count) for z in range(depth_count)]
    far = lax.ppermute(integrals, "narrow", across)
    given = [in_tile, counts, out_tile, owner_map, integrals]
    given = [
        value if value.size == 1 else pltpu.with_memory_space_constraint(value, pltpu.HBM)
        for value in given
    ]
    ordered, sent = wide_count * rows, slot_count * rows
    order, labels, near = pl.pallas_call(
        functools.partial(route_kernel, own_count, wide_count),
        out_shape=[
            jax.ShapeDtypeStruct((ordered, sent), kind),
            jax.ShapeDtypeStruct((wide_count, width), kind),
            jax.ShapeDtypeStruct(integrals.shape, kind),
        ],
        in_specs=[hbm] * len(given),
        out_specs=[vmem] * 3,
        scratch_shapes=[pltpu.SMEM(value.shape, value.dtype) for value in given[:-1]]
        + [pltpu.SemaphoreType.DMA((len(given),))],
        compiler_params=limit,
        cost_estimate=pl.CostEstimate(flops=2**30, bytes_accessed=2**20, transcendentals=0),
        name="route",
    )(*given)
    send = pl.pallas_call(
        functools.partial(pack_kernel, wide_count, near_count),
        out_shape=jax.ShapeDtypeStruct((message_count * length, width), kind),
        in_specs=[vmem] * 4,
        out_specs=vmem,
        scratch_shapes=[
            pltpu.VMEM((sent, 2 * width), kind),
            pltpu.VMEM((ordered, 2 * width), jnp.float32),
        ],
        compiler_params=limit,
        name="pack",
    )(order, labels, near, far)
    groups = [
        [w * depth_count + half * near_count + z for w in range(wide_count) for z in range(near_count)]
        for half in range(2)
    ]
    got = lax.all_to_all(
        send.reshape(message_count, length // PAIR, PAIR, width),
        ("wide", "narrow"),
        split_axis=0,
        concat_axis=0,
        tiled=True,
        axis_index_groups=groups,
    ).reshape(message_count * length, width)
    return pl.pallas_call(
        functools.partial(ladder_kernel, rows, near_count, own_count, recv_count),
        out_shape=jax.ShapeDtypeStruct((row_count, own_count * width), jnp.float32),
        in_specs=[vmem] * 2,
        out_specs=hbm,
        scratch_shapes=[
            pltpu.VMEM((row_count, own_count * width), jnp.float32),
            pltpu.VMEM(((recv_count + 1) * width, own_count * width), kind),
            pltpu.SMEM((recv_count + 1,), jnp.int32),
            pltpu.SMEM((wide_count,), jnp.int32),
            pltpu.SemaphoreType.DMA((PARTS,)),
        ],
        compiler_params=limit,
        name="ladder",
    )(amplitudes, got)


def solution(mesh):
    return jax.shard_map(
        shards,
        mesh=mesh,
        in_specs=(
            P("narrow", None),
            P("wide", "narrow", None),
            P("wide"),
            P("wide"),
            P("wide"),
            P(),
        ),
        out_specs=P("narrow", "wide"),
        check_vma=False,
    )
```

```python
import functools

import jax
import jax.numpy as jnp
from jax import lax
from jax.experimental import pallas as pl
from jax.experimental.pallas import tpu as pltpu
from jax.sharding import PartitionSpec as P

PAIR = 2
GROUP = 4
PARTS = 2
PIECES = 4
UNROLL = 8


def each(count, body, start):
    if count > UNROLL:
        return lax.fori_loop(0, count, body, start)
    for i in range(count):
        start = body(i, start)
    return start


def message_at(index, length):
    start = index * length
    if not isinstance(index, int):
        start = pl.multiple_of(start, length)
    return start


def route_kernel(own_count, wide_count, *refs):
    sources, (order_ref, label_ref, near_ref), targets, sems = refs[:5], refs[5:8], refs[8:12], refs[12]
    in_tile, counts, out_tile, owner_map = targets
    copies = [
        pltpu.make_async_copy(source, target, sems.at[i])
        for i, (source, target) in enumerate(zip(sources, (*targets, near_ref)))
    ]
    for copy in copies:
        copy.start()
    for copy in copies[:4]:
        copy.wait()
    slot_count, rows, width = near_ref.shape
    column = lax.broadcasted_iota(jnp.int32, (1, slot_count * rows), 1)
    owners = lax.broadcasted_iota(jnp.int32, (wide_count, width), 0)

    def route(h, carry):
        owner_of, labels = carry
        spot = owner_map[out_tile[h]]
        owner = lax.div(spot, own_count)
        label = in_tile[h] * own_count + lax.rem(spot, own_count) + 1
        label = jnp.where(h < counts[0], label, 0)
        owner_of = jnp.where(lax.div(column, rows) == h, owner, owner_of)
        return owner_of, jnp.where(owners == owner, label, labels)

    start = (jnp.zeros_like(column), jnp.zeros((wide_count, width), jnp.int32))
    owner_of, labels = each(slot_count, route, start)
    label_ref[...] = labels.astype(jnp.float32).astype(label_ref.dtype)
    row = lax.broadcasted_iota(jnp.int32, (wide_count * rows, 1), 0)
    hit = row == owner_of * rows + lax.rem(column, rows)
    order_ref[...] = hit.astype(jnp.float32).astype(order_ref.dtype)
    copies[4].wait()


def pack_kernel(wide_count, near_count, order_ref, label_ref, near_ref, far_ref, send_ref, both, ordered):
    slot_count, rows, width = near_ref.shape
    length = send_ref.shape[0] // (wide_count * near_count)
    for side, ref in enumerate((near_ref, far_ref)):
        block = ref[...]
        if rows % 16 != 0:
            block = block.astype(jnp.float32)
        block = block.reshape(slot_count * rows, width).astype(both.dtype)
        both[:, side * width : (side + 1) * width] = block
    ordered[...] = jnp.dot(order_ref[...], both[...], preferred_element_type=jnp.float32)
    labels = label_ref[...].astype(jnp.float32)
    ids = lax.broadcasted_iota(jnp.int32, labels.shape, 0)

    def write(owner, _):
        spot = owner * rows
        if not isinstance(owner, int):
            spot = pl.multiple_of(spot, rows)
        near = ordered[pl.ds(spot, rows), :width]
        far = ordered[pl.ds(spot, rows), width:]
        label = jnp.sum(jnp.where(ids == owner, labels, 0.0), axis=0, keepdims=True)
        label = jnp.broadcast_to(label, (length - 2 * rows, width))
        if length % 16 == 0:
            pieces = [(0, jnp.concatenate([near, far, label], axis=0))]
        else:
            pieces = [(0, near), (rows, far), (2 * rows, label)]
        for z in range(near_count):
            start = message_at(z * wide_count + owner, length)
            for offset, piece in pieces:
                send_ref[pl.ds(start + offset, piece.shape[0])] = piece.astype(send_ref.dtype)
        return 0

    each(wide_count, write, 0)


def ladder_kernel(
    rows, near_count, own_count, recv_count, amp_ref, got_ref, out_hbm, out_ref, tiles, column, seen, sems
):
    wide_count = seen.shape[0]
    width = got_ref.shape[1]
    length = got_ref.shape[0] // (wide_count * near_count)
    upper = lax.axis_index("narrow") >= near_count
    tiles[...] = jnp.zeros_like(tiles)
    for u in range(recv_count):
        column[u] = 0

    def message(w, z):
        start = message_at(z * wide_count + w, length)
        if length % 16 == 0:
            block = got_ref[pl.ds(start, length)].astype(jnp.float32)
            return block[:rows], block[rows : 2 * rows]
        return got_ref[pl.ds(start, rows)], got_ref[pl.ds(start + rows, rows)]

    def read_label(w):
        start = message_at(w, length)
        if length % 16 == 0:
            label = got_ref[pl.ds(start, length)].astype(jnp.float32)[2 * rows :]
        else:
            label = got_ref[pl.ds(start + 2 * rows, length - 2 * rows)].astype(jnp.float32)
        return jnp.max(label).astype(jnp.int32)

    def keep(w, label, found):
        live = jnp.minimum(label, 1)
        at = jnp.minimum(found, recv_count)
        place = jnp.maximum(label - 1, 0)
        column[at] = lax.div(place, own_count)
        spot = lax.rem(place, own_count)
        parts = [message(w, z) for z in range(near_count)]
        near = jnp.concatenate([part[0] for part in parts], axis=0).astype(tiles.dtype)
        far = jnp.concatenate([part[1] for part in parts], axis=0).astype(tiles.dtype)
        halves = [jnp.where(upper, far, near), jnp.where(upper, near, far)]
        tile = jnp.concatenate(halves, axis=0)
        at = pl.multiple_of(at * width, width)
        for q in range(own_count):
            kept = jnp.where((live > 0) & (spot == q), tile, jnp.zeros_like(tile))
            tiles[pl.ds(at, width), q * width : (q + 1) * width] = kept
        return found + live

    if wide_count <= UNROLL:
        labels = [read_label(w) for w in range(wide_count)]
        found = jnp.int32(0)
        for w in range(wide_count):
            found = keep(w, labels[w], found)
    else:

        def note(w, _):
            seen[w] = read_label(w)
            return 0

        lax.fori_loop(0, wide_count, note, 0)
        lax.fori_loop(0, wide_count, lambda w, found: keep(w, seen[w], found), jnp.int32(0))
    row_count = amp_ref.shape[0]
    chunk = row_count // PARTS
    copies = []
    for part in range(PARTS):
        at = slice(part * chunk, (part + 1) * chunk)
        total = None
        for first in range(0, recv_count, GROUP):
            last = min(first + GROUP, recv_count)
            spots = [pl.multiple_of(column[u] * width, width) for u in range(first, last)]
            picked = [amp_ref[at, pl.ds(spot, width)] for spot in spots]
            term = jnp.dot(
                jnp.concatenate(picked, axis=1),
                tiles[first * width : last * width],
                preferred_element_type=jnp.float32,
            )
            total = term if total is None else total + term
        out_ref[at] = total
        for piece in range(PIECES):
            size = chunk // PIECES
            rows_at = pl.ds(part * chunk + piece * size, size)
            sem = sems.at[part * PIECES + piece]
            copy = pltpu.make_async_copy(out_ref.at[rows_at], out_hbm.at[rows_at], sem)
            copy.start()
            copies.append(copy)
    for copy in copies:
        copy.wait()


def shards(amplitudes, integrals, in_tile, counts, out_tile, owner_map):
    slot_count, rows, width = integrals.shape
    row_count = amplitudes.shape[0]
    wide_count = lax.axis_size("wide")
    depth_count = lax.axis_size("narrow")
    own_count = owner_map.shape[0] // wide_count
    recv_count = slot_count // 2
    near_count = depth_count // 2
    kind = integrals.dtype
    message_count = wide_count * near_count
    length = 2 * rows + PAIR
    if wide_count > UNROLL or length % PAIR != 0 or message_count * length % 16 != 0:
        length = -(-length // 16) * 16
    hbm = pl.BlockSpec(memory_space=pltpu.HBM)
    vmem = pl.BlockSpec(memory_space=pltpu.VMEM)
    limit = pltpu.CompilerParams(vmem_limit_bytes=32 * 2**20)
    across = [(z, (z + near_count) % depth_count) for z in range(depth_count)]
    far = lax.ppermute(integrals, "narrow", across)
    given = [in_tile, counts, out_tile, owner_map, integrals]
    given = [
        value if value.size == 1 else pltpu.with_memory_space_constraint(value, pltpu.HBM)
        for value in given
    ]
    ordered, sent = wide_count * rows, slot_count * rows
    order, labels, near = pl.pallas_call(
        functools.partial(route_kernel, own_count, wide_count),
        out_shape=[
            jax.ShapeDtypeStruct((ordered, sent), kind),
            jax.ShapeDtypeStruct((wide_count, width), kind),
            jax.ShapeDtypeStruct(integrals.shape, kind),
        ],
        in_specs=[hbm] * len(given),
        out_specs=[vmem] * 3,
        scratch_shapes=[pltpu.SMEM(value.shape, value.dtype) for value in given[:-1]]
        + [pltpu.SemaphoreType.DMA((len(given),))],
        compiler_params=limit,
        cost_estimate=pl.CostEstimate(flops=2**30, bytes_accessed=2**20, transcendentals=0),
        name="route",
    )(*given)
    send = pl.pallas_call(
        functools.partial(pack_kernel, wide_count, near_count),
        out_shape=jax.ShapeDtypeStruct((message_count * length, width), kind),
        in_specs=[vmem] * 4,
        out_specs=vmem,
        scratch_shapes=[
            pltpu.VMEM((sent, 2 * width), kind),
            pltpu.VMEM((ordered, 2 * width), jnp.float32),
        ],
        compiler_params=limit,
        name="pack",
    )(order, labels, near, far)
    groups = [
        [w * depth_count + half * near_count + z for z in range(near_count) for w in range(wide_count)]
        for half in range(2)
    ]
    got = lax.all_to_all(
        send.reshape(message_count, length // PAIR, PAIR, width),
        ("wide", "narrow"),
        split_axis=0,
        concat_axis=0,
        tiled=True,
        axis_index_groups=groups,
    ).reshape(message_count * length, width)
    return pl.pallas_call(
        functools.partial(ladder_kernel, rows, near_count, own_count, recv_count),
        out_shape=jax.ShapeDtypeStruct((row_count, own_count * width), jnp.float32),
        in_specs=[vmem] * 2,
        out_specs=hbm,
        scratch_shapes=[
            pltpu.VMEM((row_count, own_count * width), jnp.float32),
            pltpu.VMEM(((recv_count + 1) * width, own_count * width), kind),
            pltpu.SMEM((recv_count + 1,), jnp.int32),
            pltpu.SMEM((wide_count,), jnp.int32),
            pltpu.SemaphoreType.DMA((PARTS * PIECES,)),
        ],
        compiler_params=limit,
        name="ladder",
    )(amplitudes, got)


def solution(mesh):
    return jax.shard_map(
        shards,
        mesh=mesh,
        in_specs=(
            P("narrow", None),
            P("wide", "narrow", None),
            P("wide"),
            P("wide"),
            P("wide"),
            P(),
        ),
        out_specs=P("narrow", "wide"),
        check_vma=False,
    )
```

```python
import functools

import jax
import jax.numpy as jnp
from jax import lax
from jax.experimental import pallas as pl
from jax.experimental.pallas import tpu as pltpu
from jax.sharding import PartitionSpec as P

PAIR = 2
GROUP = 4
UNROLL = 8
CORES = 2


def each(count, body, start):
    if count > UNROLL:
        return lax.fori_loop(0, count, body, start)
    for i in range(count):
        start = body(i, start)
    return start


def message_at(w, z, wide_count, near_count, length):
    core, chip = w % CORES, w // CORES
    index = (core * (wide_count // CORES) + chip) * near_count + z
    start = index * length
    if not isinstance(w, int):
        start = pl.multiple_of(start, length)
    return start


def route_kernel(own_count, wide_count, *refs):
    sources, (order_ref, label_ref, near_ref), targets, sems = refs[:5], refs[5:8], refs[8:12], refs[12]
    in_tile, counts, out_tile, owner_map = targets
    copies = [
        pltpu.make_async_copy(source, target, sems.at[i])
        for i, (source, target) in enumerate(zip(sources, (*targets, near_ref)))
    ]
    for copy in copies:
        copy.start()
    for copy in copies[:4]:
        copy.wait()
    slot_count, rows, width = near_ref.shape
    column = lax.broadcasted_iota(jnp.int32, (1, slot_count * rows), 1)
    owners = lax.broadcasted_iota(jnp.int32, (wide_count, width), 0)

    def route(h, carry):
        owner_of, labels = carry
        spot = owner_map[out_tile[h]]
        owner = lax.div(spot, own_count)
        label = in_tile[h] * own_count + lax.rem(spot, own_count) + 1
        label = jnp.where(h < counts[0], label, 0)
        owner_of = jnp.where(lax.div(column, rows) == h, owner, owner_of)
        return owner_of, jnp.where(owners == owner, label, labels)

    start = (jnp.zeros_like(column), jnp.zeros((wide_count, width), jnp.int32))
    owner_of, labels = each(slot_count, route, start)
    label_ref[...] = labels.astype(jnp.float32).astype(label_ref.dtype)
    row = lax.broadcasted_iota(jnp.int32, (wide_count * rows, 1), 0)
    hit = row == owner_of * rows + lax.rem(column, rows)
    order_ref[...] = hit.astype(jnp.float32).astype(order_ref.dtype)
    copies[4].wait()


def pack_kernel(wide_count, near_count, order_ref, label_ref, near_ref, far_ref, send_ref, both, ordered):
    slot_count, rows, width = near_ref.shape
    length = send_ref.shape[0] // (wide_count * near_count)
    for side, ref in enumerate((near_ref, far_ref)):
        block = ref[...]
        if rows % 16 != 0:
            block = block.astype(jnp.float32)
        block = block.reshape(slot_count * rows, width).astype(both.dtype)
        both[:, side * width : (side + 1) * width] = block
    ordered[...] = jnp.dot(order_ref[...], both[...], preferred_element_type=jnp.float32)
    labels = label_ref[...].astype(jnp.float32)
    ids = lax.broadcasted_iota(jnp.int32, labels.shape, 0)

    def write(owner, _):
        spot = owner * rows
        if not isinstance(owner, int):
            spot = pl.multiple_of(spot, rows)
        near = ordered[pl.ds(spot, rows), :width]
        far = ordered[pl.ds(spot, rows), width:]
        label = jnp.sum(jnp.where(ids == owner, labels, 0.0), axis=0, keepdims=True)
        label = jnp.broadcast_to(label, (length - 2 * rows, width))
        if length % 16 == 0:
            pieces = [(0, jnp.concatenate([near, far, label], axis=0))]
        else:
            pieces = [(0, near), (rows, far), (2 * rows, label)]
        for z in range(near_count):
            start = message_at(owner, z, wide_count, near_count, length)
            for offset, piece in pieces:
                send_ref[pl.ds(start + offset, piece.shape[0])] = piece.astype(send_ref.dtype)
        return 0

    each(wide_count, write, 0)


def ladder_kernel(
    rows, near_count, own_count, recv_count, amp_ref, got_ref, out_ref, tiles, column, seen
):
    wide_count = seen.shape[0]
    width = got_ref.shape[1]
    length = got_ref.shape[0] // (wide_count * near_count)
    upper = lax.axis_index("narrow") >= near_count
    tiles[...] = jnp.zeros_like(tiles)
    for u in range(recv_count):
        column[u] = 0

    def message(w, z):
        start = message_at(w, z, wide_count, near_count, length)
        if length % 16 == 0:
            block = got_ref[pl.ds(start, length)].astype(jnp.float32)
            return block[:rows], block[rows : 2 * rows]
        return got_ref[pl.ds(start, rows)], got_ref[pl.ds(start + rows, rows)]

    def read_label(w):
        start = message_at(w, 0, wide_count, near_count, length)
        if length % 16 == 0:
            label = got_ref[pl.ds(start, length)].astype(jnp.float32)[2 * rows :]
        else:
            label = got_ref[pl.ds(start + 2 * rows, length - 2 * rows)].astype(jnp.float32)
        return jnp.max(label).astype(jnp.int32)

    def keep(w, label, found):
        live = jnp.minimum(label, 1)
        at = jnp.minimum(found, recv_count)
        place = jnp.maximum(label - 1, 0)
        column[at] = lax.div(place, own_count)
        spot = lax.rem(place, own_count)
        parts = [message(w, z) for z in range(near_count)]
        near = jnp.concatenate([part[0] for part in parts], axis=0).astype(tiles.dtype)
        far = jnp.concatenate([part[1] for part in parts], axis=0).astype(tiles.dtype)
        halves = [jnp.where(upper, far, near), jnp.where(upper, near, far)]
        tile = jnp.concatenate(halves, axis=0)
        at = pl.multiple_of(at * width, width)
        for q in range(own_count):
            kept = jnp.where((live > 0) & (spot == q), tile, jnp.zeros_like(tile))
            tiles[pl.ds(at, width), q * width : (q + 1) * width] = kept
        return found + live

    if wide_count <= UNROLL:
        labels = [read_label(w) for w in range(wide_count)]
        found = jnp.int32(0)
        for w in range(wide_count):
            found = keep(w, labels[w], found)
    else:

        def note(w, _):
            seen[w] = read_label(w)
            return 0

        lax.fori_loop(0, wide_count, note, 0)
        lax.fori_loop(0, wide_count, lambda w, found: keep(w, seen[w], found), jnp.int32(0))
    total = None
    for first in range(0, recv_count, GROUP):
        last = min(first + GROUP, recv_count)
        spots = [pl.multiple_of(column[u] * width, width) for u in range(first, last)]
        picked = jnp.concatenate([amp_ref[:, pl.ds(spot, width)] for spot in spots], axis=1)
        term = jnp.dot(
            picked, tiles[first * width : last * width], preferred_element_type=jnp.float32
        )
        total = term if total is None else total + term
    out_ref[...] = total


def shards(amplitudes, integrals, in_tile, counts, out_tile, owner_map):
    slot_count, rows, width = integrals.shape
    row_count = amplitudes.shape[0]
    wide_count = lax.axis_size("wide")
    depth_count = lax.axis_size("narrow")
    own_count = owner_map.shape[0] // wide_count
    recv_count = slot_count // 2
    near_count = depth_count // 2
    kind = integrals.dtype
    message_count = wide_count * near_count
    length = 2 * rows + PAIR
    if wide_count > UNROLL or length % PAIR != 0 or message_count * length % 16 != 0:
        length = -(-length // 16) * 16
    hbm = pl.BlockSpec(memory_space=pltpu.HBM)
    vmem = pl.BlockSpec(memory_space=pltpu.VMEM)
    limit = pltpu.CompilerParams(vmem_limit_bytes=32 * 2**20)
    across = [(z, (z + near_count) % depth_count) for z in range(depth_count)]
    far = lax.ppermute(integrals, "narrow", across)
    given = [in_tile, counts, out_tile, owner_map, integrals]
    given = [
        value if value.size == 1 else pltpu.with_memory_space_constraint(value, pltpu.HBM)
        for value in given
    ]
    ordered, sent = wide_count * rows, slot_count * rows
    order, labels, near = pl.pallas_call(
        functools.partial(route_kernel, own_count, wide_count),
        out_shape=[
            jax.ShapeDtypeStruct((ordered, sent), kind),
            jax.ShapeDtypeStruct((wide_count, width), kind),
            jax.ShapeDtypeStruct(integrals.shape, kind),
        ],
        in_specs=[hbm] * len(given),
        out_specs=[vmem] * 3,
        scratch_shapes=[pltpu.SMEM(value.shape, value.dtype) for value in given[:-1]]
        + [pltpu.SemaphoreType.DMA((len(given),))],
        compiler_params=limit,
        cost_estimate=pl.CostEstimate(flops=2**30, bytes_accessed=2**20, transcendentals=0),
        name="route",
    )(*given)
    send = pl.pallas_call(
        functools.partial(pack_kernel, wide_count, near_count),
        out_shape=jax.ShapeDtypeStruct((message_count * length, width), kind),
        in_specs=[vmem] * 4,
        out_specs=vmem,
        scratch_shapes=[
            pltpu.VMEM((sent, 2 * width), kind),
            pltpu.VMEM((ordered, 2 * width), jnp.float32),
        ],
        compiler_params=limit,
        name="pack",
    )(order, labels, near, far)
    groups = [
        [
            (chip * CORES + core) * depth_count + half * near_count + z
            for core in range(CORES)
            for chip in range(wide_count // CORES)
            for z in range(near_count)
        ]
        for half in range(2)
    ]
    got = lax.all_to_all(
        send.reshape(message_count, length // PAIR, PAIR, width),
        ("wide", "narrow"),
        split_axis=0,
        concat_axis=0,
        tiled=True,
        axis_index_groups=groups,
    ).reshape(message_count * length, width)
    return pl.pallas_call(
        functools.partial(ladder_kernel, rows, near_count, own_count, recv_count),
        out_shape=jax.ShapeDtypeStruct((row_count, own_count * width), jnp.float32),
        in_specs=[vmem] * 2,
        out_specs=vmem,
        scratch_shapes=[
            pltpu.VMEM(((recv_count + 1) * width, own_count * width), kind),
            pltpu.SMEM((recv_count + 1,), jnp.int32),
            pltpu.SMEM((wide_count,), jnp.int32),
        ],
        compiler_params=limit,
        name="ladder",
    )(amplitudes, got)


def solution(mesh):
    return jax.shard_map(
        shards,
        mesh=mesh,
        in_specs=(
            P("narrow", None),
            P("wide", "narrow", None),
            P("wide"),
            P("wide"),
            P("wide"),
            P(),
        ),
        out_specs=P("narrow", "wide"),
        check_vma=False,
    )
```

```python
import functools

import jax
import jax.numpy as jnp
from jax import lax
from jax.experimental import pallas as pl
from jax.experimental.pallas import tpu as pltpu
from jax.sharding import PartitionSpec as P

PAIR = 2
GROUP = 4
UNROLL = 8


def each(count, body, start):
    if count > UNROLL:
        return lax.fori_loop(0, count, body, start)
    for i in range(count):
        start = body(i, start)
    return start


def message_at(w, z, wide_count, near_count, length):
    place = (w + wide_count // 2) % wide_count
    start = (place * near_count + z) * length
    if not isinstance(w, int):
        start = pl.multiple_of(start, length)
    return start


def route_kernel(own_count, wide_count, *refs):
    sources, (order_ref, label_ref, near_ref), targets, sems = refs[:5], refs[5:8], refs[8:12], refs[12]
    in_tile, counts, out_tile, owner_map = targets
    copies = [
        pltpu.make_async_copy(source, target, sems.at[i])
        for i, (source, target) in enumerate(zip(sources, (*targets, near_ref)))
    ]
    for copy in copies:
        copy.start()
    for copy in copies[:4]:
        copy.wait()
    slot_count, rows, width = near_ref.shape
    column = lax.broadcasted_iota(jnp.int32, (1, slot_count * rows), 1)
    owners = lax.broadcasted_iota(jnp.int32, (wide_count, width), 0)

    def route(h, carry):
        owner_of, labels = carry
        spot = owner_map[out_tile[h]]
        owner = lax.div(spot, own_count)
        label = in_tile[h] * own_count + lax.rem(spot, own_count) + 1
        label = jnp.where(h < counts[0], label, 0)
        owner_of = jnp.where(lax.div(column, rows) == h, owner, owner_of)
        return owner_of, jnp.where(owners == owner, label, labels)

    start = (jnp.zeros_like(column), jnp.zeros((wide_count, width), jnp.int32))
    owner_of, labels = each(slot_count, route, start)
    label_ref[...] = labels.astype(jnp.float32).astype(label_ref.dtype)
    row = lax.broadcasted_iota(jnp.int32, (wide_count * rows, 1), 0)
    hit = row == owner_of * rows + lax.rem(column, rows)
    order_ref[...] = hit.astype(jnp.float32).astype(order_ref.dtype)
    copies[4].wait()


def pack_kernel(wide_count, near_count, order_ref, label_ref, near_ref, far_ref, send_ref, both, ordered):
    slot_count, rows, width = near_ref.shape
    length = send_ref.shape[0] // (wide_count * near_count)
    for side, ref in enumerate((near_ref, far_ref)):
        block = ref[...]
        if rows % 16 != 0:
            block = block.astype(jnp.float32)
        block = block.reshape(slot_count * rows, width).astype(both.dtype)
        both[:, side * width : (side + 1) * width] = block
    ordered[...] = jnp.dot(order_ref[...], both[...], preferred_element_type=jnp.float32)
    labels = label_ref[...].astype(jnp.float32)
    ids = lax.broadcasted_iota(jnp.int32, labels.shape, 0)

    def write(owner, _):
        spot = owner * rows
        if not isinstance(owner, int):
            spot = pl.multiple_of(spot, rows)
        near = ordered[pl.ds(spot, rows), :width]
        far = ordered[pl.ds(spot, rows), width:]
        label = jnp.sum(jnp.where(ids == owner, labels, 0.0), axis=0, keepdims=True)
        label = jnp.broadcast_to(label, (length - 2 * rows, width))
        if length % 16 == 0:
            pieces = [(0, jnp.concatenate([near, far, label], axis=0))]
        else:
            pieces = [(0, near), (rows, far), (2 * rows, label)]
        for z in range(near_count):
            start = message_at(owner, z, wide_count, near_count, length)
            for offset, piece in pieces:
                send_ref[pl.ds(start + offset, piece.shape[0])] = piece.astype(send_ref.dtype)
        return 0

    each(wide_count, write, 0)


def ladder_kernel(
    rows, near_count, own_count, recv_count, amp_ref, got_ref, out_ref, tiles, column, seen
):
    wide_count = seen.shape[0]
    width = got_ref.shape[1]
    length = got_ref.shape[0] // (wide_count * near_count)
    upper = lax.axis_index("narrow") >= near_count
    tiles[...] = jnp.zeros_like(tiles)
    for u in range(recv_count):
        column[u] = 0

    def message(w, z):
        start = message_at(w, z, wide_count, near_count, length)
        if length % 16 == 0:
            block = got_ref[pl.ds(start, length)].astype(jnp.float32)
            return block[:rows], block[rows : 2 * rows]
        return got_ref[pl.ds(start, rows)], got_ref[pl.ds(start + rows, rows)]

    def read_label(w):
        start = message_at(w, 0, wide_count, near_count, length)
        if length % 16 == 0:
            label = got_ref[pl.ds(start, length)].astype(jnp.float32)[2 * rows :]
        else:
            label = got_ref[pl.ds(start + 2 * rows, length - 2 * rows)].astype(jnp.float32)
        return jnp.max(label).astype(jnp.int32)

    def keep(w, label, found):
        live = jnp.minimum(label, 1)
        at = jnp.minimum(found, recv_count)
        place = jnp.maximum(label - 1, 0)
        column[at] = lax.div(place, own_count)
        spot = lax.rem(place, own_count)
        parts = [message(w, z) for z in range(near_count)]
        near = jnp.concatenate([part[0] for part in parts], axis=0).astype(tiles.dtype)
        far = jnp.concatenate([part[1] for part in parts], axis=0).astype(tiles.dtype)
        halves = [jnp.where(upper, far, near), jnp.where(upper, near, far)]
        tile = jnp.concatenate(halves, axis=0)
        at = pl.multiple_of(at * width, width)
        for q in range(own_count):
            kept = jnp.where((live > 0) & (spot == q), tile, jnp.zeros_like(tile))
            tiles[pl.ds(at, width), q * width : (q + 1) * width] = kept
        return found + live

    if wide_count <= UNROLL:
        labels = [read_label(w) for w in range(wide_count)]
        found = jnp.int32(0)
        for w in range(wide_count):
            found = keep(w, labels[w], found)
    else:

        def note(w, _):
            seen[w] = read_label(w)
            return 0

        lax.fori_loop(0, wide_count, note, 0)
        lax.fori_loop(0, wide_count, lambda w, found: keep(w, seen[w], found), jnp.int32(0))
    total = None
    for first in range(0, recv_count, GROUP):
        last = min(first + GROUP, recv_count)
        spots = [pl.multiple_of(column[u] * width, width) for u in range(first, last)]
        picked = jnp.concatenate([amp_ref[:, pl.ds(spot, width)] for spot in spots], axis=1)
        term = jnp.dot(
            picked, tiles[first * width : last * width], preferred_element_type=jnp.float32
        )
        total = term if total is None else total + term
    out_ref[...] = total


def shards(amplitudes, integrals, in_tile, counts, out_tile, owner_map):
    slot_count, rows, width = integrals.shape
    row_count = amplitudes.shape[0]
    wide_count = lax.axis_size("wide")
    depth_count = lax.axis_size("narrow")
    own_count = owner_map.shape[0] // wide_count
    recv_count = slot_count // 2
    near_count = depth_count // 2
    kind = integrals.dtype
    message_count = wide_count * near_count
    length = 2 * rows + PAIR
    if wide_count > UNROLL or length % PAIR != 0 or message_count * length % 16 != 0:
        length = -(-length // 16) * 16
    hbm = pl.BlockSpec(memory_space=pltpu.HBM)
    vmem = pl.BlockSpec(memory_space=pltpu.VMEM)
    limit = pltpu.CompilerParams(vmem_limit_bytes=32 * 2**20)
    across = [(z, (z + near_count) % depth_count) for z in range(depth_count)]
    far = lax.ppermute(integrals, "narrow", across)
    given = [in_tile, counts, out_tile, owner_map, integrals]
    given = [
        value if value.size == 1 else pltpu.with_memory_space_constraint(value, pltpu.HBM)
        for value in given
    ]
    ordered, sent = wide_count * rows, slot_count * rows
    order, labels, near = pl.pallas_call(
        functools.partial(route_kernel, own_count, wide_count),
        out_shape=[
            jax.ShapeDtypeStruct((ordered, sent), kind),
            jax.ShapeDtypeStruct((wide_count, width), kind),
            jax.ShapeDtypeStruct(integrals.shape, kind),
        ],
        in_specs=[hbm] * len(given),
        out_specs=[vmem] * 3,
        scratch_shapes=[pltpu.SMEM(value.shape, value.dtype) for value in given[:-1]]
        + [pltpu.SemaphoreType.DMA((len(given),))],
        compiler_params=limit,
        cost_estimate=pl.CostEstimate(flops=2**30, bytes_accessed=2**20, transcendentals=0),
        name="route",
    )(*given)
    send = pl.pallas_call(
        functools.partial(pack_kernel, wide_count, near_count),
        out_shape=jax.ShapeDtypeStruct((message_count * length, width), kind),
        in_specs=[vmem] * 4,
        out_specs=vmem,
        scratch_shapes=[
            pltpu.VMEM((sent, 2 * width), kind),
            pltpu.VMEM((ordered, 2 * width), jnp.float32),
        ],
        compiler_params=limit,
        name="pack",
    )(order, labels, near, far)
    groups = [
        [
            (place - wide_count // 2) % wide_count * depth_count + half * near_count + z
            for place in range(wide_count)
            for z in range(near_count)
        ]
        for half in range(2)
    ]
    got = lax.all_to_all(
        send.reshape(message_count, length // PAIR, PAIR, width),
        ("wide", "narrow"),
        split_axis=0,
        concat_axis=0,
        tiled=True,
        axis_index_groups=groups,
    ).reshape(message_count * length, width)
    return pl.pallas_call(
        functools.partial(ladder_kernel, rows, near_count, own_count, recv_count),
        out_shape=jax.ShapeDtypeStruct((row_count, own_count * width), jnp.float32),
        in_specs=[vmem] * 2,
        out_specs=vmem,
        scratch_shapes=[
            pltpu.VMEM(((recv_count + 1) * width, own_count * width), kind),
            pltpu.SMEM((recv_count + 1,), jnp.int32),
            pltpu.SMEM((wide_count,), jnp.int32),
        ],
        compiler_params=limit,
        name="ladder",
    )(amplitudes, got)


def solution(mesh):
    return jax.shard_map(
        shards,
        mesh=mesh,
        in_specs=(
            P("narrow", None),
            P("wide", "narrow", None),
            P("wide"),
            P("wide"),
            P("wide"),
            P(),
        ),
        out_specs=P("narrow", "wide"),
        check_vma=False,
    )
```

```python
import functools

import jax
import jax.numpy as jnp
from jax import lax
from jax.experimental import pallas as pl
from jax.experimental.pallas import tpu as pltpu
from jax.sharding import PartitionSpec as P

PAIR = 2
GROUP = 4
UNROLL = 8
SHIFT = 2


def each(count, body, start):
    if count > UNROLL:
        return lax.fori_loop(0, count, body, start)
    for i in range(count):
        start = body(i, start)
    return start


def message_at(w, z, wide_count, near_count, length):
    place = (w + wide_count - SHIFT) % wide_count
    start = (place * near_count + z) * length
    if not isinstance(w, int):
        start = pl.multiple_of(start, length)
    return start


def route_kernel(own_count, wide_count, *refs):
    sources, (order_ref, label_ref, near_ref), targets, sems = refs[:5], refs[5:8], refs[8:12], refs[12]
    in_tile, counts, out_tile, owner_map = targets
    copies = [
        pltpu.make_async_copy(source, target, sems.at[i])
        for i, (source, target) in enumerate(zip(sources, (*targets, near_ref)))
    ]
    for copy in copies:
        copy.start()
    for copy in copies[:4]:
        copy.wait()
    slot_count, rows, width = near_ref.shape
    column = lax.broadcasted_iota(jnp.int32, (1, slot_count * rows), 1)
    owners = lax.broadcasted_iota(jnp.int32, (wide_count, width), 0)

    def route(h, carry):
        owner_of, labels = carry
        spot = owner_map[out_tile[h]]
        owner = lax.div(spot, own_count)
        label = in_tile[h] * own_count + lax.rem(spot, own_count) + 1
        label = jnp.where(h < counts[0], label, 0)
        owner_of = jnp.where(lax.div(column, rows) == h, owner, owner_of)
        return owner_of, jnp.where(owners == owner, label, labels)

    start = (jnp.zeros_like(column), jnp.zeros((wide_count, width), jnp.int32))
    owner_of, labels = each(slot_count, route, start)
    label_ref[...] = labels.astype(jnp.float32).astype(label_ref.dtype)
    row = lax.broadcasted_iota(jnp.int32, (wide_count * rows, 1), 0)
    hit = row == owner_of * rows + lax.rem(column, rows)
    order_ref[...] = hit.astype(jnp.float32).astype(order_ref.dtype)
    copies[4].wait()


def pack_kernel(wide_count, near_count, order_ref, label_ref, near_ref, far_ref, send_ref, both, ordered):
    slot_count, rows, width = near_ref.shape
    length = send_ref.shape[0] // (wide_count * near_count)
    for side, ref in enumerate((near_ref, far_ref)):
        block = ref[...]
        if rows % 16 != 0:
            block = block.astype(jnp.float32)
        block = block.reshape(slot_count * rows, width).astype(both.dtype)
        both[:, side * width : (side + 1) * width] = block
    ordered[...] = jnp.dot(order_ref[...], both[...], preferred_element_type=jnp.float32)
    labels = label_ref[...].astype(jnp.float32)
    ids = lax.broadcasted_iota(jnp.int32, labels.shape, 0)

    def write(owner, _):
        spot = owner * rows
        if not isinstance(owner, int):
            spot = pl.multiple_of(spot, rows)
        near = ordered[pl.ds(spot, rows), :width]
        far = ordered[pl.ds(spot, rows), width:]
        label = jnp.sum(jnp.where(ids == owner, labels, 0.0), axis=0, keepdims=True)
        label = jnp.broadcast_to(label, (length - 2 * rows, width))
        if length % 16 == 0:
            pieces = [(0, jnp.concatenate([near, far, label], axis=0))]
        else:
            pieces = [(0, near), (rows, far), (2 * rows, label)]
        for z in range(near_count):
            start = message_at(owner, z, wide_count, near_count, length)
            for offset, piece in pieces:
                send_ref[pl.ds(start + offset, piece.shape[0])] = piece.astype(send_ref.dtype)
        return 0

    each(wide_count, write, 0)


def ladder_kernel(
    rows, near_count, own_count, recv_count, amp_ref, got_ref, out_ref, tiles, column, seen
):
    wide_count = seen.shape[0]
    width = got_ref.shape[1]
    length = got_ref.shape[0] // (wide_count * near_count)
    upper = lax.axis_index("narrow") >= near_count
    tiles[...] = jnp.zeros_like(tiles)
    for u in range(recv_count):
        column[u] = 0

    def message(w, z):
        start = message_at(w, z, wide_count, near_count, length)
        if length % 16 == 0:
            block = got_ref[pl.ds(start, length)].astype(jnp.float32)
            return block[:rows], block[rows : 2 * rows]
        return got_ref[pl.ds(start, rows)], got_ref[pl.ds(start + rows, rows)]

    def read_label(w):
        start = message_at(w, 0, wide_count, near_count, length)
        if length % 16 == 0:
            label = got_ref[pl.ds(start, length)].astype(jnp.float32)[2 * rows :]
        else:
            label = got_ref[pl.ds(start + 2 * rows, length - 2 * rows)].astype(jnp.float32)
        return jnp.max(label).astype(jnp.int32)

    def keep(w, label, found):
        live = jnp.minimum(label, 1)
        at = jnp.minimum(found, recv_count)
        place = jnp.maximum(label - 1, 0)
        column[at] = lax.div(place, own_count)
        spot = lax.rem(place, own_count)
        parts = [message(w, z) for z in range(near_count)]
        near = jnp.concatenate([part[0] for part in parts], axis=0).astype(tiles.dtype)
        far = jnp.concatenate([part[1] for part in parts], axis=0).astype(tiles.dtype)
        halves = [jnp.where(upper, far, near), jnp.where(upper, near, far)]
        tile = jnp.concatenate(halves, axis=0)
        at = pl.multiple_of(at * width, width)
        for q in range(own_count):
            kept = jnp.where((live > 0) & (spot == q), tile, jnp.zeros_like(tile))
            tiles[pl.ds(at, width), q * width : (q + 1) * width] = kept
        return found + live

    if wide_count <= UNROLL:
        labels = [read_label(w) for w in range(wide_count)]
        found = jnp.int32(0)
        for w in range(wide_count):
            found = keep(w, labels[w], found)
    else:

        def note(w, _):
            seen[w] = read_label(w)
            return 0

        lax.fori_loop(0, wide_count, note, 0)
        lax.fori_loop(0, wide_count, lambda w, found: keep(w, seen[w], found), jnp.int32(0))
    total = None
    for first in range(0, recv_count, GROUP):
        last = min(first + GROUP, recv_count)
        spots = [pl.multiple_of(column[u] * width, width) for u in range(first, last)]
        picked = jnp.concatenate([amp_ref[:, pl.ds(spot, width)] for spot in spots], axis=1)
        term = jnp.dot(
            picked, tiles[first * width : last * width], preferred_element_type=jnp.float32
        )
        total = term if total is None else total + term
    out_ref[...] = total


def shards(amplitudes, integrals, in_tile, counts, out_tile, owner_map):
    slot_count, rows, width = integrals.shape
    row_count = amplitudes.shape[0]
    wide_count = lax.axis_size("wide")
    depth_count = lax.axis_size("narrow")
    own_count = owner_map.shape[0] // wide_count
    recv_count = slot_count // 2
    near_count = depth_count // 2
    kind = integrals.dtype
    message_count = wide_count * near_count
    length = 2 * rows + PAIR
    if wide_count > UNROLL or length % PAIR != 0 or message_count * length % 16 != 0:
        length = -(-length // 16) * 16
    hbm = pl.BlockSpec(memory_space=pltpu.HBM)
    vmem = pl.BlockSpec(memory_space=pltpu.VMEM)
    limit = pltpu.CompilerParams(vmem_limit_bytes=32 * 2**20)
    across = [(z, (z + near_count) % depth_count) for z in range(depth_count)]
    far = lax.ppermute(integrals, "narrow", across)
    given = [in_tile, counts, out_tile, owner_map, integrals]
    given = [
        value if value.size == 1 else pltpu.with_memory_space_constraint(value, pltpu.HBM)
        for value in given
    ]
    ordered, sent = wide_count * rows, slot_count * rows
    order, labels, near = pl.pallas_call(
        functools.partial(route_kernel, own_count, wide_count),
        out_shape=[
            jax.ShapeDtypeStruct((ordered, sent), kind),
            jax.ShapeDtypeStruct((wide_count, width), kind),
            jax.ShapeDtypeStruct(integrals.shape, kind),
        ],
        in_specs=[hbm] * len(given),
        out_specs=[vmem] * 3,
        scratch_shapes=[pltpu.SMEM(value.shape, value.dtype) for value in given[:-1]]
        + [pltpu.SemaphoreType.DMA((len(given),))],
        compiler_params=limit,
        cost_estimate=pl.CostEstimate(flops=2**30, bytes_accessed=2**20, transcendentals=0),
        name="route",
    )(*given)
    send = pl.pallas_call(
        functools.partial(pack_kernel, wide_count, near_count),
        out_shape=jax.ShapeDtypeStruct((message_count * length, width), kind),
        in_specs=[vmem] * 4,
        out_specs=vmem,
        scratch_shapes=[
            pltpu.VMEM((sent, 2 * width), kind),
            pltpu.VMEM((ordered, 2 * width), jnp.float32),
        ],
        compiler_params=limit,
        name="pack",
    )(order, labels, near, far)
    groups = [
        [
            (place + SHIFT) % wide_count * depth_count + half * near_count + z
            for place in range(wide_count)
            for z in range(near_count)
        ]
        for half in range(2)
    ]
    got = lax.all_to_all(
        send.reshape(message_count, length // PAIR, PAIR, width),
        ("wide", "narrow"),
        split_axis=0,
        concat_axis=0,
        tiled=True,
        axis_index_groups=groups,
    ).reshape(message_count * length, width)
    return pl.pallas_call(
        functools.partial(ladder_kernel, rows, near_count, own_count, recv_count),
        out_shape=jax.ShapeDtypeStruct((row_count, own_count * width), jnp.float32),
        in_specs=[vmem] * 2,
        out_specs=vmem,
        scratch_shapes=[
            pltpu.VMEM(((recv_count + 1) * width, own_count * width), kind),
            pltpu.SMEM((recv_count + 1,), jnp.int32),
            pltpu.SMEM((wide_count,), jnp.int32),
        ],
        compiler_params=limit,
        name="ladder",
    )(amplitudes, got)


def solution(mesh):
    return jax.shard_map(
        shards,
        mesh=mesh,
        in_specs=(
            P("narrow", None),
            P("wide", "narrow", None),
            P("wide"),
            P("wide"),
            P("wide"),
            P(),
        ),
        out_specs=P("narrow", "wide"),
        check_vma=False,
    )
```

```python
import functools

import jax
import jax.numpy as jnp
from jax import lax
from jax.experimental import pallas as pl
from jax.experimental.pallas import tpu as pltpu
from jax.sharding import PartitionSpec as P

PAIR = 2
GROUP = 4
UNROLL = 8
CORES = 2


def each(count, body, start):
    if count > UNROLL:
        return lax.fori_loop(0, count, body, start)
    for i in range(count):
        start = body(i, start)
    return start


def message_at(w, z, wide_count, near_count, length):
    place = (wide_count // CORES - 1 - w // CORES) * CORES + w % CORES
    start = (place * near_count + z) * length
    if not isinstance(w, int):
        start = pl.multiple_of(start, length)
    return start


def route_kernel(own_count, wide_count, *refs):
    sources, (order_ref, label_ref, near_ref), targets, sems = refs[:5], refs[5:8], refs[8:12], refs[12]
    in_tile, counts, out_tile, owner_map = targets
    copies = [
        pltpu.make_async_copy(source, target, sems.at[i])
        for i, (source, target) in enumerate(zip(sources, (*targets, near_ref)))
    ]
    for copy in copies:
        copy.start()
    for copy in copies[:4]:
        copy.wait()
    slot_count, rows, width = near_ref.shape
    column = lax.broadcasted_iota(jnp.int32, (1, slot_count * rows), 1)
    owners = lax.broadcasted_iota(jnp.int32, (wide_count, width), 0)

    def route(h, carry):
        owner_of, labels = carry
        spot = owner_map[out_tile[h]]
        owner = lax.div(spot, own_count)
        label = in_tile[h] * own_count + lax.rem(spot, own_count) + 1
        label = jnp.where(h < counts[0], label, 0)
        owner_of = jnp.where(lax.div(column, rows) == h, owner, owner_of)
        return owner_of, jnp.where(owners == owner, label, labels)

    start = (jnp.zeros_like(column), jnp.zeros((wide_count, width), jnp.int32))
    owner_of, labels = each(slot_count, route, start)
    label_ref[...] = labels.astype(jnp.float32).astype(label_ref.dtype)
    row = lax.broadcasted_iota(jnp.int32, (wide_count * rows, 1), 0)
    hit = row == owner_of * rows + lax.rem(column, rows)
    order_ref[...] = hit.astype(jnp.float32).astype(order_ref.dtype)
    copies[4].wait()


def pack_kernel(wide_count, near_count, order_ref, label_ref, near_ref, far_ref, send_ref, both, ordered):
    slot_count, rows, width = near_ref.shape
    length = send_ref.shape[0] // (wide_count * near_count)
    for side, ref in enumerate((near_ref, far_ref)):
        block = ref[...]
        if rows % 16 != 0:
            block = block.astype(jnp.float32)
        block = block.reshape(slot_count * rows, width).astype(both.dtype)
        both[:, side * width : (side + 1) * width] = block
    ordered[...] = jnp.dot(order_ref[...], both[...], preferred_element_type=jnp.float32)
    labels = label_ref[...].astype(jnp.float32)
    ids = lax.broadcasted_iota(jnp.int32, labels.shape, 0)

    def write(owner, _):
        spot = owner * rows
        if not isinstance(owner, int):
            spot = pl.multiple_of(spot, rows)
        near = ordered[pl.ds(spot, rows), :width]
        far = ordered[pl.ds(spot, rows), width:]
        label = jnp.sum(jnp.where(ids == owner, labels, 0.0), axis=0, keepdims=True)
        label = jnp.broadcast_to(label, (length - 2 * rows, width))
        if length % 16 == 0:
            pieces = [(0, jnp.concatenate([near, far, label], axis=0))]
        else:
            pieces = [(0, near), (rows, far), (2 * rows, label)]
        for z in range(near_count):
            start = message_at(owner, z, wide_count, near_count, length)
            for offset, piece in pieces:
                send_ref[pl.ds(start + offset, piece.shape[0])] = piece.astype(send_ref.dtype)
        return 0

    each(wide_count, write, 0)


def ladder_kernel(
    rows, near_count, own_count, recv_count, amp_ref, got_ref, out_ref, tiles, column, seen
):
    wide_count = seen.shape[0]
    width = got_ref.shape[1]
    length = got_ref.shape[0] // (wide_count * near_count)
    upper = lax.axis_index("narrow") >= near_count
    tiles[...] = jnp.zeros_like(tiles)
    for u in range(recv_count):
        column[u] = 0

    def message(w, z):
        start = message_at(w, z, wide_count, near_count, length)
        if length % 16 == 0:
            block = got_ref[pl.ds(start, length)].astype(jnp.float32)
            return block[:rows], block[rows : 2 * rows]
        return got_ref[pl.ds(start, rows)], got_ref[pl.ds(start + rows, rows)]

    def read_label(w):
        start = message_at(w, 0, wide_count, near_count, length)
        if length % 16 == 0:
            label = got_ref[pl.ds(start, length)].astype(jnp.float32)[2 * rows :]
        else:
            label = got_ref[pl.ds(start + 2 * rows, length - 2 * rows)].astype(jnp.float32)
        return jnp.max(label).astype(jnp.int32)

    def keep(w, label, found):
        live = jnp.minimum(label, 1)
        at = jnp.minimum(found, recv_count)
        place = jnp.maximum(label - 1, 0)
        column[at] = lax.div(place, own_count)
        spot = lax.rem(place, own_count)
        parts = [message(w, z) for z in range(near_count)]
        near = jnp.concatenate([part[0] for part in parts], axis=0).astype(tiles.dtype)
        far = jnp.concatenate([part[1] for part in parts], axis=0).astype(tiles.dtype)
        halves = [jnp.where(upper, far, near), jnp.where(upper, near, far)]
        tile = jnp.concatenate(halves, axis=0)
        at = pl.multiple_of(at * width, width)
        for q in range(own_count):
            kept = jnp.where((live > 0) & (spot == q), tile, jnp.zeros_like(tile))
            tiles[pl.ds(at, width), q * width : (q + 1) * width] = kept
        return found + live

    if wide_count <= UNROLL:
        labels = [read_label(w) for w in range(wide_count)]
        found = jnp.int32(0)
        for w in range(wide_count):
            found = keep(w, labels[w], found)
    else:

        def note(w, _):
            seen[w] = read_label(w)
            return 0

        lax.fori_loop(0, wide_count, note, 0)
        lax.fori_loop(0, wide_count, lambda w, found: keep(w, seen[w], found), jnp.int32(0))
    total = None
    for first in range(0, recv_count, GROUP):
        last = min(first + GROUP, recv_count)
        spots = [pl.multiple_of(column[u] * width, width) for u in range(first, last)]
        picked = jnp.concatenate([amp_ref[:, pl.ds(spot, width)] for spot in spots], axis=1)
        term = jnp.dot(
            picked, tiles[first * width : last * width], preferred_element_type=jnp.float32
        )
        total = term if total is None else total + term
    out_ref[...] = total


def shards(amplitudes, integrals, in_tile, counts, out_tile, owner_map):
    slot_count, rows, width = integrals.shape
    row_count = amplitudes.shape[0]
    wide_count = lax.axis_size("wide")
    depth_count = lax.axis_size("narrow")
    own_count = owner_map.shape[0] // wide_count
    recv_count = slot_count // 2
    near_count = depth_count // 2
    kind = integrals.dtype
    message_count = wide_count * near_count
    length = 2 * rows + PAIR
    if wide_count > UNROLL or length % PAIR != 0 or message_count * length % 16 != 0:
        length = -(-length // 16) * 16
    hbm = pl.BlockSpec(memory_space=pltpu.HBM)
    vmem = pl.BlockSpec(memory_space=pltpu.VMEM)
    limit = pltpu.CompilerParams(vmem_limit_bytes=32 * 2**20)
    across = [(z, (z + near_count) % depth_count) for z in range(depth_count)]
    far = lax.ppermute(integrals, "narrow", across)
    given = [in_tile, counts, out_tile, owner_map, integrals]
    given = [
        value if value.size == 1 else pltpu.with_memory_space_constraint(value, pltpu.HBM)
        for value in given
    ]
    ordered, sent = wide_count * rows, slot_count * rows
    order, labels, near = pl.pallas_call(
        functools.partial(route_kernel, own_count, wide_count),
        out_shape=[
            jax.ShapeDtypeStruct((ordered, sent), kind),
            jax.ShapeDtypeStruct((wide_count, width), kind),
            jax.ShapeDtypeStruct(integrals.shape, kind),
        ],
        in_specs=[hbm] * len(given),
        out_specs=[vmem] * 3,
        scratch_shapes=[pltpu.SMEM(value.shape, value.dtype) for value in given[:-1]]
        + [pltpu.SemaphoreType.DMA((len(given),))],
        compiler_params=limit,
        cost_estimate=pl.CostEstimate(flops=2**30, bytes_accessed=2**20, transcendentals=0),
        name="route",
    )(*given)
    send = pl.pallas_call(
        functools.partial(pack_kernel, wide_count, near_count),
        out_shape=jax.ShapeDtypeStruct((message_count * length, width), kind),
        in_specs=[vmem] * 4,
        out_specs=vmem,
        scratch_shapes=[
            pltpu.VMEM((sent, 2 * width), kind),
            pltpu.VMEM((ordered, 2 * width), jnp.float32),
        ],
        compiler_params=limit,
        name="pack",
    )(order, labels, near, far)
    groups = [
        [
            (chip * CORES + core) * depth_count + half * near_count + z
            for chip in reversed(range(wide_count // CORES))
            for core in range(CORES)
            for z in range(near_count)
        ]
        for half in range(2)
    ]
    got = lax.all_to_all(
        send.reshape(message_count, length // PAIR, PAIR, width),
        ("wide", "narrow"),
        split_axis=0,
        concat_axis=0,
        tiled=True,
        axis_index_groups=groups,
    ).reshape(message_count * length, width)
    return pl.pallas_call(
        functools.partial(ladder_kernel, rows, near_count, own_count, recv_count),
        out_shape=jax.ShapeDtypeStruct((row_count, own_count * width), jnp.float32),
        in_specs=[vmem] * 2,
        out_specs=vmem,
        scratch_shapes=[
            pltpu.VMEM(((recv_count + 1) * width, own_count * width), kind),
            pltpu.SMEM((recv_count + 1,), jnp.int32),
            pltpu.SMEM((wide_count,), jnp.int32),
        ],
        compiler_params=limit,
        name="ladder",
    )(amplitudes, got)


def solution(mesh):
    return jax.shard_map(
        shards,
        mesh=mesh,
        in_specs=(
            P("narrow", None),
            P("wide", "narrow", None),
            P("wide"),
            P("wide"),
            P("wide"),
            P(),
        ),
        out_specs=P("narrow", "wide"),
        check_vma=False,
    )
```

```python
import functools

import jax
import jax.numpy as jnp
from jax import lax
from jax.experimental import pallas as pl
from jax.experimental.pallas import tpu as pltpu
from jax.sharding import PartitionSpec as P

PAIR = 2
GROUP = 4
UNROLL = 8
CORES = 2


def each(count, body, start):
    if count > UNROLL:
        return lax.fori_loop(0, count, body, start)
    for i in range(count):
        start = body(i, start)
    return start


def chip_order(wide_count):
    chip_count = wide_count // CORES
    if wide_count > UNROLL:
        return list(range(chip_count))
    bits = (chip_count - 1).bit_length()
    flipped = [int(format(chip, "b").zfill(bits)[::-1], 2) for chip in range(2**bits)]
    return [chip for chip in flipped[1:] if chip < chip_count] + [0]


def message_at(w, z, wide_count, near_count, length):
    if isinstance(w, int):
        place = chip_order(wide_count).index(w // CORES) * CORES + w % CORES
    else:
        place = w
    start = (place * near_count + z) * length
    if not isinstance(w, int):
        start = pl.multiple_of(start, length)
    return start


def route_kernel(own_count, wide_count, *refs):
    sources, (order_ref, label_ref, near_ref), targets, sems = refs[:5], refs[5:8], refs[8:12], refs[12]
    in_tile, counts, out_tile, owner_map = targets
    copies = [
        pltpu.make_async_copy(source, target, sems.at[i])
        for i, (source, target) in enumerate(zip(sources, (*targets, near_ref)))
    ]
    for copy in copies:
        copy.start()
    for copy in copies[:4]:
        copy.wait()
    slot_count, rows, width = near_ref.shape
    column = lax.broadcasted_iota(jnp.int32, (1, slot_count * rows), 1)
    owners = lax.broadcasted_iota(jnp.int32, (wide_count, width), 0)

    def route(h, carry):
        owner_of, labels = carry
        spot = owner_map[out_tile[h]]
        owner = lax.div(spot, own_count)
        label = in_tile[h] * own_count + lax.rem(spot, own_count) + 1
        label = jnp.where(h < counts[0], label, 0)
        owner_of = jnp.where(lax.div(column, rows) == h, owner, owner_of)
        return owner_of, jnp.where(owners == owner, label, labels)

    start = (jnp.zeros_like(column), jnp.zeros((wide_count, width), jnp.int32))
    owner_of, labels = each(slot_count, route, start)
    label_ref[...] = labels.astype(jnp.float32).astype(label_ref.dtype)
    row = lax.broadcasted_iota(jnp.int32, (wide_count * rows, 1), 0)
    hit = row == owner_of * rows + lax.rem(column, rows)
    order_ref[...] = hit.astype(jnp.float32).astype(order_ref.dtype)
    copies[4].wait()


def pack_kernel(wide_count, near_count, order_ref, label_ref, near_ref, far_ref, send_ref, both, ordered):
    slot_count, rows, width = near_ref.shape
    length = send_ref.shape[0] // (wide_count * near_count)
    for side, ref in enumerate((near_ref, far_ref)):
        block = ref[...]
        if rows % 16 != 0:
            block = block.astype(jnp.float32)
        block = block.reshape(slot_count * rows, width).astype(both.dtype)
        both[:, side * width : (side + 1) * width] = block
    ordered[...] = jnp.dot(order_ref[...], both[...], preferred_element_type=jnp.float32)
    labels = label_ref[...].astype(jnp.float32)
    ids = lax.broadcasted_iota(jnp.int32, labels.shape, 0)

    def write(owner, _):
        spot = owner * rows
        if not isinstance(owner, int):
            spot = pl.multiple_of(spot, rows)
        near = ordered[pl.ds(spot, rows), :width]
        far = ordered[pl.ds(spot, rows), width:]
        label = jnp.sum(jnp.where(ids == owner, labels, 0.0), axis=0, keepdims=True)
        label = jnp.broadcast_to(label, (length - 2 * rows, width))
        if length % 16 == 0:
            pieces = [(0, jnp.concatenate([near, far, label], axis=0))]
        else:
            pieces = [(0, near), (rows, far), (2 * rows, label)]
        for z in range(near_count):
            start = message_at(owner, z, wide_count, near_count, length)
            for offset, piece in pieces:
                send_ref[pl.ds(start + offset, piece.shape[0])] = piece.astype(send_ref.dtype)
        return 0

    each(wide_count, write, 0)


def ladder_kernel(
    rows, near_count, own_count, recv_count, amp_ref, got_ref, out_ref, tiles, column, seen
):
    wide_count = seen.shape[0]
    width = got_ref.shape[1]
    length = got_ref.shape[0] // (wide_count * near_count)
    upper = lax.axis_index("narrow") >= near_count

    def message(w, z):
        start = message_at(w, z, wide_count, near_count, length)
        if length % 16 == 0:
            block = got_ref[pl.ds(start, length)].astype(jnp.float32)
            return block[:rows], block[rows : 2 * rows]
        return got_ref[pl.ds(start, rows)], got_ref[pl.ds(start + rows, rows)]

    def read_label(w):
        start = message_at(w, 0, wide_count, near_count, length)
        if length % 16 == 0:
            label = got_ref[pl.ds(start, length)].astype(jnp.float32)[2 * rows :]
        else:
            label = got_ref[pl.ds(start + 2 * rows, length - 2 * rows)].astype(jnp.float32)
        return jnp.max(label).astype(jnp.int32)

    def whole_tile(w):
        parts = [message(w, z) for z in range(near_count)]
        near = jnp.concatenate([part[0] for part in parts], axis=0).astype(tiles.dtype)
        far = jnp.concatenate([part[1] for part in parts], axis=0).astype(tiles.dtype)
        halves = [jnp.where(upper, far, near), jnp.where(upper, near, far)]
        return jnp.concatenate(halves, axis=0)

    def keep(w, label, found):
        live = jnp.minimum(label, 1)
        at = jnp.minimum(found, recv_count)
        place = jnp.maximum(label - 1, 0)
        column[at] = lax.div(place, own_count)
        spot = lax.rem(place, own_count)
        tile = whole_tile(w)
        at = pl.multiple_of(at * width, width)
        for q in range(own_count):
            kept = jnp.where((live > 0) & (spot == q), tile, jnp.zeros_like(tile))
            tiles[pl.ds(at, width), q * width : (q + 1) * width] = kept
        return found + live

    if wide_count <= UNROLL:
        used = wide_count
        for w in range(wide_count):
            start = message_at(w, 0, wide_count, near_count, length) + 2 * rows
            label = got_ref[pl.ds(start, length - 2 * rows)].astype(jnp.float32)[:1]
            column[w] = lax.div(jnp.maximum(read_label(w) - 1, 0), own_count)
            code = label.astype(jnp.int32) - 1
            tile = whole_tile(w)
            for q in range(own_count):
                kept = (code >= 0) & (lax.rem(code, own_count) == q)
                factor = jnp.where(kept, 1.0, 0.0).astype(tiles.dtype)
                at = slice(w * width, (w + 1) * width)
                tiles[at, q * width : (q + 1) * width] = tile * factor
    else:
        used = recv_count
        tiles[...] = jnp.zeros_like(tiles)
        for u in range(recv_count):
            column[u] = 0

        def note(w, _):
            seen[w] = read_label(w)
            return 0

        lax.fori_loop(0, wide_count, note, 0)
        lax.fori_loop(0, wide_count, lambda w, found: keep(w, seen[w], found), jnp.int32(0))
    total = None
    for first in range(0, used, GROUP):
        last = min(first + GROUP, used)
        spots = [pl.multiple_of(column[u] * width, width) for u in range(first, last)]
        picked = jnp.concatenate([amp_ref[:, pl.ds(spot, width)] for spot in spots], axis=1)
        term = jnp.dot(
            picked, tiles[first * width : last * width], preferred_element_type=jnp.float32
        )
        total = term if total is None else total + term
    out_ref[...] = total


def shards(amplitudes, integrals, in_tile, counts, out_tile, owner_map):
    slot_count, rows, width = integrals.shape
    row_count = amplitudes.shape[0]
    wide_count = lax.axis_size("wide")
    depth_count = lax.axis_size("narrow")
    own_count = owner_map.shape[0] // wide_count
    recv_count = slot_count // 2
    near_count = depth_count // 2
    held = max(recv_count + 1, min(wide_count, UNROLL))
    kind = integrals.dtype
    message_count = wide_count * near_count
    length = 2 * rows + PAIR
    if wide_count > UNROLL or length % PAIR != 0 or message_count * length % 16 != 0:
        length = -(-length // 16) * 16
    hbm = pl.BlockSpec(memory_space=pltpu.HBM)
    vmem = pl.BlockSpec(memory_space=pltpu.VMEM)
    limit = pltpu.CompilerParams(vmem_limit_bytes=32 * 2**20)
    across = [(z, (z + near_count) % depth_count) for z in range(depth_count)]
    far = lax.ppermute(integrals, "narrow", across)
    given = [in_tile, counts, out_tile, owner_map, integrals]
    given = [
        value if value.size == 1 else pltpu.with_memory_space_constraint(value, pltpu.HBM)
        for value in given
    ]
    ordered, sent = wide_count * rows, slot_count * rows
    order, labels, near = pl.pallas_call(
        functools.partial(route_kernel, own_count, wide_count),
        out_shape=[
            jax.ShapeDtypeStruct((ordered, sent), kind),
            jax.ShapeDtypeStruct((wide_count, width), kind),
            jax.ShapeDtypeStruct(integrals.shape, kind),
        ],
        in_specs=[hbm] * len(given),
        out_specs=[vmem] * 3,
        scratch_shapes=[pltpu.SMEM(value.shape, value.dtype) for value in given[:-1]]
        + [pltpu.SemaphoreType.DMA((len(given),))],
        compiler_params=limit,
        cost_estimate=pl.CostEstimate(flops=2**30, bytes_accessed=2**20, transcendentals=0),
        name="route",
    )(*given)
    send = pl.pallas_call(
        functools.partial(pack_kernel, wide_count, near_count),
        out_shape=jax.ShapeDtypeStruct((message_count * length, width), kind),
        in_specs=[vmem] * 4,
        out_specs=vmem,
        scratch_shapes=[
            pltpu.VMEM((sent, 2 * width), kind),
            pltpu.VMEM((ordered, 2 * width), jnp.float32),
        ],
        compiler_params=limit,
        name="pack",
    )(order, labels, near, far)
    groups = [
        [
            (chip * CORES + core) * depth_count + half * near_count + z
            for chip in chip_order(wide_count)
            for core in range(CORES)
            for z in range(near_count)
        ]
        for half in range(2)
    ]
    got = lax.all_to_all(
        send.reshape(message_count, length // PAIR, PAIR, width),
        ("wide", "narrow"),
        split_axis=0,
        concat_axis=0,
        tiled=True,
        axis_index_groups=groups,
    ).reshape(message_count * length, width)
    return pl.pallas_call(
        functools.partial(ladder_kernel, rows, near_count, own_count, recv_count),
        out_shape=jax.ShapeDtypeStruct((row_count, own_count * width), jnp.float32),
        in_specs=[vmem] * 2,
        out_specs=vmem,
        scratch_shapes=[
            pltpu.VMEM((held * width, own_count * width), kind),
            pltpu.SMEM((held,), jnp.int32),
            pltpu.SMEM((wide_count,), jnp.int32),
        ],
        compiler_params=limit,
        name="ladder",
    )(amplitudes, got)


def solution(mesh):
    return jax.shard_map(
        shards,
        mesh=mesh,
        in_specs=(
            P("narrow", None),
            P("wide", "narrow", None),
            P("wide"),
            P("wide"),
            P("wide"),
            P(),
        ),
        out_specs=P("narrow", "wide"),
        check_vma=False,
    )
```

```python
import functools

import jax
import jax.numpy as jnp
from jax import lax
from jax.experimental import pallas as pl
from jax.experimental.pallas import tpu as pltpu
from jax.sharding import PartitionSpec as P

PAIR = 2
GROUP = 4
UNROLL = 8
CORES = 2


def each(count, body, start):
    if count > UNROLL:
        return lax.fori_loop(0, count, body, start)
    for i in range(count):
        start = body(i, start)
    return start


def chip_order(wide_count):
    chip_count = wide_count // CORES
    if wide_count > UNROLL:
        return list(range(chip_count))
    bits = (chip_count - 1).bit_length()
    flipped = [int(format(chip, "b").zfill(bits)[::-1], 2) for chip in range(2**bits)]
    return [chip for chip in flipped[1:] if chip < chip_count] + [0]


def group_places(wide_count, near_count):
    depths = list(reversed(range(near_count)))
    cores = range(CORES)
    return [(chip * CORES + core, z) for chip in chip_order(wide_count) for z in depths for core in cores]


def message_at(w, z, wide_count, near_count, length):
    if isinstance(w, int):
        return group_places(wide_count, near_count).index((w, z)) * length
    place = (w // CORES * near_count + near_count - 1 - z) * CORES + w % CORES
    return pl.multiple_of(place * length, length)


def route_kernel(own_count, wide_count, *refs):
    sources, (order_ref, label_ref, near_ref), targets, sems = refs[:5], refs[5:8], refs[8:12], refs[12]
    in_tile, counts, out_tile, owner_map = targets
    copies = [
        pltpu.make_async_copy(source, target, sems.at[i])
        for i, (source, target) in enumerate(zip(sources, (*targets, near_ref)))
    ]
    for copy in copies:
        copy.start()
    for copy in copies[:4]:
        copy.wait()
    slot_count, rows, width = near_ref.shape
    column = lax.broadcasted_iota(jnp.int32, (1, slot_count * rows), 1)
    owners = lax.broadcasted_iota(jnp.int32, (wide_count, width), 0)

    def route(h, carry):
        owner_of, labels = carry
        spot = owner_map[out_tile[h]]
        owner = lax.div(spot, own_count)
        label = in_tile[h] * own_count + lax.rem(spot, own_count) + 1
        label = jnp.where(h < counts[0], label, 0)
        owner_of = jnp.where(lax.div(column, rows) == h, owner, owner_of)
        return owner_of, jnp.where(owners == owner, label, labels)

    start = (jnp.zeros_like(column), jnp.zeros((wide_count, width), jnp.int32))
    owner_of, labels = each(slot_count, route, start)
    label_ref[...] = labels.astype(jnp.float32).astype(label_ref.dtype)
    row = lax.broadcasted_iota(jnp.int32, (wide_count * rows, 1), 0)
    hit = row == owner_of * rows + lax.rem(column, rows)
    order_ref[...] = hit.astype(jnp.float32).astype(order_ref.dtype)
    copies[4].wait()


def pack_kernel(wide_count, near_count, order_ref, label_ref, near_ref, far_ref, send_ref, both, ordered):
    slot_count, rows, width = near_ref.shape
    length = send_ref.shape[0] // (wide_count * near_count)
    for side, ref in enumerate((near_ref, far_ref)):
        block = ref[...]
        if rows % 16 != 0:
            block = block.astype(jnp.float32)
        block = block.reshape(slot_count * rows, width).astype(both.dtype)
        both[:, side * width : (side + 1) * width] = block
    ordered[...] = jnp.dot(order_ref[...], both[...], preferred_element_type=jnp.float32)
    labels = label_ref[...].astype(jnp.float32)
    ids = lax.broadcasted_iota(jnp.int32, labels.shape, 0)

    def write(owner, _):
        spot = owner * rows
        if not isinstance(owner, int):
            spot = pl.multiple_of(spot, rows)
        near = ordered[pl.ds(spot, rows), :width]
        far = ordered[pl.ds(spot, rows), width:]
        label = jnp.sum(jnp.where(ids == owner, labels, 0.0), axis=0, keepdims=True)
        label = jnp.broadcast_to(label, (length - 2 * rows, width))
        if length % 16 == 0:
            pieces = [(0, jnp.concatenate([near, far, label], axis=0))]
        else:
            pieces = [(0, near), (rows, far), (2 * rows, label)]
        for z in range(near_count):
            start = message_at(owner, z, wide_count, near_count, length)
            for offset, piece in pieces:
                send_ref[pl.ds(start + offset, piece.shape[0])] = piece.astype(send_ref.dtype)
        return 0

    each(wide_count, write, 0)


def ladder_kernel(
    rows, near_count, own_count, recv_count, amp_ref, got_ref, out_ref, tiles, column, seen
):
    wide_count = seen.shape[0]
    width = got_ref.shape[1]
    length = got_ref.shape[0] // (wide_count * near_count)
    upper = lax.axis_index("narrow") >= near_count
    tiles[...] = jnp.zeros_like(tiles)
    for u in range(recv_count):
        column[u] = 0

    def message(w, z):
        start = message_at(w, z, wide_count, near_count, length)
        if length % 16 == 0:
            block = got_ref[pl.ds(start, length)].astype(jnp.float32)
            return block[:rows], block[rows : 2 * rows]
        return got_ref[pl.ds(start, rows)], got_ref[pl.ds(start + rows, rows)]

    def read_label(w):
        start = message_at(w, 0, wide_count, near_count, length)
        if length % 16 == 0:
            label = got_ref[pl.ds(start, length)].astype(jnp.float32)[2 * rows :]
        else:
            label = got_ref[pl.ds(start + 2 * rows, length - 2 * rows)].astype(jnp.float32)
        return jnp.max(label).astype(jnp.int32)

    def keep(w, label, found):
        live = jnp.minimum(label, 1)
        at = jnp.minimum(found, recv_count)
        place = jnp.maximum(label - 1, 0)
        column[at] = lax.div(place, own_count)
        spot = lax.rem(place, own_count)
        parts = [message(w, z) for z in range(near_count)]
        near = jnp.concatenate([part[0] for part in parts], axis=0).astype(tiles.dtype)
        far = jnp.concatenate([part[1] for part in parts], axis=0).astype(tiles.dtype)
        halves = [jnp.where(upper, far, near), jnp.where(upper, near, far)]
        tile = jnp.concatenate(halves, axis=0)
        at = pl.multiple_of(at * width, width)
        for q in range(own_count):
            kept = jnp.where((live > 0) & (spot == q), tile, jnp.zeros_like(tile))
            tiles[pl.ds(at, width), q * width : (q + 1) * width] = kept
        return found + live

    if wide_count <= UNROLL:
        labels = [read_label(w) for w in range(wide_count)]
        found = jnp.int32(0)
        for w in range(wide_count):
            found = keep(w, labels[w], found)
    else:

        def note(w, _):
            seen[w] = read_label(w)
            return 0

        lax.fori_loop(0, wide_count, note, 0)
        lax.fori_loop(0, wide_count, lambda w, found: keep(w, seen[w], found), jnp.int32(0))
    total = None
    for first in range(0, recv_count, GROUP):
        last = min(first + GROUP, recv_count)
        spots = [pl.multiple_of(column[u] * width, width) for u in range(first, last)]
        picked = jnp.concatenate([amp_ref[:, pl.ds(spot, width)] for spot in spots], axis=1)
        term = jnp.dot(
            picked, tiles[first * width : last * width], preferred_element_type=jnp.float32
        )
        total = term if total is None else total + term
    out_ref[...] = total


def shards(amplitudes, integrals, in_tile, counts, out_tile, owner_map):
    slot_count, rows, width = integrals.shape
    row_count = amplitudes.shape[0]
    wide_count = lax.axis_size("wide")
    depth_count = lax.axis_size("narrow")
    own_count = owner_map.shape[0] // wide_count
    recv_count = slot_count // 2
    near_count = depth_count // 2
    kind = integrals.dtype
    message_count = wide_count * near_count
    length = 2 * rows + PAIR
    if wide_count > UNROLL or length % PAIR != 0 or message_count * length % 16 != 0:
        length = -(-length // 16) * 16
    hbm = pl.BlockSpec(memory_space=pltpu.HBM)
    vmem = pl.BlockSpec(memory_space=pltpu.VMEM)
    limit = pltpu.CompilerParams(vmem_limit_bytes=32 * 2**20)
    across = [(z, (z + near_count) % depth_count) for z in range(depth_count)]
    far = lax.ppermute(integrals, "narrow", across)
    given = [in_tile, counts, out_tile, owner_map, integrals]
    given = [
        value if value.size == 1 else pltpu.with_memory_space_constraint(value, pltpu.HBM)
        for value in given
    ]
    ordered, sent = wide_count * rows, slot_count * rows
    order, labels, near = pl.pallas_call(
        functools.partial(route_kernel, own_count, wide_count),
        out_shape=[
            jax.ShapeDtypeStruct((ordered, sent), kind),
            jax.ShapeDtypeStruct((wide_count, width), kind),
            jax.ShapeDtypeStruct(integrals.shape, kind),
        ],
        in_specs=[hbm] * len(given),
        out_specs=[vmem] * 3,
        scratch_shapes=[pltpu.SMEM(value.shape, value.dtype) for value in given[:-1]]
        + [pltpu.SemaphoreType.DMA((len(given),))],
        compiler_params=limit,
        cost_estimate=pl.CostEstimate(flops=2**30, bytes_accessed=2**20, transcendentals=0),
        name="route",
    )(*given)
    send = pl.pallas_call(
        functools.partial(pack_kernel, wide_count, near_count),
        out_shape=jax.ShapeDtypeStruct((message_count * length, width), kind),
        in_specs=[vmem] * 4,
        out_specs=vmem,
        scratch_shapes=[
            pltpu.VMEM((sent, 2 * width), kind),
            pltpu.VMEM((ordered, 2 * width), jnp.float32),
        ],
        compiler_params=limit,
        name="pack",
    )(order, labels, near, far)
    places = group_places(wide_count, near_count)
    groups = [
        [w * depth_count + half * near_count + z for w, z in places] for half in range(2)
    ]
    got = lax.all_to_all(
        send.reshape(message_count, length // PAIR, PAIR, width),
        ("wide", "narrow"),
        split_axis=0,
        concat_axis=0,
        tiled=True,
        axis_index_groups=groups,
    ).reshape(message_count * length, width)
    return pl.pallas_call(
        functools.partial(ladder_kernel, rows, near_count, own_count, recv_count),
        out_shape=jax.ShapeDtypeStruct((row_count, own_count * width), jnp.float32),
        in_specs=[vmem] * 2,
        out_specs=vmem,
        scratch_shapes=[
            pltpu.VMEM(((recv_count + 1) * width, own_count * width), kind),
            pltpu.SMEM((recv_count + 1,), jnp.int32),
            pltpu.SMEM((wide_count,), jnp.int32),
        ],
        compiler_params=limit,
        name="ladder",
    )(amplitudes, got)


def solution(mesh):
    return jax.shard_map(
        shards,
        mesh=mesh,
        in_specs=(
            P("narrow", None),
            P("wide", "narrow", None),
            P("wide"),
            P("wide"),
            P("wide"),
            P(),
        ),
        out_specs=P("narrow", "wide"),
        check_vma=False,
    )
```

```python
import functools

import jax
import jax.numpy as jnp
from jax import lax
from jax.experimental import pallas as pl
from jax.experimental.pallas import tpu as pltpu
from jax.sharding import PartitionSpec as P

PAIR = 2
GROUP = 4
UNROLL = 8
CORES = 2


def each(count, body, start):
    if count > UNROLL:
        return lax.fori_loop(0, count, body, start)
    for i in range(count):
        start = body(i, start)
    return start


def chip_order(wide_count):
    chip_count = wide_count // CORES
    if wide_count > UNROLL:
        return list(range(chip_count))
    bits = (chip_count - 1).bit_length()
    flipped = [int(format(chip, "b").zfill(bits)[::-1], 2) for chip in range(2**bits)]
    return [chip for chip in flipped[1:] if chip < chip_count] + [0]


def group_places(wide_count, near_count):
    depths = list(reversed(range(near_count)))
    cores = range(CORES)
    places = []
    for chip in chip_order(wide_count):
        if chip == 0 and wide_count <= UNROLL:
            places += [(core, z) for core in cores for z in range(near_count)]
        else:
            places += [(chip * CORES + core, z) for z in depths for core in cores]
    return places


def message_at(w, z, wide_count, near_count, length):
    if isinstance(w, int):
        return group_places(wide_count, near_count).index((w, z)) * length
    place = (w // CORES * near_count + near_count - 1 - z) * CORES + w % CORES
    return pl.multiple_of(place * length, length)


def route_kernel(own_count, wide_count, *refs):
    sources, (order_ref, label_ref, near_ref), targets, sems = refs[:5], refs[5:8], refs[8:12], refs[12]
    in_tile, counts, out_tile, owner_map = targets
    copies = [
        pltpu.make_async_copy(source, target, sems.at[i])
        for i, (source, target) in enumerate(zip(sources, (*targets, near_ref)))
    ]
    for copy in copies:
        copy.start()
    for copy in copies[:4]:
        copy.wait()
    slot_count, rows, width = near_ref.shape
    column = lax.broadcasted_iota(jnp.int32, (1, slot_count * rows), 1)
    owners = lax.broadcasted_iota(jnp.int32, (wide_count, width), 0)

    def route(h, carry):
        owner_of, labels = carry
        spot = owner_map[out_tile[h]]
        owner = lax.div(spot, own_count)
        label = in_tile[h] * own_count + lax.rem(spot, own_count) + 1
        label = jnp.where(h < counts[0], label, 0)
        owner_of = jnp.where(lax.div(column, rows) == h, owner, owner_of)
        return owner_of, jnp.where(owners == owner, label, labels)

    start = (jnp.zeros_like(column), jnp.zeros((wide_count, width), jnp.int32))
    owner_of, labels = each(slot_count, route, start)
    label_ref[...] = labels.astype(jnp.float32).astype(label_ref.dtype)
    row = lax.broadcasted_iota(jnp.int32, (wide_count * rows, 1), 0)
    hit = row == owner_of * rows + lax.rem(column, rows)
    order_ref[...] = hit.astype(jnp.float32).astype(order_ref.dtype)
    copies[4].wait()


def pack_kernel(wide_count, near_count, order_ref, label_ref, near_ref, far_ref, send_ref, both, ordered):
    slot_count, rows, width = near_ref.shape
    length = send_ref.shape[0] // (wide_count * near_count)
    for side, ref in enumerate((near_ref, far_ref)):
        block = ref[...]
        if rows % 16 != 0:
            block = block.astype(jnp.float32)
        block = block.reshape(slot_count * rows, width).astype(both.dtype)
        both[:, side * width : (side + 1) * width] = block
    ordered[...] = jnp.dot(order_ref[...], both[...], preferred_element_type=jnp.float32)
    labels = label_ref[...].astype(jnp.float32)
    ids = lax.broadcasted_iota(jnp.int32, labels.shape, 0)

    def write(owner, _):
        spot = owner * rows
        if not isinstance(owner, int):
            spot = pl.multiple_of(spot, rows)
        near = ordered[pl.ds(spot, rows), :width]
        far = ordered[pl.ds(spot, rows), width:]
        label = jnp.sum(jnp.where(ids == owner, labels, 0.0), axis=0, keepdims=True)
        label = jnp.broadcast_to(label, (length - 2 * rows, width))
        if length % 16 == 0:
            pieces = [(0, jnp.concatenate([near, far, label], axis=0))]
        else:
            pieces = [(0, near), (rows, far), (2 * rows, label)]
        for z in range(near_count):
            start = message_at(owner, z, wide_count, near_count, length)
            for offset, piece in pieces:
                send_ref[pl.ds(start + offset, piece.shape[0])] = piece.astype(send_ref.dtype)
        return 0

    each(wide_count, write, 0)


def fetch_kernel(source, target, sem):
    copy = pltpu.make_async_copy(source, target, sem)
    copy.start()
    copy.wait()


def ladder_kernel(
    rows, near_count, own_count, recv_count, amp_ref, got_ref, out_ref, tiles, column, seen
):
    wide_count = seen.shape[0]
    width = got_ref.shape[1]
    length = got_ref.shape[0] // (wide_count * near_count)
    upper = lax.axis_index("narrow") >= near_count
    tiles[...] = jnp.zeros_like(tiles)
    for u in range(recv_count):
        column[u] = 0

    def message(w, z):
        start = message_at(w, z, wide_count, near_count, length)
        if length % 16 == 0:
            block = got_ref[pl.ds(start, length)].astype(jnp.float32)
            return block[:rows], block[rows : 2 * rows]
        return got_ref[pl.ds(start, rows)], got_ref[pl.ds(start + rows, rows)]

    def read_label(w):
        start = message_at(w, 0, wide_count, near_count, length)
        if length % 16 == 0:
            label = got_ref[pl.ds(start, length)].astype(jnp.float32)[2 * rows :]
        else:
            label = got_ref[pl.ds(start + 2 * rows, length - 2 * rows)].astype(jnp.float32)
        return jnp.max(label).astype(jnp.int32)

    def keep(w, label, found):
        live = jnp.minimum(label, 1)
        at = jnp.minimum(found, recv_count)
        place = jnp.maximum(label - 1, 0)
        column[at] = lax.div(place, own_count)
        spot = lax.rem(place, own_count)
        parts = [message(w, z) for z in range(near_count)]
        near = jnp.concatenate([part[0] for part in parts], axis=0).astype(tiles.dtype)
        far = jnp.concatenate([part[1] for part in parts], axis=0).astype(tiles.dtype)
        halves = [jnp.where(upper, far, near), jnp.where(upper, near, far)]
        tile = jnp.concatenate(halves, axis=0)
        at = pl.multiple_of(at * width, width)
        for q in range(own_count):
            kept = jnp.where((live > 0) & (spot == q), tile, jnp.zeros_like(tile))
            tiles[pl.ds(at, width), q * width : (q + 1) * width] = kept
        return found + live

    if wide_count <= UNROLL:
        labels = [read_label(w) for w in range(wide_count)]
        found = jnp.int32(0)
        for w in range(wide_count):
            found = keep(w, labels[w], found)
    else:

        def note(w, _):
            seen[w] = read_label(w)
            return 0

        lax.fori_loop(0, wide_count, note, 0)
        lax.fori_loop(0, wide_count, lambda w, found: keep(w, seen[w], found), jnp.int32(0))
    total = None
    for first in range(0, recv_count, GROUP):
        last = min(first + GROUP, recv_count)
        spots = [pl.multiple_of(column[u] * width, width) for u in range(first, last)]
        picked = jnp.concatenate([amp_ref[:, pl.ds(spot, width)] for spot in spots], axis=1)
        term = jnp.dot(
            picked, tiles[first * width : last * width], preferred_element_type=jnp.float32
        )
        total = term if total is None else total + term
    out_ref[...] = total


def shards(amplitudes, integrals, in_tile, counts, out_tile, owner_map):
    slot_count, rows, width = integrals.shape
    row_count = amplitudes.shape[0]
    wide_count = lax.axis_size("wide")
    depth_count = lax.axis_size("narrow")
    own_count = owner_map.shape[0] // wide_count
    recv_count = slot_count // 2
    near_count = depth_count // 2
    kind = integrals.dtype
    message_count = wide_count * near_count
    length = 2 * rows + PAIR
    if wide_count > UNROLL or length % PAIR != 0 or message_count * length % 16 != 0:
        length = -(-length // 16) * 16
    hbm = pl.BlockSpec(memory_space=pltpu.HBM)
    vmem = pl.BlockSpec(memory_space=pltpu.VMEM)
    limit = pltpu.CompilerParams(vmem_limit_bytes=32 * 2**20)
    across = [(z, (z + near_count) % depth_count) for z in range(depth_count)]
    far = lax.ppermute(integrals, "narrow", across)
    given = [in_tile, counts, out_tile, owner_map, integrals]
    given = [
        value if value.size == 1 else pltpu.with_memory_space_constraint(value, pltpu.HBM)
        for value in given
    ]
    ordered, sent = wide_count * rows, slot_count * rows
    order, labels, near = pl.pallas_call(
        functools.partial(route_kernel, own_count, wide_count),
        out_shape=[
            jax.ShapeDtypeStruct((ordered, sent), kind),
            jax.ShapeDtypeStruct((wide_count, width), kind),
            jax.ShapeDtypeStruct(integrals.shape, kind),
        ],
        in_specs=[hbm] * len(given),
        out_specs=[vmem] * 3,
        scratch_shapes=[pltpu.SMEM(value.shape, value.dtype) for value in given[:-1]]
        + [pltpu.SemaphoreType.DMA((len(given),))],
        compiler_params=limit,
        name="route",
    )(*given)
    send = pl.pallas_call(
        functools.partial(pack_kernel, wide_count, near_count),
        out_shape=jax.ShapeDtypeStruct((message_count * length, width), kind),
        in_specs=[vmem] * 4,
        out_specs=vmem,
        scratch_shapes=[
            pltpu.VMEM((sent, 2 * width), kind),
            pltpu.VMEM((ordered, 2 * width), jnp.float32),
        ],
        compiler_params=limit,
        name="pack",
    )(order, labels, near, far)
    places = group_places(wide_count, near_count)
    groups = [
        [w * depth_count + half * near_count + z for w, z in places] for half in range(2)
    ]
    got = lax.all_to_all(
        send.reshape(message_count, length // PAIR, PAIR, width),
        ("wide", "narrow"),
        split_axis=0,
        concat_axis=0,
        tiled=True,
        axis_index_groups=groups,
    ).reshape(message_count * length, width)
    near = pl.pallas_call(
        fetch_kernel,
        out_shape=jax.ShapeDtypeStruct(amplitudes.shape, amplitudes.dtype),
        in_specs=[hbm],
        out_specs=vmem,
        scratch_shapes=[pltpu.SemaphoreType.DMA],
        compiler_params=limit,
        cost_estimate=pl.CostEstimate(flops=2**30, bytes_accessed=2**21, transcendentals=0),
        name="fetch",
    )(pltpu.with_memory_space_constraint(amplitudes, pltpu.HBM))
    return pl.pallas_call(
        functools.partial(ladder_kernel, rows, near_count, own_count, recv_count),
        out_shape=jax.ShapeDtypeStruct((row_count, own_count * width), jnp.float32),
        in_specs=[vmem] * 2,
        out_specs=vmem,
        scratch_shapes=[
            pltpu.VMEM(((recv_count + 1) * width, own_count * width), kind),
            pltpu.SMEM((recv_count + 1,), jnp.int32),
            pltpu.SMEM((wide_count,), jnp.int32),
        ],
        compiler_params=limit,
        name="ladder",
    )(near, got)


def solution(mesh):
    return jax.shard_map(
        shards,
        mesh=mesh,
        in_specs=(
            P("narrow", None),
            P("wide", "narrow", None),
            P("wide"),
            P("wide"),
            P("wide"),
            P(),
        ),
        out_specs=P("narrow", "wide"),
        check_vma=False,
    )
```

```python
import functools

import jax
import jax.numpy as jnp
from jax import lax
from jax.experimental import pallas as pl
from jax.experimental.pallas import tpu as pltpu
from jax.sharding import PartitionSpec as P

PAIR = 2
GROUP = 4
UNROLL = 8
CORES = 2


def each(count, body, start):
    if count > UNROLL:
        return lax.fori_loop(0, count, body, start)
    for i in range(count):
        start = body(i, start)
    return start


def chip_order(wide_count):
    chip_count = wide_count // CORES
    if wide_count > UNROLL:
        return list(range(chip_count))
    bits = (chip_count - 1).bit_length()
    flipped = [int(format(chip, "b").zfill(bits)[::-1], 2) for chip in range(2**bits)]
    return [chip for chip in flipped[1:] if chip < chip_count] + [0]


def group_places(wide_count, near_count):
    depths = list(reversed(range(near_count)))
    cores = range(CORES)
    places = []
    for chip in chip_order(wide_count):
        if chip == 0 and wide_count <= UNROLL:
            places += [(core, z) for core in cores for z in range(near_count)]
        else:
            places += [(chip * CORES + core, z) for z in depths for core in cores]
    return places


def message_at(w, z, wide_count, near_count, length):
    if isinstance(w, int):
        return group_places(wide_count, near_count).index((w, z)) * length
    place = (w // CORES * near_count + near_count - 1 - z) * CORES + w % CORES
    return pl.multiple_of(place * length, length)


def route_kernel(own_count, wide_count, *refs):
    sources, (order_ref, label_ref, near_ref), targets, sems = refs[:5], refs[5:8], refs[8:12], refs[12]
    in_tile, counts, out_tile, owner_map = targets
    copies = [
        pltpu.make_async_copy(source, target, sems.at[i])
        for i, (source, target) in enumerate(zip(sources, (*targets, near_ref)))
    ]
    for copy in copies:
        copy.start()
    for copy in copies[:4]:
        copy.wait()
    slot_count, rows, width = near_ref.shape
    column = lax.broadcasted_iota(jnp.int32, (1, slot_count * rows), 1)
    owners = lax.broadcasted_iota(jnp.int32, (wide_count, width), 0)

    def route(h, carry):
        owner_of, labels = carry
        spot = owner_map[out_tile[h]]
        owner = lax.div(spot, own_count)
        label = in_tile[h] * own_count + lax.rem(spot, own_count) + 1
        label = jnp.where(h < counts[0], label, 0)
        owner_of = jnp.where(lax.div(column, rows) == h, owner, owner_of)
        return owner_of, jnp.where(owners == owner, label, labels)

    start = (jnp.zeros_like(column), jnp.zeros((wide_count, width), jnp.int32))
    owner_of, labels = each(slot_count, route, start)
    label_ref[...] = labels.astype(jnp.float32).astype(label_ref.dtype)
    row = lax.broadcasted_iota(jnp.int32, (wide_count * rows, 1), 0)
    hit = row == owner_of * rows + lax.rem(column, rows)
    order_ref[...] = hit.astype(jnp.float32).astype(order_ref.dtype)
    copies[4].wait()


def pack_kernel(wide_count, near_count, order_ref, label_ref, near_ref, far_ref, send_ref, both, ordered):
    slot_count, rows, width = near_ref.shape
    length = send_ref.shape[0] // (wide_count * near_count)
    for side, ref in enumerate((near_ref, far_ref)):
        block = ref[...]
        if rows % 16 != 0:
            block = block.astype(jnp.float32)
        block = block.reshape(slot_count * rows, width).astype(both.dtype)
        both[:, side * width : (side + 1) * width] = block
    ordered[...] = jnp.dot(order_ref[...], both[...], preferred_element_type=jnp.float32)
    labels = label_ref[...].astype(jnp.float32)
    ids = lax.broadcasted_iota(jnp.int32, labels.shape, 0)

    def write(owner, _):
        spot = owner * rows
        if not isinstance(owner, int):
            spot = pl.multiple_of(spot, rows)
        near = ordered[pl.ds(spot, rows), :width]
        far = ordered[pl.ds(spot, rows), width:]
        label = jnp.sum(jnp.where(ids == owner, labels, 0.0), axis=0, keepdims=True)
        label = jnp.broadcast_to(label, (length - 2 * rows, width))
        if length % 16 == 0:
            pieces = [(0, jnp.concatenate([near, far, label], axis=0))]
        else:
            pieces = [(0, near), (rows, far), (2 * rows, label)]
        for z in range(near_count):
            start = message_at(owner, z, wide_count, near_count, length)
            for offset, piece in pieces:
                send_ref[pl.ds(start + offset, piece.shape[0])] = piece.astype(send_ref.dtype)
        return 0

    each(wide_count, write, 0)


def ladder_kernel(
    rows, near_count, own_count, recv_count, amp_ref, got_ref, out_ref, tiles, column, seen
):
    wide_count = seen.shape[0]
    width = got_ref.shape[1]
    length = got_ref.shape[0] // (wide_count * near_count)
    upper = lax.axis_index("narrow") >= near_count
    tiles[...] = jnp.zeros_like(tiles)
    for u in range(recv_count):
        column[u] = 0

    def message(w, z):
        start = message_at(w, z, wide_count, near_count, length)
        if length % 16 == 0:
            block = got_ref[pl.ds(start, length)].astype(jnp.float32)
            return block[:rows], block[rows : 2 * rows]
        return got_ref[pl.ds(start, rows)], got_ref[pl.ds(start + rows, rows)]

    def read_label(w):
        start = message_at(w, 0, wide_count, near_count, length)
        if length % 16 == 0:
            label = got_ref[pl.ds(start, length)].astype(jnp.float32)[2 * rows :]
        else:
            label = got_ref[pl.ds(start + 2 * rows, length - 2 * rows)].astype(jnp.float32)
        return jnp.max(label).astype(jnp.int32)

    def keep(w, label, found):
        live = jnp.minimum(label, 1)
        at = jnp.minimum(found, recv_count)
        place = jnp.maximum(label - 1, 0)
        column[at] = lax.div(place, own_count)
        spot = lax.rem(place, own_count)
        parts = [message(w, z) for z in range(near_count)]
        near = jnp.concatenate([part[0] for part in parts], axis=0).astype(tiles.dtype)
        far = jnp.concatenate([part[1] for part in parts], axis=0).astype(tiles.dtype)
        halves = [jnp.where(upper, far, near), jnp.where(upper, near, far)]
        tile = jnp.concatenate(halves, axis=0)
        at = pl.multiple_of(at * width, width)
        for q in range(own_count):
            kept = jnp.where((live > 0) & (spot == q), tile, jnp.zeros_like(tile))
            tiles[pl.ds(at, width), q * width : (q + 1) * width] = kept
        return found + live

    if wide_count <= UNROLL:
        labels = [read_label(w) for w in range(wide_count)]
        found = jnp.int32(0)
        for w in range(wide_count):
            found = keep(w, labels[w], found)
    else:

        def note(w, _):
            seen[w] = read_label(w)
            return 0

        lax.fori_loop(0, wide_count, note, 0)
        lax.fori_loop(0, wide_count, lambda w, found: keep(w, seen[w], found), jnp.int32(0))
    total = None
    for first in range(0, recv_count, GROUP):
        last = min(first + GROUP, recv_count)
        spots = [pl.multiple_of(column[u] * width, width) for u in range(first, last)]
        picked = jnp.concatenate([amp_ref[:, pl.ds(spot, width)] for spot in spots], axis=1)
        term = jnp.dot(
            picked, tiles[first * width : last * width], preferred_element_type=jnp.float32
        )
        total = term if total is None else total + term
    out_ref[...] = total


def shards(amplitudes, integrals, in_tile, counts, out_tile, owner_map):
    slot_count, rows, width = integrals.shape
    row_count = amplitudes.shape[0]
    wide_count = lax.axis_size("wide")
    depth_count = lax.axis_size("narrow")
    own_count = owner_map.shape[0] // wide_count
    recv_count = slot_count // 2
    near_count = depth_count // 2
    kind = integrals.dtype
    message_count = wide_count * near_count
    length = 2 * rows + PAIR
    if wide_count > UNROLL or length % PAIR != 0 or message_count * length % 16 != 0:
        length = -(-length // 16) * 16
    hbm = pl.BlockSpec(memory_space=pltpu.HBM)
    vmem = pl.BlockSpec(memory_space=pltpu.VMEM)
    limit = pltpu.CompilerParams(vmem_limit_bytes=32 * 2**20)
    across = [(z, (z + near_count) % depth_count) for z in range(depth_count)]
    far = lax.ppermute(integrals, "narrow", across)
    given = [in_tile, counts, out_tile, owner_map, integrals]
    given = [
        value if value.size == 1 else pltpu.with_memory_space_constraint(value, pltpu.HBM)
        for value in given
    ]
    ordered, sent = wide_count * rows, slot_count * rows
    order, labels, near = pl.pallas_call(
        functools.partial(route_kernel, own_count, wide_count),
        out_shape=[
            jax.ShapeDtypeStruct((ordered, sent), kind),
            jax.ShapeDtypeStruct((wide_count, width), kind),
            jax.ShapeDtypeStruct(integrals.shape, kind),
        ],
        in_specs=[hbm] * len(given),
        out_specs=[vmem] * 3,
        scratch_shapes=[pltpu.SMEM(value.shape, value.dtype) for value in given[:-1]]
        + [pltpu.SemaphoreType.DMA((len(given),))],
        compiler_params=limit,
        cost_estimate=pl.CostEstimate(flops=2**30, bytes_accessed=2**20, transcendentals=0),
        name="route",
    )(*given)
    send = pl.pallas_call(
        functools.partial(pack_kernel, wide_count, near_count),
        out_shape=jax.ShapeDtypeStruct((message_count * length, width), kind),
        in_specs=[vmem] * 4,
        out_specs=vmem,
        scratch_shapes=[
            pltpu.VMEM((sent, 2 * width), kind),
            pltpu.VMEM((ordered, 2 * width), jnp.float32),
        ],
        compiler_params=limit,
        name="pack",
    )(order, labels, near, far)
    places = group_places(wide_count, near_count)
    groups = [
        [w * depth_count + half * near_count + z for w, z in places] for half in range(2)
    ]
    got = lax.all_to_all(
        send.reshape(message_count, length // PAIR, PAIR, width),
        ("wide", "narrow"),
        split_axis=0,
        concat_axis=0,
        tiled=True,
        axis_index_groups=groups,
    ).reshape(message_count * length, width)
    return pl.pallas_call(
        functools.partial(ladder_kernel, rows, near_count, own_count, recv_count),
        out_shape=jax.ShapeDtypeStruct((row_count, own_count * width), jnp.float32),
        in_specs=[vmem] * 2,
        out_specs=vmem,
        scratch_shapes=[
            pltpu.VMEM(((recv_count + 1) * width, own_count * width), kind),
            pltpu.SMEM((recv_count + 1,), jnp.int32),
            pltpu.SMEM((wide_count,), jnp.int32),
        ],
        compiler_params=limit,
        name="ladder",
    )(amplitudes, got)


def solution(mesh):
    return jax.shard_map(
        shards,
        mesh=mesh,
        in_specs=(
            P("narrow", None),
            P("wide", "narrow", None),
            P("wide"),
            P("wide"),
            P("wide"),
            P(),
        ),
        out_specs=P("narrow", "wide"),
        check_vma=False,
    )
```

```python
import functools

import jax
import jax.numpy as jnp
from jax import lax
from jax.experimental import pallas as pl
from jax.experimental.pallas import tpu as pltpu
from jax.sharding import PartitionSpec as P

PAIR = 2
GROUP = 4
UNROLL = 8
CORES = 2


def each(count, body, start):
    if count > UNROLL:
        return lax.fori_loop(0, count, body, start)
    for i in range(count):
        start = body(i, start)
    return start


def chip_order(wide_count):
    chip_count = wide_count // CORES
    if wide_count > UNROLL:
        return list(range(chip_count))
    bits = (chip_count - 1).bit_length()
    flipped = [int(format(chip, "b").zfill(bits)[::-1], 2) for chip in range(2**bits)]
    return [chip for chip in flipped[1:] if chip < chip_count] + [0]


def group_places(wide_count, near_count):
    depths = list(reversed(range(near_count)))
    cores = range(CORES)
    places = []
    for chip in chip_order(wide_count):
        if chip == 0 and wide_count <= UNROLL:
            places += [(core, z) for core in reversed(cores) for z in depths]
        else:
            places += [(chip * CORES + core, z) for z in depths for core in cores]
    return places


def message_at(w, z, wide_count, near_count, length):
    if isinstance(w, int):
        return group_places(wide_count, near_count).index((w, z)) * length
    place = (w // CORES * near_count + near_count - 1 - z) * CORES + w % CORES
    return pl.multiple_of(place * length, length)


def route_kernel(own_count, wide_count, *refs):
    sources, (order_ref, label_ref, near_ref), targets, sems = refs[:5], refs[5:8], refs[8:12], refs[12]
    in_tile, counts, out_tile, owner_map = targets
    copies = [
        pltpu.make_async_copy(source, target, sems.at[i])
        for i, (source, target) in enumerate(zip(sources, (*targets, near_ref)))
    ]
    for copy in copies:
        copy.start()
    for copy in copies[:4]:
        copy.wait()
    slot_count, rows, width = near_ref.shape
    column = lax.broadcasted_iota(jnp.int32, (1, slot_count * rows), 1)
    owners = lax.broadcasted_iota(jnp.int32, (wide_count, width), 0)

    def route(h, carry):
        owner_of, labels = carry
        spot = owner_map[out_tile[h]]
        owner = lax.div(spot, own_count)
        label = in_tile[h] * own_count + lax.rem(spot, own_count) + 1
        label = jnp.where(h < counts[0], label, 0)
        owner_of = jnp.where(lax.div(column, rows) == h, owner, owner_of)
        return owner_of, jnp.where(owners == owner, label, labels)

    start = (jnp.zeros_like(column), jnp.zeros((wide_count, width), jnp.int32))
    owner_of, labels = each(slot_count, route, start)
    label_ref[...] = labels.astype(jnp.float32).astype(label_ref.dtype)
    row = lax.broadcasted_iota(jnp.int32, (wide_count * rows, 1), 0)
    hit = row == owner_of * rows + lax.rem(column, rows)
    order_ref[...] = hit.astype(jnp.float32).astype(order_ref.dtype)
    copies[4].wait()


def pack_kernel(wide_count, near_count, order_ref, label_ref, near_ref, far_ref, send_ref, both, ordered):
    slot_count, rows, width = near_ref.shape
    length = send_ref.shape[0] // (wide_count * near_count)
    for side, ref in enumerate((near_ref, far_ref)):
        block = ref[...]
        if rows % 16 != 0:
            block = block.astype(jnp.float32)
        block = block.reshape(slot_count * rows, width).astype(both.dtype)
        both[:, side * width : (side + 1) * width] = block
    ordered[...] = jnp.dot(order_ref[...], both[...], preferred_element_type=jnp.float32)
    labels = label_ref[...].astype(jnp.float32)
    ids = lax.broadcasted_iota(jnp.int32, labels.shape, 0)

    def write(owner, _):
        spot = owner * rows
        if not isinstance(owner, int):
            spot = pl.multiple_of(spot, rows)
        near = ordered[pl.ds(spot, rows), :width]
        far = ordered[pl.ds(spot, rows), width:]
        label = jnp.sum(jnp.where(ids == owner, labels, 0.0), axis=0, keepdims=True)
        label = jnp.broadcast_to(label, (length - 2 * rows, width))
        if length % 16 == 0:
            pieces = [(0, jnp.concatenate([near, far, label], axis=0))]
        else:
            pieces = [(0, near), (rows, far), (2 * rows, label)]
        for z in range(near_count):
            start = message_at(owner, z, wide_count, near_count, length)
            for offset, piece in pieces:
                send_ref[pl.ds(start + offset, piece.shape[0])] = piece.astype(send_ref.dtype)
        return 0

    each(wide_count, write, 0)


def ladder_kernel(
    rows, near_count, own_count, recv_count, amp_ref, got_ref, out_ref, tiles, column, seen
):
    wide_count = seen.shape[0]
    width = got_ref.shape[1]
    length = got_ref.shape[0] // (wide_count * near_count)
    upper = lax.axis_index("narrow") >= near_count
    tiles[...] = jnp.zeros_like(tiles)
    for u in range(recv_count):
        column[u] = 0

    def message(w, z):
        start = message_at(w, z, wide_count, near_count, length)
        if length % 16 == 0:
            block = got_ref[pl.ds(start, length)].astype(jnp.float32)
            return block[:rows], block[rows : 2 * rows]
        return got_ref[pl.ds(start, rows)], got_ref[pl.ds(start + rows, rows)]

    def read_label(w):
        start = message_at(w, 0, wide_count, near_count, length)
        if length % 16 == 0:
            label = got_ref[pl.ds(start, length)].astype(jnp.float32)[2 * rows :]
        else:
            label = got_ref[pl.ds(start + 2 * rows, length - 2 * rows)].astype(jnp.float32)
        return jnp.max(label).astype(jnp.int32)

    def keep(w, label, found):
        live = jnp.minimum(label, 1)
        at = jnp.minimum(found, recv_count)
        place = jnp.maximum(label - 1, 0)
        column[at] = lax.div(place, own_count)
        spot = lax.rem(place, own_count)
        parts = [message(w, z) for z in range(near_count)]
        near = jnp.concatenate([part[0] for part in parts], axis=0).astype(tiles.dtype)
        far = jnp.concatenate([part[1] for part in parts], axis=0).astype(tiles.dtype)
        halves = [jnp.where(upper, far, near), jnp.where(upper, near, far)]
        tile = jnp.concatenate(halves, axis=0)
        at = pl.multiple_of(at * width, width)
        for q in range(own_count):
            kept = jnp.where((live > 0) & (spot == q), tile, jnp.zeros_like(tile))
            tiles[pl.ds(at, width), q * width : (q + 1) * width] = kept
        return found + live

    if wide_count <= UNROLL:
        labels = [read_label(w) for w in range(wide_count)]
        found = jnp.int32(0)
        for w in range(wide_count):
            found = keep(w, labels[w], found)
    else:

        def note(w, _):
            seen[w] = read_label(w)
            return 0

        lax.fori_loop(0, wide_count, note, 0)
        lax.fori_loop(0, wide_count, lambda w, found: keep(w, seen[w], found), jnp.int32(0))
    total = None
    for first in range(0, recv_count, GROUP):
        last = min(first + GROUP, recv_count)
        spots = [pl.multiple_of(column[u] * width, width) for u in range(first, last)]
        picked = jnp.concatenate([amp_ref[:, pl.ds(spot, width)] for spot in spots], axis=1)
        term = jnp.dot(
            picked, tiles[first * width : last * width], preferred_element_type=jnp.float32
        )
        total = term if total is None else total + term
    out_ref[...] = total


def shards(amplitudes, integrals, in_tile, counts, out_tile, owner_map):
    slot_count, rows, width = integrals.shape
    row_count = amplitudes.shape[0]
    wide_count = lax.axis_size("wide")
    depth_count = lax.axis_size("narrow")
    own_count = owner_map.shape[0] // wide_count
    recv_count = slot_count // 2
    near_count = depth_count // 2
    kind = integrals.dtype
    message_count = wide_count * near_count
    length = 2 * rows + PAIR
    if wide_count > UNROLL or length % PAIR != 0 or message_count * length % 16 != 0:
        length = -(-length // 16) * 16
    hbm = pl.BlockSpec(memory_space=pltpu.HBM)
    vmem = pl.BlockSpec(memory_space=pltpu.VMEM)
    limit = pltpu.CompilerParams(vmem_limit_bytes=32 * 2**20)
    across = [(z, (z + near_count) % depth_count) for z in range(depth_count)]
    far = lax.ppermute(integrals, "narrow", across)
    given = [in_tile, counts, out_tile, owner_map, integrals]
    given = [
        value if value.size == 1 else pltpu.with_memory_space_constraint(value, pltpu.HBM)
        for value in given
    ]
    ordered, sent = wide_count * rows, slot_count * rows
    order, labels, near = pl.pallas_call(
        functools.partial(route_kernel, own_count, wide_count),
        out_shape=[
            jax.ShapeDtypeStruct((ordered, sent), kind),
            jax.ShapeDtypeStruct((wide_count, width), kind),
            jax.ShapeDtypeStruct(integrals.shape, kind),
        ],
        in_specs=[hbm] * len(given),
        out_specs=[vmem] * 3,
        scratch_shapes=[pltpu.SMEM(value.shape, value.dtype) for value in given[:-1]]
        + [pltpu.SemaphoreType.DMA((len(given),))],
        compiler_params=limit,
        cost_estimate=pl.CostEstimate(flops=2**30, bytes_accessed=2**20, transcendentals=0),
        name="route",
    )(*given)
    send = pl.pallas_call(
        functools.partial(pack_kernel, wide_count, near_count),
        out_shape=jax.ShapeDtypeStruct((message_count * length, width), kind),
        in_specs=[vmem] * 4,
        out_specs=vmem,
        scratch_shapes=[
            pltpu.VMEM((sent, 2 * width), kind),
            pltpu.VMEM((ordered, 2 * width), jnp.float32),
        ],
        compiler_params=limit,
        name="pack",
    )(order, labels, near, far)
    places = group_places(wide_count, near_count)
    groups = [
        [w * depth_count + half * near_count + z for w, z in places] for half in range(2)
    ]
    got = lax.all_to_all(
        send.reshape(message_count, length // PAIR, PAIR, width),
        ("wide", "narrow"),
        split_axis=0,
        concat_axis=0,
        tiled=True,
        axis_index_groups=groups,
    ).reshape(message_count * length, width)
    return pl.pallas_call(
        functools.partial(ladder_kernel, rows, near_count, own_count, recv_count),
        out_shape=jax.ShapeDtypeStruct((row_count, own_count * width), jnp.float32),
        in_specs=[vmem] * 2,
        out_specs=vmem,
        scratch_shapes=[
            pltpu.VMEM(((recv_count + 1) * width, own_count * width), kind),
            pltpu.SMEM((recv_count + 1,), jnp.int32),
            pltpu.SMEM((wide_count,), jnp.int32),
        ],
        compiler_params=limit,
        name="ladder",
    )(amplitudes, got)


def solution(mesh):
    return jax.shard_map(
        shards,
        mesh=mesh,
        in_specs=(
            P("narrow", None),
            P("wide", "narrow", None),
            P("wide"),
            P("wide"),
            P("wide"),
            P(),
        ),
        out_specs=P("narrow", "wide"),
        check_vma=False,
    )
```

```python
import functools

import jax
import jax.numpy as jnp
from jax import lax
from jax.experimental import pallas as pl
from jax.experimental.pallas import tpu as pltpu
from jax.sharding import PartitionSpec as P

PAIR = 2
GROUP = 4
UNROLL = 8
CORES = 2


def each(count, body, start):
    if count > UNROLL:
        return lax.fori_loop(0, count, body, start)
    for i in range(count):
        start = body(i, start)
    return start


def chip_order(wide_count):
    chip_count = wide_count // CORES
    if wide_count > UNROLL:
        return list(range(chip_count))
    bits = (chip_count - 1).bit_length()
    flipped = [int(format(chip, "b").zfill(bits)[::-1], 2) for chip in range(2**bits)]
    return [chip for chip in flipped[1:] if chip < chip_count] + [0]


def group_places(wide_count, near_count):
    depths = list(reversed(range(near_count)))
    cores = range(CORES)
    return [(chip * CORES + core, z) for chip in chip_order(wide_count) for core in cores for z in depths]


def message_at(w, z, wide_count, near_count, length):
    if isinstance(w, int):
        return group_places(wide_count, near_count).index((w, z)) * length
    place = w * near_count + near_count - 1 - z
    return pl.multiple_of(place * length, length)


def route_kernel(own_count, wide_count, *refs):
    sources, (order_ref, label_ref, near_ref), targets, sems = refs[:5], refs[5:8], refs[8:12], refs[12]
    in_tile, counts, out_tile, owner_map = targets
    copies = [
        pltpu.make_async_copy(source, target, sems.at[i])
        for i, (source, target) in enumerate(zip(sources, (*targets, near_ref)))
    ]
    for copy in copies:
        copy.start()
    for copy in copies[:4]:
        copy.wait()
    slot_count, rows, width = near_ref.shape
    column = lax.broadcasted_iota(jnp.int32, (1, slot_count * rows), 1)
    owners = lax.broadcasted_iota(jnp.int32, (wide_count, width), 0)

    def route(h, carry):
        owner_of, labels = carry
        spot = owner_map[out_tile[h]]
        owner = lax.div(spot, own_count)
        label = in_tile[h] * own_count + lax.rem(spot, own_count) + 1
        label = jnp.where(h < counts[0], label, 0)
        owner_of = jnp.where(lax.div(column, rows) == h, owner, owner_of)
        return owner_of, jnp.where(owners == owner, label, labels)

    start = (jnp.zeros_like(column), jnp.zeros((wide_count, width), jnp.int32))
    owner_of, labels = each(slot_count, route, start)
    label_ref[...] = labels.astype(jnp.float32).astype(label_ref.dtype)
    row = lax.broadcasted_iota(jnp.int32, (wide_count * rows, 1), 0)
    hit = row == owner_of * rows + lax.rem(column, rows)
    order_ref[...] = hit.astype(jnp.float32).astype(order_ref.dtype)
    copies[4].wait()


def pack_kernel(wide_count, near_count, order_ref, label_ref, near_ref, far_ref, send_ref, both, ordered):
    slot_count, rows, width = near_ref.shape
    length = send_ref.shape[0] // (wide_count * near_count)
    for side, ref in enumerate((near_ref, far_ref)):
        block = ref[...]
        if rows % 16 != 0:
            block = block.astype(jnp.float32)
        block = block.reshape(slot_count * rows, width).astype(both.dtype)
        both[:, side * width : (side + 1) * width] = block
    ordered[...] = jnp.dot(order_ref[...], both[...], preferred_element_type=jnp.float32)
    labels = label_ref[...].astype(jnp.float32)
    ids = lax.broadcasted_iota(jnp.int32, labels.shape, 0)

    def write(owner, _):
        spot = owner * rows
        if not isinstance(owner, int):
            spot = pl.multiple_of(spot, rows)
        near = ordered[pl.ds(spot, rows), :width]
        far = ordered[pl.ds(spot, rows), width:]
        label = jnp.sum(jnp.where(ids == owner, labels, 0.0), axis=0, keepdims=True)
        label = jnp.broadcast_to(label, (length - 2 * rows, width))
        if length % 16 == 0:
            pieces = [(0, jnp.concatenate([near, far, label], axis=0))]
        else:
            pieces = [(0, near), (rows, far), (2 * rows, label)]
        for z in range(near_count):
            start = message_at(owner, z, wide_count, near_count, length)
            for offset, piece in pieces:
                send_ref[pl.ds(start + offset, piece.shape[0])] = piece.astype(send_ref.dtype)
        return 0

    each(wide_count, write, 0)


def ladder_kernel(
    rows, near_count, own_count, recv_count, amp_ref, got_ref, out_ref, tiles, column, seen
):
    wide_count = seen.shape[0]
    width = got_ref.shape[1]
    length = got_ref.shape[0] // (wide_count * near_count)
    upper = lax.axis_index("narrow") >= near_count
    tiles[...] = jnp.zeros_like(tiles)
    for u in range(recv_count):
        column[u] = 0

    def message(w, z):
        start = message_at(w, z, wide_count, near_count, length)
        if length % 16 == 0:
            block = got_ref[pl.ds(start, length)].astype(jnp.float32)
            return block[:rows], block[rows : 2 * rows]
        return got_ref[pl.ds(start, rows)], got_ref[pl.ds(start + rows, rows)]

    def read_label(w):
        start = message_at(w, 0, wide_count, near_count, length)
        if length % 16 == 0:
            label = got_ref[pl.ds(start, length)].astype(jnp.float32)[2 * rows :]
        else:
            label = got_ref[pl.ds(start + 2 * rows, length - 2 * rows)].astype(jnp.float32)
        return jnp.max(label).astype(jnp.int32)

    def keep(w, label, found):
        live = jnp.minimum(label, 1)
        at = jnp.minimum(found, recv_count)
        place = jnp.maximum(label - 1, 0)
        column[at] = lax.div(place, own_count)
        spot = lax.rem(place, own_count)
        parts = [message(w, z) for z in range(near_count)]
        near = jnp.concatenate([part[0] for part in parts], axis=0).astype(tiles.dtype)
        far = jnp.concatenate([part[1] for part in parts], axis=0).astype(tiles.dtype)
        halves = [jnp.where(upper, far, near), jnp.where(upper, near, far)]
        tile = jnp.concatenate(halves, axis=0)
        at = pl.multiple_of(at * width, width)
        for q in range(own_count):
            kept = jnp.where((live > 0) & (spot == q), tile, jnp.zeros_like(tile))
            tiles[pl.ds(at, width), q * width : (q + 1) * width] = kept
        return found + live

    if wide_count <= UNROLL:
        labels = [read_label(w) for w in range(wide_count)]
        found = jnp.int32(0)
        for w in range(wide_count):
            found = keep(w, labels[w], found)
    else:

        def note(w, _):
            seen[w] = read_label(w)
            return 0

        lax.fori_loop(0, wide_count, note, 0)
        lax.fori_loop(0, wide_count, lambda w, found: keep(w, seen[w], found), jnp.int32(0))
    total = None
    for first in range(0, recv_count, GROUP):
        last = min(first + GROUP, recv_count)
        spots = [pl.multiple_of(column[u] * width, width) for u in range(first, last)]
        picked = jnp.concatenate([amp_ref[:, pl.ds(spot, width)] for spot in spots], axis=1)
        term = jnp.dot(
            picked, tiles[first * width : last * width], preferred_element_type=jnp.float32
        )
        total = term if total is None else total + term
    out_ref[...] = total


def shards(amplitudes, integrals, in_tile, counts, out_tile, owner_map):
    slot_count, rows, width = integrals.shape
    row_count = amplitudes.shape[0]
    wide_count = lax.axis_size("wide")
    depth_count = lax.axis_size("narrow")
    own_count = owner_map.shape[0] // wide_count
    recv_count = slot_count // 2
    near_count = depth_count // 2
    kind = integrals.dtype
    message_count = wide_count * near_count
    length = 2 * rows + PAIR
    if wide_count > UNROLL or length % PAIR != 0 or message_count * length % 16 != 0:
        length = -(-length // 16) * 16
    hbm = pl.BlockSpec(memory_space=pltpu.HBM)
    vmem = pl.BlockSpec(memory_space=pltpu.VMEM)
    limit = pltpu.CompilerParams(vmem_limit_bytes=32 * 2**20)
    across = [(z, (z + near_count) % depth_count) for z in range(depth_count)]
    far = lax.ppermute(integrals, "narrow", across)
    given = [in_tile, counts, out_tile, owner_map, integrals]
    given = [
        value if value.size == 1 else pltpu.with_memory_space_constraint(value, pltpu.HBM)
        for value in given
    ]
    ordered, sent = wide_count * rows, slot_count * rows
    order, labels, near = pl.pallas_call(
        functools.partial(route_kernel, own_count, wide_count),
        out_shape=[
            jax.ShapeDtypeStruct((ordered, sent), kind),
            jax.ShapeDtypeStruct((wide_count, width), kind),
            jax.ShapeDtypeStruct(integrals.shape, kind),
        ],
        in_specs=[hbm] * len(given),
        out_specs=[vmem] * 3,
        scratch_shapes=[pltpu.SMEM(value.shape, value.dtype) for value in given[:-1]]
        + [pltpu.SemaphoreType.DMA((len(given),))],
        compiler_params=limit,
        cost_estimate=pl.CostEstimate(flops=2**30, bytes_accessed=2**20, transcendentals=0),
        name="route",
    )(*given)
    send = pl.pallas_call(
        functools.partial(pack_kernel, wide_count, near_count),
        out_shape=jax.ShapeDtypeStruct((message_count * length, width), kind),
        in_specs=[vmem] * 4,
        out_specs=vmem,
        scratch_shapes=[
            pltpu.VMEM((sent, 2 * width), kind),
            pltpu.VMEM((ordered, 2 * width), jnp.float32),
        ],
        compiler_params=limit,
        name="pack",
    )(order, labels, near, far)
    places = group_places(wide_count, near_count)
    groups = [
        [w * depth_count + half * near_count + z for w, z in places] for half in range(2)
    ]
    got = lax.all_to_all(
        send.reshape(message_count, length // PAIR, PAIR, width),
        ("wide", "narrow"),
        split_axis=0,
        concat_axis=0,
        tiled=True,
        axis_index_groups=groups,
    ).reshape(message_count * length, width)
    return pl.pallas_call(
        functools.partial(ladder_kernel, rows, near_count, own_count, recv_count),
        out_shape=jax.ShapeDtypeStruct((row_count, own_count * width), jnp.float32),
        in_specs=[vmem] * 2,
        out_specs=vmem,
        scratch_shapes=[
            pltpu.VMEM(((recv_count + 1) * width, own_count * width), kind),
            pltpu.SMEM((recv_count + 1,), jnp.int32),
            pltpu.SMEM((wide_count,), jnp.int32),
        ],
        compiler_params=limit,
        name="ladder",
    )(amplitudes, got)


def solution(mesh):
    return jax.shard_map(
        shards,
        mesh=mesh,
        in_specs=(
            P("narrow", None),
            P("wide", "narrow", None),
            P("wide"),
            P("wide"),
            P("wide"),
            P(),
        ),
        out_specs=P("narrow", "wide"),
        check_vma=False,
    )
```

```python
import functools

import jax
import jax.numpy as jnp
from jax import lax
from jax.experimental import pallas as pl
from jax.experimental.pallas import tpu as pltpu
from jax.sharding import PartitionSpec as P

PAIR = 2
GROUP = 4
UNROLL = 8
CORES = 2


def each(count, body, start):
    if count > UNROLL:
        return lax.fori_loop(0, count, body, start)
    for i in range(count):
        start = body(i, start)
    return start


def chip_order(wide_count):
    chip_count = wide_count // CORES
    if wide_count > UNROLL:
        return list(range(chip_count))
    bits = (chip_count - 1).bit_length()
    flipped = [int(format(chip, "b").zfill(bits)[::-1], 2) for chip in range(2**bits)]
    return [chip for chip in flipped[1:] if chip < chip_count] + [0]


def group_places(wide_count, near_count):
    cores = range(CORES)
    depths = range(near_count)
    return [(chip * CORES + core, z) for chip in chip_order(wide_count) for core in cores for z in depths]


def message_at(w, z, wide_count, near_count, length):
    if isinstance(w, int):
        return group_places(wide_count, near_count).index((w, z)) * length
    place = w * near_count + z
    return pl.multiple_of(place * length, length)


def route_kernel(own_count, wide_count, *refs):
    sources, (order_ref, label_ref, near_ref), targets, sems = refs[:5], refs[5:8], refs[8:12], refs[12]
    in_tile, counts, out_tile, owner_map = targets
    copies = [
        pltpu.make_async_copy(source, target, sems.at[i])
        for i, (source, target) in enumerate(zip(sources, (*targets, near_ref)))
    ]
    for copy in copies:
        copy.start()
    for copy in copies[:4]:
        copy.wait()
    slot_count, rows, width = near_ref.shape
    column = lax.broadcasted_iota(jnp.int32, (1, slot_count * rows), 1)
    owners = lax.broadcasted_iota(jnp.int32, (wide_count, width), 0)

    def route(h, carry):
        owner_of, labels = carry
        spot = owner_map[out_tile[h]]
        owner = lax.div(spot, own_count)
        label = in_tile[h] * own_count + lax.rem(spot, own_count) + 1
        label = jnp.where(h < counts[0], label, 0)
        owner_of = jnp.where(lax.div(column, rows) == h, owner, owner_of)
        return owner_of, jnp.where(owners == owner, label, labels)

    start = (jnp.zeros_like(column), jnp.zeros((wide_count, width), jnp.int32))
    owner_of, labels = each(slot_count, route, start)
    label_ref[...] = labels.astype(jnp.float32).astype(label_ref.dtype)
    row = lax.broadcasted_iota(jnp.int32, (wide_count * rows, 1), 0)
    hit = row == owner_of * rows + lax.rem(column, rows)
    order_ref[...] = hit.astype(jnp.float32).astype(order_ref.dtype)
    copies[4].wait()


def pack_kernel(wide_count, near_count, order_ref, label_ref, near_ref, far_ref, send_ref, both, ordered):
    slot_count, rows, width = near_ref.shape
    length = send_ref.shape[0] // (wide_count * near_count)
    for side, ref in enumerate((near_ref, far_ref)):
        block = ref[...]
        if rows % 16 != 0:
            block = block.astype(jnp.float32)
        block = block.reshape(slot_count * rows, width).astype(both.dtype)
        both[:, side * width : (side + 1) * width] = block
    ordered[...] = jnp.dot(order_ref[...], both[...], preferred_element_type=jnp.float32)
    labels = label_ref[...].astype(jnp.float32)
    ids = lax.broadcasted_iota(jnp.int32, labels.shape, 0)

    def write(owner, _):
        spot = owner * rows
        if not isinstance(owner, int):
            spot = pl.multiple_of(spot, rows)
        near = ordered[pl.ds(spot, rows), :width]
        far = ordered[pl.ds(spot, rows), width:]
        label = jnp.sum(jnp.where(ids == owner, labels, 0.0), axis=0, keepdims=True)
        label = jnp.broadcast_to(label, (length - 2 * rows, width))
        if length % 16 == 0:
            pieces = [(0, jnp.concatenate([near, far, label], axis=0))]
        else:
            pieces = [(0, near), (rows, far), (2 * rows, label)]
        for z in range(near_count):
            start = message_at(owner, z, wide_count, near_count, length)
            for offset, piece in pieces:
                send_ref[pl.ds(start + offset, piece.shape[0])] = piece.astype(send_ref.dtype)
        return 0

    each(wide_count, write, 0)


def ladder_kernel(
    rows, near_count, own_count, recv_count, amp_ref, got_ref, out_ref, tiles, column, seen
):
    wide_count = seen.shape[0]
    width = got_ref.shape[1]
    length = got_ref.shape[0] // (wide_count * near_count)
    upper = lax.axis_index("narrow") >= near_count
    tiles[...] = jnp.zeros_like(tiles)
    for u in range(recv_count):
        column[u] = 0

    def message(w, z):
        start = message_at(w, z, wide_count, near_count, length)
        if length % 16 == 0:
            block = got_ref[pl.ds(start, length)].astype(jnp.float32)
            return block[:rows], block[rows : 2 * rows]
        return got_ref[pl.ds(start, rows)], got_ref[pl.ds(start + rows, rows)]

    def read_label(w):
        start = message_at(w, 0, wide_count, near_count, length)
        if length % 16 == 0:
            label = got_ref[pl.ds(start, length)].astype(jnp.float32)[2 * rows :]
        else:
            label = got_ref[pl.ds(start + 2 * rows, length - 2 * rows)].astype(jnp.float32)
        return jnp.max(label).astype(jnp.int32)

    def keep(w, label, found):
        live = jnp.minimum(label, 1)
        at = jnp.minimum(found, recv_count)
        place = jnp.maximum(label - 1, 0)
        column[at] = lax.div(place, own_count)
        spot = lax.rem(place, own_count)
        parts = [message(w, z) for z in range(near_count)]
        near = jnp.concatenate([part[0] for part in parts], axis=0).astype(tiles.dtype)
        far = jnp.concatenate([part[1] for part in parts], axis=0).astype(tiles.dtype)
        halves = [jnp.where(upper, far, near), jnp.where(upper, near, far)]
        tile = jnp.concatenate(halves, axis=0)
        at = pl.multiple_of(at * width, width)
        for q in range(own_count):
            kept = jnp.where((live > 0) & (spot == q), tile, jnp.zeros_like(tile))
            tiles[pl.ds(at, width), q * width : (q + 1) * width] = kept
        return found + live

    if wide_count <= UNROLL:
        labels = [read_label(w) for w in range(wide_count)]
        found = jnp.int32(0)
        for w in range(wide_count):
            found = keep(w, labels[w], found)
    else:

        def note(w, _):
            seen[w] = read_label(w)
            return 0

        lax.fori_loop(0, wide_count, note, 0)
        lax.fori_loop(0, wide_count, lambda w, found: keep(w, seen[w], found), jnp.int32(0))
    total = None
    for first in range(0, recv_count, GROUP):
        last = min(first + GROUP, recv_count)
        spots = [pl.multiple_of(column[u] * width, width) for u in range(first, last)]
        picked = jnp.concatenate([amp_ref[:, pl.ds(spot, width)] for spot in spots], axis=1)
        term = jnp.dot(
            picked, tiles[first * width : last * width], preferred_element_type=jnp.float32
        )
        total = term if total is None else total + term
    out_ref[...] = total


def shards(amplitudes, integrals, in_tile, counts, out_tile, owner_map):
    slot_count, rows, width = integrals.shape
    row_count = amplitudes.shape[0]
    wide_count = lax.axis_size("wide")
    depth_count = lax.axis_size("narrow")
    own_count = owner_map.shape[0] // wide_count
    recv_count = slot_count // 2
    near_count = depth_count // 2
    kind = integrals.dtype
    message_count = wide_count * near_count
    length = 2 * rows + PAIR
    if wide_count > UNROLL or length % PAIR != 0 or message_count * length % 16 != 0:
        length = -(-length // 16) * 16
    hbm = pl.BlockSpec(memory_space=pltpu.HBM)
    vmem = pl.BlockSpec(memory_space=pltpu.VMEM)
    limit = pltpu.CompilerParams(vmem_limit_bytes=32 * 2**20)
    across = [(z, (z + near_count) % depth_count) for z in range(depth_count)]
    far = lax.ppermute(integrals, "narrow", across)
    given = [in_tile, counts, out_tile, owner_map, integrals]
    given = [
        value if value.size == 1 else pltpu.with_memory_space_constraint(value, pltpu.HBM)
        for value in given
    ]
    ordered, sent = wide_count * rows, slot_count * rows
    order, labels, near = pl.pallas_call(
        functools.partial(route_kernel, own_count, wide_count),
        out_shape=[
            jax.ShapeDtypeStruct((ordered, sent), kind),
            jax.ShapeDtypeStruct((wide_count, width), kind),
            jax.ShapeDtypeStruct(integrals.shape, kind),
        ],
        in_specs=[hbm] * len(given),
        out_specs=[vmem] * 3,
        scratch_shapes=[pltpu.SMEM(value.shape, value.dtype) for value in given[:-1]]
        + [pltpu.SemaphoreType.DMA((len(given),))],
        compiler_params=limit,
        cost_estimate=pl.CostEstimate(flops=2**30, bytes_accessed=2**20, transcendentals=0),
        name="route",
    )(*given)
    send = pl.pallas_call(
        functools.partial(pack_kernel, wide_count, near_count),
        out_shape=jax.ShapeDtypeStruct((message_count * length, width), kind),
        in_specs=[vmem] * 4,
        out_specs=vmem,
        scratch_shapes=[
            pltpu.VMEM((sent, 2 * width), kind),
            pltpu.VMEM((ordered, 2 * width), jnp.float32),
        ],
        compiler_params=limit,
        name="pack",
    )(order, labels, near, far)
    places = group_places(wide_count, near_count)
    groups = [
        [w * depth_count + half * near_count + z for w, z in places] for half in range(2)
    ]
    got = lax.all_to_all(
        send.reshape(message_count, length // PAIR, PAIR, width),
        ("wide", "narrow"),
        split_axis=0,
        concat_axis=0,
        tiled=True,
        axis_index_groups=groups,
    ).reshape(message_count * length, width)
    return pl.pallas_call(
        functools.partial(ladder_kernel, rows, near_count, own_count, recv_count),
        out_shape=jax.ShapeDtypeStruct((row_count, own_count * width), jnp.float32),
        in_specs=[vmem] * 2,
        out_specs=vmem,
        scratch_shapes=[
            pltpu.VMEM(((recv_count + 1) * width, own_count * width), kind),
            pltpu.SMEM((recv_count + 1,), jnp.int32),
            pltpu.SMEM((wide_count,), jnp.int32),
        ],
        compiler_params=limit,
        name="ladder",
    )(amplitudes, got)


def solution(mesh):
    return jax.shard_map(
        shards,
        mesh=mesh,
        in_specs=(
            P("narrow", None),
            P("wide", "narrow", None),
            P("wide"),
            P("wide"),
            P("wide"),
            P(),
        ),
        out_specs=P("narrow", "wide"),
        check_vma=False,
    )
```

```python
import functools

import jax
import jax.numpy as jnp
from jax import lax
from jax.experimental import pallas as pl
from jax.experimental.pallas import tpu as pltpu
from jax.sharding import PartitionSpec as P

PAIR = 2
GROUP = 4
UNROLL = 8
CORES = 2


def each(count, body, start):
    if count > UNROLL:
        return lax.fori_loop(0, count, body, start)
    for i in range(count):
        start = body(i, start)
    return start


def chip_order(wide_count):
    chip_count = wide_count // CORES
    if wide_count > UNROLL:
        return list(range(chip_count))
    bits = (chip_count - 1).bit_length()
    flipped = [int(format(chip, "b").zfill(bits)[::-1], 2) for chip in range(2**bits)]
    return [chip for chip in flipped[1:] if chip < chip_count] + [0]


def group_places(wide_count, near_count):
    cores = range(CORES)
    depths = range(near_count)
    return [(chip * CORES + core, z) for chip in chip_order(wide_count) for core in cores for z in depths]


def message_at(w, z, wide_count, near_count, length):
    if isinstance(w, int):
        return group_places(wide_count, near_count).index((w, z)) * length
    place = w * near_count + z
    return pl.multiple_of(place * length, length)


def route_kernel(own_count, wide_count, *refs):
    sources, (order_ref, label_ref, near_ref), targets, sems = refs[:5], refs[5:8], refs[8:12], refs[12]
    in_tile, counts, out_tile, owner_map = targets
    copies = [
        pltpu.make_async_copy(source, target, sems.at[i])
        for i, (source, target) in enumerate(zip(sources, (*targets, near_ref)))
    ]
    for copy in copies:
        copy.start()
    for copy in copies[:4]:
        copy.wait()
    slot_count, rows, width = near_ref.shape
    column = lax.broadcasted_iota(jnp.int32, (1, slot_count * rows), 1)
    owners = lax.broadcasted_iota(jnp.int32, (wide_count, width), 0)

    def route(h, carry):
        owner_of, labels = carry
        spot = owner_map[out_tile[h]]
        owner = lax.div(spot, own_count)
        label = in_tile[h] * own_count + lax.rem(spot, own_count) + 1
        label = jnp.where(h < counts[0], label, 0)
        owner_of = jnp.where(lax.div(column, rows) == h, owner, owner_of)
        return owner_of, jnp.where(owners == owner, label, labels)

    start = (jnp.zeros_like(column), jnp.zeros((wide_count, width), jnp.int32))
    owner_of, labels = each(slot_count, route, start)
    label_ref[...] = labels.astype(jnp.float32).astype(label_ref.dtype)
    row = lax.broadcasted_iota(jnp.int32, (wide_count * rows, 1), 0)
    hit = row == owner_of * rows + lax.rem(column, rows)
    order_ref[...] = hit.astype(jnp.float32).astype(order_ref.dtype)
    copies[4].wait()


def pack_kernel(wide_count, near_count, order_ref, label_ref, near_ref, far_ref, send_ref, both, ordered):
    slot_count, rows, width = near_ref.shape
    length = send_ref.shape[0] // (wide_count * near_count)
    for side, ref in enumerate((near_ref, far_ref)):
        block = ref[...]
        if rows % 16 != 0:
            block = block.astype(jnp.float32)
        block = block.reshape(slot_count * rows, width).astype(both.dtype)
        both[:, side * width : (side + 1) * width] = block
    ordered[...] = jnp.dot(order_ref[...], both[...], preferred_element_type=jnp.float32)
    labels = label_ref[...].astype(jnp.float32)
    ids = lax.broadcasted_iota(jnp.int32, labels.shape, 0)

    def write(owner, _):
        spot = owner * rows
        if not isinstance(owner, int):
            spot = pl.multiple_of(spot, rows)
        near = ordered[pl.ds(spot, rows), :width]
        far = ordered[pl.ds(spot, rows), width:]
        label = jnp.sum(jnp.where(ids == owner, labels, 0.0), axis=0, keepdims=True)
        label = jnp.broadcast_to(label, (length - 2 * rows, width))
        if length % 16 == 0:
            pieces = [(0, jnp.concatenate([near, far, label], axis=0))]
        else:
            pieces = [(0, near), (rows, far), (2 * rows, label)]
        for z in range(near_count):
            start = message_at(owner, z, wide_count, near_count, length)
            for offset, piece in pieces:
                send_ref[pl.ds(start + offset, piece.shape[0])] = piece.astype(send_ref.dtype)
        return 0

    each(wide_count, write, 0)


def ladder_kernel(
    rows, near_count, own_count, recv_count, amp_ref, got_ref, out_ref, tiles, column, seen
):
    wide_count = seen.shape[0]
    width = got_ref.shape[1]
    length = got_ref.shape[0] // (wide_count * near_count)
    half_size = near_count * rows
    upper = (lax.axis_index("narrow") >= near_count).astype(jnp.int32)
    near_at, far_at = upper * half_size, (1 - upper) * half_size
    tiles[...] = jnp.zeros_like(tiles)
    for u in range(recv_count):
        column[u] = 0

    def message(w, z):
        start = message_at(w, z, wide_count, near_count, length)
        if length % 16 == 0:
            block = got_ref[pl.ds(start, length)].astype(jnp.float32)
            return block[:rows], block[rows : 2 * rows]
        return got_ref[pl.ds(start, rows)], got_ref[pl.ds(start + rows, rows)]

    def read_label(w):
        start = message_at(w, 0, wide_count, near_count, length)
        if length % 16 == 0:
            label = got_ref[pl.ds(start, length)].astype(jnp.float32)[2 * rows :]
        else:
            label = got_ref[pl.ds(start + 2 * rows, length - 2 * rows)].astype(jnp.float32)
        return jnp.max(label).astype(jnp.int32)

    def keep(w, label, found):
        live = jnp.minimum(label, 1)
        at = jnp.where(label > 0, jnp.minimum(found, recv_count), recv_count)
        code = jnp.maximum(label - 1, 0)
        column[at] = lax.div(code, own_count)
        spot = pl.ds(pl.multiple_of(lax.rem(code, own_count) * width, width), width)
        parts = [message(w, z) for z in range(near_count)]
        for side in range(2):
            half = jnp.concatenate([part[side] for part in parts], axis=0).astype(tiles.dtype)
            start = at * width + (near_at if side == 0 else far_at)
            tiles[pl.ds(pl.multiple_of(start, half_size), half_size), spot] = half
        return found + live

    if wide_count <= UNROLL:
        labels = [read_label(w) for w in range(wide_count)]
        found = jnp.int32(0)
        for w in range(wide_count):
            found = keep(w, labels[w], found)
    else:

        def note(w, _):
            seen[w] = read_label(w)
            return 0

        lax.fori_loop(0, wide_count, note, 0)
        lax.fori_loop(0, wide_count, lambda w, found: keep(w, seen[w], found), jnp.int32(0))
    total = None
    for first in range(0, recv_count, GROUP):
        last = min(first + GROUP, recv_count)
        spots = [pl.multiple_of(column[u] * width, width) for u in range(first, last)]
        picked = jnp.concatenate([amp_ref[:, pl.ds(spot, width)] for spot in spots], axis=1)
        term = jnp.dot(
            picked, tiles[first * width : last * width], preferred_element_type=jnp.float32
        )
        total = term if total is None else total + term
    out_ref[...] = total


def shards(amplitudes, integrals, in_tile, counts, out_tile, owner_map):
    slot_count, rows, width = integrals.shape
    row_count = amplitudes.shape[0]
    wide_count = lax.axis_size("wide")
    depth_count = lax.axis_size("narrow")
    own_count = owner_map.shape[0] // wide_count
    recv_count = slot_count // 2
    near_count = depth_count // 2
    kind = integrals.dtype
    message_count = wide_count * near_count
    length = 2 * rows + PAIR
    if wide_count > UNROLL or length % PAIR != 0 or message_count * length % 16 != 0:
        length = -(-length // 16) * 16
    hbm = pl.BlockSpec(memory_space=pltpu.HBM)
    vmem = pl.BlockSpec(memory_space=pltpu.VMEM)
    limit = pltpu.CompilerParams(vmem_limit_bytes=32 * 2**20)
    across = [(z, (z + near_count) % depth_count) for z in range(depth_count)]
    far = lax.ppermute(integrals, "narrow", across)
    given = [in_tile, counts, out_tile, owner_map, integrals]
    given = [
        value if value.size == 1 else pltpu.with_memory_space_constraint(value, pltpu.HBM)
        for value in given
    ]
    ordered, sent = wide_count * rows, slot_count * rows
    order, labels, near = pl.pallas_call(
        functools.partial(route_kernel, own_count, wide_count),
        out_shape=[
            jax.ShapeDtypeStruct((ordered, sent), kind),
            jax.ShapeDtypeStruct((wide_count, width), kind),
            jax.ShapeDtypeStruct(integrals.shape, kind),
        ],
        in_specs=[hbm] * len(given),
        out_specs=[vmem] * 3,
        scratch_shapes=[pltpu.SMEM(value.shape, value.dtype) for value in given[:-1]]
        + [pltpu.SemaphoreType.DMA((len(given),))],
        compiler_params=limit,
        cost_estimate=pl.CostEstimate(flops=2**30, bytes_accessed=2**20, transcendentals=0),
        name="route",
    )(*given)
    send = pl.pallas_call(
        functools.partial(pack_kernel, wide_count, near_count),
        out_shape=jax.ShapeDtypeStruct((message_count * length, width), kind),
        in_specs=[vmem] * 4,
        out_specs=vmem,
        scratch_shapes=[
            pltpu.VMEM((sent, 2 * width), kind),
            pltpu.VMEM((ordered, 2 * width), jnp.float32),
        ],
        compiler_params=limit,
        name="pack",
    )(order, labels, near, far)
    places = group_places(wide_count, near_count)
    groups = [
        [w * depth_count + half * near_count + z for w, z in places] for half in range(2)
    ]
    got = lax.all_to_all(
        send.reshape(message_count, length // PAIR, PAIR, width),
        ("wide", "narrow"),
        split_axis=0,
        concat_axis=0,
        tiled=True,
        axis_index_groups=groups,
    ).reshape(message_count * length, width)
    return pl.pallas_call(
        functools.partial(ladder_kernel, rows, near_count, own_count, recv_count),
        out_shape=jax.ShapeDtypeStruct((row_count, own_count * width), jnp.float32),
        in_specs=[vmem] * 2,
        out_specs=vmem,
        scratch_shapes=[
            pltpu.VMEM(((recv_count + 1) * width, own_count * width), kind),
            pltpu.SMEM((recv_count + 1,), jnp.int32),
            pltpu.SMEM((wide_count,), jnp.int32),
        ],
        compiler_params=limit,
        name="ladder",
    )(amplitudes, got)


def solution(mesh):
    return jax.shard_map(
        shards,
        mesh=mesh,
        in_specs=(
            P("narrow", None),
            P("wide", "narrow", None),
            P("wide"),
            P("wide"),
            P("wide"),
            P(),
        ),
        out_specs=P("narrow", "wide"),
        check_vma=False,
    )
```

```python
import functools

import jax
import jax.numpy as jnp
from jax import lax
from jax.experimental import pallas as pl
from jax.experimental.pallas import tpu as pltpu
from jax.sharding import PartitionSpec as P

PAIR = 2
GROUP = 4
UNROLL = 8
CORES = 2


def each(count, body, start):
    if count > UNROLL:
        return lax.fori_loop(0, count, body, start)
    for i in range(count):
        start = body(i, start)
    return start


def chip_order(wide_count):
    chip_count = wide_count // CORES
    if wide_count > UNROLL:
        return list(range(chip_count))
    bits = (chip_count - 1).bit_length()
    flipped = [int(format(chip, "b").zfill(bits)[::-1], 2) for chip in range(2**bits)]
    return [chip for chip in flipped[1:] if chip < chip_count] + [0]


def group_places(wide_count, near_count):
    cores = range(CORES)
    depths = range(near_count)
    return [(chip * CORES + core, z) for chip in chip_order(wide_count) for core in cores for z in depths]


def message_at(w, z, wide_count, near_count, length):
    if isinstance(w, int):
        return group_places(wide_count, near_count).index((w, z)) * length
    place = w * near_count + z
    return pl.multiple_of(place * length, length)


def route_kernel(own_count, wide_count, *refs):
    sources, (order_ref, label_ref, near_ref), targets, sems = refs[:5], refs[5:8], refs[8:12], refs[12]
    in_tile, counts, out_tile, owner_map = targets
    copies = [
        pltpu.make_async_copy(source, target, sems.at[i])
        for i, (source, target) in enumerate(zip(sources, (*targets, near_ref)))
    ]
    for copy in copies:
        copy.start()
    for copy in copies[:4]:
        copy.wait()
    slot_count, rows, width = near_ref.shape
    column = lax.broadcasted_iota(jnp.int32, (1, slot_count * rows), 1)
    owners = lax.broadcasted_iota(jnp.int32, (wide_count, width), 0)

    def route(h, carry):
        owner_of, labels = carry
        spot = owner_map[out_tile[h]]
        owner = lax.div(spot, own_count)
        label = in_tile[h] * own_count + lax.rem(spot, own_count) + 1
        label = jnp.where(h < counts[0], label, 0)
        owner_of = jnp.where(lax.div(column, rows) == h, owner, owner_of)
        return owner_of, jnp.where(owners == owner, label, labels)

    start = (jnp.zeros_like(column), jnp.zeros((wide_count, width), jnp.int32))
    owner_of, labels = each(slot_count, route, start)
    label_ref[...] = labels.astype(jnp.float32).astype(label_ref.dtype)
    row = lax.broadcasted_iota(jnp.int32, (wide_count * rows, 1), 0)
    hit = row == owner_of * rows + lax.rem(column, rows)
    order_ref[...] = hit.astype(jnp.float32).astype(order_ref.dtype)
    copies[4].wait()


def pack_kernel(wide_count, near_count, order_ref, label_ref, near_ref, far_ref, send_ref, both, ordered):
    slot_count, rows, width = near_ref.shape
    length = send_ref.shape[0] // (wide_count * near_count)
    for side, ref in enumerate((near_ref, far_ref)):
        block = ref[...]
        if rows % 16 != 0:
            block = block.astype(jnp.float32)
        block = block.reshape(slot_count * rows, width).astype(both.dtype)
        both[:, side * width : (side + 1) * width] = block
    ordered[...] = jnp.dot(order_ref[...], both[...], preferred_element_type=jnp.float32)
    labels = label_ref[...].astype(jnp.float32)
    ids = lax.broadcasted_iota(jnp.int32, labels.shape, 0)

    def write(owner, _):
        spot = owner * rows
        if not isinstance(owner, int):
            spot = pl.multiple_of(spot, rows)
        near = ordered[pl.ds(spot, rows), :width]
        far = ordered[pl.ds(spot, rows), width:]
        label = jnp.sum(jnp.where(ids == owner, labels, 0.0), axis=0, keepdims=True)
        label = jnp.broadcast_to(label, (length - 2 * rows, width))
        if length % 16 == 0:
            pieces = [(0, jnp.concatenate([near, far, label], axis=0))]
        else:
            pieces = [(0, near), (rows, far), (2 * rows, label)]
        for z in range(near_count):
            start = message_at(owner, z, wide_count, near_count, length)
            for offset, piece in pieces:
                send_ref[pl.ds(start + offset, piece.shape[0])] = piece.astype(send_ref.dtype)
        return 0

    each(wide_count, write, 0)


def ladder_kernel(
    rows, near_count, own_count, recv_count, amp_ref, got_ref, out_ref, tiles, column, seen
):
    wide_count = seen.shape[0]
    width = got_ref.shape[1]
    length = got_ref.shape[0] // (wide_count * near_count)
    half_size = near_count * rows
    upper = (lax.axis_index("narrow") >= near_count).astype(jnp.int32)
    near_at, far_at = upper * half_size, (1 - upper) * half_size
    tiles[...] = jnp.zeros_like(tiles)
    for u in range(recv_count):
        column[u] = 0

    def message(w, z):
        start = message_at(w, z, wide_count, near_count, length)
        if length % 16 == 0:
            block = got_ref[pl.ds(start, length)].astype(jnp.float32)
            return block[:rows], block[rows : 2 * rows]
        return got_ref[pl.ds(start, rows)], got_ref[pl.ds(start + rows, rows)]

    def read_label(w):
        start = message_at(w, 0, wide_count, near_count, length)
        if length % 16 == 0:
            label = got_ref[pl.ds(start, length)].astype(jnp.float32)[2 * rows :]
        else:
            label = got_ref[pl.ds(start + 2 * rows, length - 2 * rows)].astype(jnp.float32)
        return jnp.max(label).astype(jnp.int32)

    def keep(w, label, found):
        live = jnp.minimum(label, 1)
        at = jnp.where(label > 0, jnp.minimum(found, recv_count), recv_count)
        code = jnp.maximum(label - 1, 0)
        column[at] = lax.div(code, own_count)
        spot = pl.ds(pl.multiple_of(lax.rem(code, own_count) * width, width), width)
        parts = [message(w, z) for z in range(near_count)]
        for side in range(2):
            half = jnp.concatenate([part[side] for part in parts], axis=0).astype(tiles.dtype)
            start = at * width + (near_at if side == 0 else far_at)
            tiles[pl.ds(pl.multiple_of(start, half_size), half_size), spot] = half
        return found + live

    if wide_count <= UNROLL:
        labels = [read_label(w) for w in range(wide_count)]
        found = jnp.int32(0)
        for w in range(wide_count):
            found = keep(w, labels[w], found)
    else:

        def note(w, _):
            seen[w] = read_label(w)
            return 0

        lax.fori_loop(0, wide_count, note, 0)
        lax.fori_loop(0, wide_count, lambda w, found: keep(w, seen[w], found), jnp.int32(0))
    total = None
    for first in range(0, recv_count, GROUP):
        last = min(first + GROUP, recv_count)
        spots = [pl.multiple_of(column[u] * width, width) for u in range(first, last)]
        picked = jnp.concatenate([amp_ref[:, pl.ds(spot, width)] for spot in spots], axis=1)
        term = jnp.dot(
            picked, tiles[first * width : last * width], preferred_element_type=jnp.float32
        )
        total = term if total is None else total + term
    out_ref[...] = total


def shards(amplitudes, integrals, in_tile, counts, out_tile, owner_map):
    slot_count, rows, width = integrals.shape
    row_count = amplitudes.shape[0]
    wide_count = lax.axis_size("wide")
    depth_count = lax.axis_size("narrow")
    own_count = owner_map.shape[0] // wide_count
    recv_count = slot_count // 2
    near_count = depth_count // 2
    kind = integrals.dtype
    message_count = wide_count * near_count
    length = -(-(2 * rows + 1) // 16) * 16
    hbm = pl.BlockSpec(memory_space=pltpu.HBM)
    vmem = pl.BlockSpec(memory_space=pltpu.VMEM)
    limit = pltpu.CompilerParams(vmem_limit_bytes=32 * 2**20)
    across = [(z, (z + near_count) % depth_count) for z in range(depth_count)]
    far = lax.ppermute(integrals, "narrow", across)
    given = [in_tile, counts, out_tile, owner_map, integrals]
    given = [
        value if value.size == 1 else pltpu.with_memory_space_constraint(value, pltpu.HBM)
        for value in given
    ]
    ordered, sent = wide_count * rows, slot_count * rows
    order, labels, near = pl.pallas_call(
        functools.partial(route_kernel, own_count, wide_count),
        out_shape=[
            jax.ShapeDtypeStruct((ordered, sent), kind),
            jax.ShapeDtypeStruct((wide_count, width), kind),
            jax.ShapeDtypeStruct(integrals.shape, kind),
        ],
        in_specs=[hbm] * len(given),
        out_specs=[vmem] * 3,
        scratch_shapes=[pltpu.SMEM(value.shape, value.dtype) for value in given[:-1]]
        + [pltpu.SemaphoreType.DMA((len(given),))],
        compiler_params=limit,
        cost_estimate=pl.CostEstimate(flops=2**30, bytes_accessed=2**20, transcendentals=0),
        name="route",
    )(*given)
    send = pl.pallas_call(
        functools.partial(pack_kernel, wide_count, near_count),
        out_shape=jax.ShapeDtypeStruct((message_count * length, width), kind),
        in_specs=[vmem] * 4,
        out_specs=vmem,
        scratch_shapes=[
            pltpu.VMEM((sent, 2 * width), kind),
            pltpu.VMEM((ordered, 2 * width), jnp.float32),
        ],
        compiler_params=limit,
        name="pack",
    )(order, labels, near, far)
    places = group_places(wide_count, near_count)
    groups = [
        [w * depth_count + half * near_count + z for w, z in places] for half in range(2)
    ]
    got = lax.all_to_all(
        send.reshape(message_count, length // PAIR, PAIR, width),
        ("wide", "narrow"),
        split_axis=0,
        concat_axis=0,
        tiled=True,
        axis_index_groups=groups,
    ).reshape(message_count * length, width)
    return pl.pallas_call(
        functools.partial(ladder_kernel, rows, near_count, own_count, recv_count),
        out_shape=jax.ShapeDtypeStruct((row_count, own_count * width), jnp.float32),
        in_specs=[vmem] * 2,
        out_specs=vmem,
        scratch_shapes=[
            pltpu.VMEM(((recv_count + 1) * width, own_count * width), kind),
            pltpu.SMEM((recv_count + 1,), jnp.int32),
            pltpu.SMEM((wide_count,), jnp.int32),
        ],
        compiler_params=limit,
        name="ladder",
    )(amplitudes, got)


def solution(mesh):
    return jax.shard_map(
        shards,
        mesh=mesh,
        in_specs=(
            P("narrow", None),
            P("wide", "narrow", None),
            P("wide"),
            P("wide"),
            P("wide"),
            P(),
        ),
        out_specs=P("narrow", "wide"),
        check_vma=False,
    )
```

```python
import functools

import jax
import jax.numpy as jnp
from jax import lax
from jax.experimental import pallas as pl
from jax.experimental.pallas import tpu as pltpu
from jax.sharding import PartitionSpec as P

PAIR = 2
GROUP = 4
UNROLL = 8
CORES = 2


def each(count, body, start):
    if count > UNROLL:
        return lax.fori_loop(0, count, body, start)
    for i in range(count):
        start = body(i, start)
    return start


def chip_order(wide_count):
    chip_count = wide_count // CORES
    if wide_count > UNROLL:
        return list(range(chip_count))
    size = 2 ** (chip_count - 1).bit_length()
    ring = [step ^ (step >> 1) for step in range(1, size)]
    return [chip for chip in ring if chip < chip_count] + [0]


def group_places(wide_count, near_count):
    cores = range(CORES)
    depths = range(near_count)
    return [(chip * CORES + core, z) for chip in chip_order(wide_count) for core in cores for z in depths]


def message_at(w, z, wide_count, near_count, length):
    if isinstance(w, int):
        return group_places(wide_count, near_count).index((w, z)) * length
    place = w * near_count + z
    return pl.multiple_of(place * length, length)


def route_kernel(own_count, wide_count, *refs):
    sources, (order_ref, label_ref, near_ref), targets, sems = refs[:5], refs[5:8], refs[8:12], refs[12]
    in_tile, counts, out_tile, owner_map = targets
    copies = [
        pltpu.make_async_copy(source, target, sems.at[i])
        for i, (source, target) in enumerate(zip(sources, (*targets, near_ref)))
    ]
    for copy in copies:
        copy.start()
    for copy in copies[:4]:
        copy.wait()
    slot_count, rows, width = near_ref.shape
    column = lax.broadcasted_iota(jnp.int32, (1, slot_count * rows), 1)
    owners = lax.broadcasted_iota(jnp.int32, (wide_count, width), 0)

    def route(h, carry):
        owner_of, labels = carry
        spot = owner_map[out_tile[h]]
        owner = lax.div(spot, own_count)
        label = in_tile[h] * own_count + lax.rem(spot, own_count) + 1
        label = jnp.where(h < counts[0], label, 0)
        owner_of = jnp.where(lax.div(column, rows) == h, owner, owner_of)
        return owner_of, jnp.where(owners == owner, label, labels)

    start = (jnp.zeros_like(column), jnp.zeros((wide_count, width), jnp.int32))
    owner_of, labels = each(slot_count, route, start)
    label_ref[...] = labels.astype(jnp.float32).astype(label_ref.dtype)
    row = lax.broadcasted_iota(jnp.int32, (wide_count * rows, 1), 0)
    hit = row == owner_of * rows + lax.rem(column, rows)
    order_ref[...] = hit.astype(jnp.float32).astype(order_ref.dtype)
    copies[4].wait()


def pack_kernel(wide_count, near_count, order_ref, label_ref, near_ref, far_ref, send_ref, both, ordered):
    slot_count, rows, width = near_ref.shape
    length = send_ref.shape[0] // (wide_count * near_count)
    for side, ref in enumerate((near_ref, far_ref)):
        block = ref[...]
        if rows % 16 != 0:
            block = block.astype(jnp.float32)
        block = block.reshape(slot_count * rows, width).astype(both.dtype)
        both[:, side * width : (side + 1) * width] = block
    ordered[...] = jnp.dot(order_ref[...], both[...], preferred_element_type=jnp.float32)
    labels = label_ref[...].astype(jnp.float32)
    ids = lax.broadcasted_iota(jnp.int32, labels.shape, 0)

    def write(owner, _):
        spot = owner * rows
        if not isinstance(owner, int):
            spot = pl.multiple_of(spot, rows)
        near = ordered[pl.ds(spot, rows), :width]
        far = ordered[pl.ds(spot, rows), width:]
        label = jnp.sum(jnp.where(ids == owner, labels, 0.0), axis=0, keepdims=True)
        label = jnp.broadcast_to(label, (length - 2 * rows, width))
        if length % 16 == 0:
            pieces = [(0, jnp.concatenate([near, far, label], axis=0))]
        else:
            pieces = [(0, near), (rows, far), (2 * rows, label)]
        for z in range(near_count):
            start = message_at(owner, z, wide_count, near_count, length)
            for offset, piece in pieces:
                send_ref[pl.ds(start + offset, piece.shape[0])] = piece.astype(send_ref.dtype)
        return 0

    each(wide_count, write, 0)


def ladder_kernel(
    rows, near_count, own_count, recv_count, amp_ref, got_ref, out_ref, tiles, column, seen
):
    wide_count = seen.shape[0]
    width = got_ref.shape[1]
    length = got_ref.shape[0] // (wide_count * near_count)
    half_size = near_count * rows
    upper = (lax.axis_index("narrow") >= near_count).astype(jnp.int32)
    near_at, far_at = upper * half_size, (1 - upper) * half_size
    tiles[...] = jnp.zeros_like(tiles)
    for u in range(recv_count):
        column[u] = 0

    def message(w, z):
        start = message_at(w, z, wide_count, near_count, length)
        if length % 16 == 0:
            block = got_ref[pl.ds(start, length)].astype(jnp.float32)
            return block[:rows], block[rows : 2 * rows]
        return got_ref[pl.ds(start, rows)], got_ref[pl.ds(start + rows, rows)]

    def read_label(w):
        start = message_at(w, 0, wide_count, near_count, length)
        if length % 16 == 0:
            label = got_ref[pl.ds(start, length)].astype(jnp.float32)[2 * rows :]
        else:
            label = got_ref[pl.ds(start + 2 * rows, length - 2 * rows)].astype(jnp.float32)
        return jnp.max(label).astype(jnp.int32)

    def keep(w, label, found):
        live = jnp.minimum(label, 1)
        at = jnp.where(label > 0, jnp.minimum(found, recv_count), recv_count)
        code = jnp.maximum(label - 1, 0)
        column[at] = lax.div(code, own_count)
        spot = pl.ds(pl.multiple_of(lax.rem(code, own_count) * width, width), width)
        parts = [message(w, z) for z in range(near_count)]
        for side in range(2):
            half = jnp.concatenate([part[side] for part in parts], axis=0).astype(tiles.dtype)
            start = at * width + (near_at if side == 0 else far_at)
            tiles[pl.ds(pl.multiple_of(start, half_size), half_size), spot] = half
        return found + live

    if wide_count <= UNROLL:
        labels = [read_label(w) for w in range(wide_count)]
        found = jnp.int32(0)
        for w in range(wide_count):
            found = keep(w, labels[w], found)
    else:

        def note(w, _):
            seen[w] = read_label(w)
            return 0

        lax.fori_loop(0, wide_count, note, 0)
        lax.fori_loop(0, wide_count, lambda w, found: keep(w, seen[w], found), jnp.int32(0))
    total = None
    for first in range(0, recv_count, GROUP):
        last = min(first + GROUP, recv_count)
        spots = [pl.multiple_of(column[u] * width, width) for u in range(first, last)]
        picked = jnp.concatenate([amp_ref[:, pl.ds(spot, width)] for spot in spots], axis=1)
        term = jnp.dot(
            picked, tiles[first * width : last * width], preferred_element_type=jnp.float32
        )
        total = term if total is None else total + term
    out_ref[...] = total


def shards(amplitudes, integrals, in_tile, counts, out_tile, owner_map):
    slot_count, rows, width = integrals.shape
    row_count = amplitudes.shape[0]
    wide_count = lax.axis_size("wide")
    depth_count = lax.axis_size("narrow")
    own_count = owner_map.shape[0] // wide_count
    recv_count = slot_count // 2
    near_count = depth_count // 2
    kind = integrals.dtype
    message_count = wide_count * near_count
    length = 2 * rows + PAIR
    if wide_count > UNROLL or length % PAIR != 0 or message_count * length % 16 != 0:
        length = -(-length // 16) * 16
    hbm = pl.BlockSpec(memory_space=pltpu.HBM)
    vmem = pl.BlockSpec(memory_space=pltpu.VMEM)
    limit = pltpu.CompilerParams(vmem_limit_bytes=32 * 2**20)
    across = [(z, (z + near_count) % depth_count) for z in range(depth_count)]
    far = lax.ppermute(integrals, "narrow", across)
    given = [in_tile, counts, out_tile, owner_map, integrals]
    given = [
        value if value.size == 1 else pltpu.with_memory_space_constraint(value, pltpu.HBM)
        for value in given
    ]
    ordered, sent = wide_count * rows, slot_count * rows
    order, labels, near = pl.pallas_call(
        functools.partial(route_kernel, own_count, wide_count),
        out_shape=[
            jax.ShapeDtypeStruct((ordered, sent), kind),
            jax.ShapeDtypeStruct((wide_count, width), kind),
            jax.ShapeDtypeStruct(integrals.shape, kind),
        ],
        in_specs=[hbm] * len(given),
        out_specs=[vmem] * 3,
        scratch_shapes=[pltpu.SMEM(value.shape, value.dtype) for value in given[:-1]]
        + [pltpu.SemaphoreType.DMA((len(given),))],
        compiler_params=limit,
        cost_estimate=pl.CostEstimate(flops=2**30, bytes_accessed=2**20, transcendentals=0),
        name="route",
    )(*given)
    send = pl.pallas_call(
        functools.partial(pack_kernel, wide_count, near_count),
        out_shape=jax.ShapeDtypeStruct((message_count * length, width), kind),
        in_specs=[vmem] * 4,
        out_specs=vmem,
        scratch_shapes=[
            pltpu.VMEM((sent, 2 * width), kind),
            pltpu.VMEM((ordered, 2 * width), jnp.float32),
        ],
        compiler_params=limit,
        name="pack",
    )(order, labels, near, far)
    places = group_places(wide_count, near_count)
    groups = [
        [w * depth_count + half * near_count + z for w, z in places] for half in range(2)
    ]
    got = lax.all_to_all(
        send.reshape(message_count, length // PAIR, PAIR, width),
        ("wide", "narrow"),
        split_axis=0,
        concat_axis=0,
        tiled=True,
        axis_index_groups=groups,
    ).reshape(message_count * length, width)
    return pl.pallas_call(
        functools.partial(ladder_kernel, rows, near_count, own_count, recv_count),
        out_shape=jax.ShapeDtypeStruct((row_count, own_count * width), jnp.float32),
        in_specs=[vmem] * 2,
        out_specs=vmem,
        scratch_shapes=[
            pltpu.VMEM(((recv_count + 1) * width, own_count * width), kind),
            pltpu.SMEM((recv_count + 1,), jnp.int32),
            pltpu.SMEM((wide_count,), jnp.int32),
        ],
        compiler_params=limit,
        name="ladder",
    )(amplitudes, got)


def solution(mesh):
    return jax.shard_map(
        shards,
        mesh=mesh,
        in_specs=(
            P("narrow", None),
            P("wide", "narrow", None),
            P("wide"),
            P("wide"),
            P("wide"),
            P(),
        ),
        out_specs=P("narrow", "wide"),
        check_vma=False,
    )
```

```python
import functools

import jax
import jax.numpy as jnp
from jax import lax
from jax.experimental import pallas as pl
from jax.experimental.pallas import tpu as pltpu
from jax.sharding import PartitionSpec as P

PAIR = 2
GROUP = 4
UNROLL = 8
CORES = 2
PARTS = 2


def each(count, body, start):
    if count > UNROLL:
        return lax.fori_loop(0, count, body, start)
    for i in range(count):
        start = body(i, start)
    return start


def chip_order(wide_count):
    chip_count = wide_count // CORES
    if wide_count > UNROLL:
        return list(range(chip_count))
    bits = (chip_count - 1).bit_length()
    flipped = [int(format(chip, "b").zfill(bits)[::-1], 2) for chip in range(2**bits)]
    return [chip for chip in flipped[1:] if chip < chip_count] + [0]


def group_places(wide_count, near_count):
    cores = range(CORES)
    depths = range(near_count)
    return [(chip * CORES + core, z) for chip in chip_order(wide_count) for core in cores for z in depths]


def message_at(w, z, wide_count, near_count, length):
    if isinstance(w, int):
        return group_places(wide_count, near_count).index((w, z)) * length
    place = w * near_count + z
    return pl.multiple_of(place * length, length)


def stage_kernel(source, *refs):
    *targets, sems = refs
    size = targets[0].shape[0]
    copies = [
        pltpu.make_async_copy(source.at[pl.ds(i * size, size)], target, sems.at[i])
        for i, target in enumerate(targets)
    ]
    for copy in copies:
        copy.start()
    for copy in copies:
        copy.wait()


def route_kernel(own_count, wide_count, *refs):
    sources, (order_ref, label_ref), targets, sems = refs[:4], refs[4:6], refs[6:10], refs[10]
    in_tile, counts, out_tile, owner_map = targets
    copies = [
        pltpu.make_async_copy(source, target, sems.at[i])
        for i, (source, target) in enumerate(zip(sources, targets))
    ]
    for copy in copies:
        copy.start()
    for copy in copies:
        copy.wait()
    slot_count = in_tile.shape[0]
    rows, width = order_ref.shape[0] // wide_count, label_ref.shape[1]
    column = lax.broadcasted_iota(jnp.int32, (1, slot_count * rows), 1)
    owners = lax.broadcasted_iota(jnp.int32, (wide_count, width), 0)

    def route(h, carry):
        owner_of, labels = carry
        spot = owner_map[out_tile[h]]
        owner = lax.div(spot, own_count)
        label = in_tile[h] * own_count + lax.rem(spot, own_count) + 1
        label = jnp.where(h < counts[0], label, 0)
        owner_of = jnp.where(lax.div(column, rows) == h, owner, owner_of)
        return owner_of, jnp.where(owners == owner, label, labels)

    start = (jnp.zeros_like(column), jnp.zeros((wide_count, width), jnp.int32))
    owner_of, labels = each(slot_count, route, start)
    label_ref[...] = labels.astype(jnp.float32).astype(label_ref.dtype)
    row = lax.broadcasted_iota(jnp.int32, (wide_count * rows, 1), 0)
    hit = row == owner_of * rows + lax.rem(column, rows)
    order_ref[...] = hit.astype(jnp.float32).astype(order_ref.dtype)


def pack_kernel(wide_count, near_count, order_ref, label_ref, *refs):
    *given, send_ref, both, ordered = refs
    part_count = len(given) // 2
    slots, rows, width = given[0].shape
    length = send_ref.shape[0] // (wide_count * near_count)
    for i, ref in enumerate(given):
        side, part = divmod(i, part_count)
        block = ref[...]
        if rows % 16 != 0:
            block = block.astype(jnp.float32)
        block = block.reshape(slots * rows, width).astype(both.dtype)
        at = slice(part * slots * rows, (part + 1) * slots * rows)
        both[at, side * width : (side + 1) * width] = block
    ordered[...] = jnp.dot(order_ref[...], both[...], preferred_element_type=jnp.float32)
    labels = label_ref[...].astype(jnp.float32)
    ids = lax.broadcasted_iota(jnp.int32, labels.shape, 0)

    def write(owner, _):
        spot = owner * rows
        if not isinstance(owner, int):
            spot = pl.multiple_of(spot, rows)
        near = ordered[pl.ds(spot, rows), :width]
        far = ordered[pl.ds(spot, rows), width:]
        label = jnp.sum(jnp.where(ids == owner, labels, 0.0), axis=0, keepdims=True)
        label = jnp.broadcast_to(label, (length - 2 * rows, width))
        if length % 16 == 0:
            pieces = [(0, jnp.concatenate([near, far, label], axis=0))]
        else:
            pieces = [(0, near), (rows, far), (2 * rows, label)]
        for z in range(near_count):
            start = message_at(owner, z, wide_count, near_count, length)
            for offset, piece in pieces:
                send_ref[pl.ds(start + offset, piece.shape[0])] = piece.astype(send_ref.dtype)
        return 0

    each(wide_count, write, 0)


def ladder_kernel(
    rows, near_count, own_count, recv_count, amp_ref, got_ref, out_ref, tiles, column, seen
):
    wide_count = seen.shape[0]
    width = got_ref.shape[1]
    length = got_ref.shape[0] // (wide_count * near_count)
    half_size = near_count * rows
    upper = (lax.axis_index("narrow") >= near_count).astype(jnp.int32)
    near_at, far_at = upper * half_size, (1 - upper) * half_size
    tiles[...] = jnp.zeros_like(tiles)
    for u in range(recv_count):
        column[u] = 0

    def message(w, z):
        start = message_at(w, z, wide_count, near_count, length)
        if length % 16 == 0:
            block = got_ref[pl.ds(start, length)].astype(jnp.float32)
            return block[:rows], block[rows : 2 * rows]
        return got_ref[pl.ds(start, rows)], got_ref[pl.ds(start + rows, rows)]

    def read_label(w):
        start = message_at(w, 0, wide_count, near_count, length)
        if length % 16 == 0:
            label = got_ref[pl.ds(start, length)].astype(jnp.float32)[2 * rows :]
        else:
            label = got_ref[pl.ds(start + 2 * rows, length - 2 * rows)].astype(jnp.float32)
        return jnp.max(label).astype(jnp.int32)

    def keep(w, label, found):
        live = jnp.minimum(label, 1)
        at = jnp.where(label > 0, jnp.minimum(found, recv_count), recv_count)
        code = jnp.maximum(label - 1, 0)
        column[at] = lax.div(code, own_count)
        spot = pl.ds(pl.multiple_of(lax.rem(code, own_count) * width, width), width)
        parts = [message(w, z) for z in range(near_count)]
        for side in range(2):
            half = jnp.concatenate([part[side] for part in parts], axis=0).astype(tiles.dtype)
            start = at * width + (near_at if side == 0 else far_at)
            tiles[pl.ds(pl.multiple_of(start, half_size), half_size), spot] = half
        return found + live

    if wide_count <= UNROLL:
        labels = [read_label(w) for w in range(wide_count)]
        found = jnp.int32(0)
        for w in range(wide_count):
            found = keep(w, labels[w], found)
    else:

        def note(w, _):
            seen[w] = read_label(w)
            return 0

        lax.fori_loop(0, wide_count, note, 0)
        lax.fori_loop(0, wide_count, lambda w, found: keep(w, seen[w], found), jnp.int32(0))
    total = None
    for first in range(0, recv_count, GROUP):
        last = min(first + GROUP, recv_count)
        spots = [pl.multiple_of(column[u] * width, width) for u in range(first, last)]
        picked = jnp.concatenate([amp_ref[:, pl.ds(spot, width)] for spot in spots], axis=1)
        term = jnp.dot(
            picked, tiles[first * width : last * width], preferred_element_type=jnp.float32
        )
        total = term if total is None else total + term
    out_ref[...] = total


def shards(amplitudes, integrals, in_tile, counts, out_tile, owner_map):
    slot_count, rows, width = integrals.shape
    row_count = amplitudes.shape[0]
    wide_count = lax.axis_size("wide")
    depth_count = lax.axis_size("narrow")
    own_count = owner_map.shape[0] // wide_count
    recv_count = slot_count // 2
    near_count = depth_count // 2
    kind = integrals.dtype
    message_count = wide_count * near_count
    length = 2 * rows + PAIR
    if wide_count > UNROLL or length % PAIR != 0 or message_count * length % 16 != 0:
        length = -(-length // 16) * 16
    hbm = pl.BlockSpec(memory_space=pltpu.HBM)
    vmem = pl.BlockSpec(memory_space=pltpu.VMEM)
    limit = pltpu.CompilerParams(vmem_limit_bytes=32 * 2**20)
    across = [(z, (z + near_count) % depth_count) for z in range(depth_count)]
    part_shape = jax.ShapeDtypeStruct((slot_count // PARTS, rows, width), kind)
    near = pl.pallas_call(
        stage_kernel,
        out_shape=[part_shape] * PARTS,
        in_specs=[hbm],
        out_specs=[vmem] * PARTS,
        scratch_shapes=[pltpu.SemaphoreType.DMA((PARTS,))],
        compiler_params=limit,
        name="stage",
    )(pltpu.with_memory_space_constraint(integrals, pltpu.HBM))
    far = [lax.ppermute(part, "narrow", across) for part in near]
    given = [in_tile, counts, out_tile, owner_map]
    given = [
        value if value.size == 1 else pltpu.with_memory_space_constraint(value, pltpu.HBM)
        for value in given
    ]
    ordered, sent = wide_count * rows, slot_count * rows
    order, labels = pl.pallas_call(
        functools.partial(route_kernel, own_count, wide_count),
        out_shape=[
            jax.ShapeDtypeStruct((ordered, sent), kind),
            jax.ShapeDtypeStruct((wide_count, width), kind),
        ],
        in_specs=[hbm] * len(given),
        out_specs=[vmem] * 2,
        scratch_shapes=[pltpu.SMEM(value.shape, value.dtype) for value in given]
        + [pltpu.SemaphoreType.DMA((len(given),))],
        compiler_params=limit,
        cost_estimate=pl.CostEstimate(flops=2**30, bytes_accessed=2**20, transcendentals=0),
        name="route",
    )(*given)
    send = pl.pallas_call(
        functools.partial(pack_kernel, wide_count, near_count),
        out_shape=jax.ShapeDtypeStruct((message_count * length, width), kind),
        in_specs=[vmem] * (2 + 2 * PARTS),
        out_specs=vmem,
        scratch_shapes=[
            pltpu.VMEM((sent, 2 * width), kind),
            pltpu.VMEM((ordered, 2 * width), jnp.float32),
        ],
        compiler_params=limit,
        name="pack",
    )(order, labels, *near, *far)
    places = group_places(wide_count, near_count)
    groups = [
        [w * depth_count + half * near_count + z for w, z in places] for half in range(2)
    ]
    got = lax.all_to_all(
        send.reshape(message_count, length // PAIR, PAIR, width),
        ("wide", "narrow"),
        split_axis=0,
        concat_axis=0,
        tiled=True,
        axis_index_groups=groups,
    ).reshape(message_count * length, width)
    return pl.pallas_call(
        functools.partial(ladder_kernel, rows, near_count, own_count, recv_count),
        out_shape=jax.ShapeDtypeStruct((row_count, own_count * width), jnp.float32),
        in_specs=[vmem] * 2,
        out_specs=vmem,
        scratch_shapes=[
            pltpu.VMEM(((recv_count + 1) * width, own_count * width), kind),
            pltpu.SMEM((recv_count + 1,), jnp.int32),
            pltpu.SMEM((wide_count,), jnp.int32),
        ],
        compiler_params=limit,
        name="ladder",
    )(amplitudes, got)


def solution(mesh):
    return jax.shard_map(
        shards,
        mesh=mesh,
        in_specs=(
            P("narrow", None),
            P("wide", "narrow", None),
            P("wide"),
            P("wide"),
            P("wide"),
            P(),
        ),
        out_specs=P("narrow", "wide"),
        check_vma=False,
    )
```

```python
import functools

import jax
import jax.numpy as jnp
from jax import lax
from jax.experimental import pallas as pl
from jax.experimental.pallas import tpu as pltpu
from jax.sharding import PartitionSpec as P

PAIR = 2
GROUP = 4
UNROLL = 8
CORES = 2


def each(count, body, start):
    if count > UNROLL:
        return lax.fori_loop(0, count, body, start)
    for i in range(count):
        start = body(i, start)
    return start


def chip_order(wide_count):
    chip_count = wide_count // CORES
    if wide_count > UNROLL:
        return list(range(chip_count))
    bits = (chip_count - 1).bit_length()
    flipped = [int(format(chip, "b").zfill(bits)[::-1], 2) for chip in range(2**bits)]
    return [chip for chip in flipped[1:] if chip < chip_count] + [0]


def group_places(wide_count, near_count):
    cores = range(CORES)
    depths = range(near_count)
    return [(chip * CORES + core, z) for chip in chip_order(wide_count) for core in cores for z in depths]


def message_at(w, z, wide_count, near_count, length):
    if isinstance(w, int):
        return group_places(wide_count, near_count).index((w, z)) * length
    place = w * near_count + z
    return pl.multiple_of(place * length, length)


def route_kernel(own_count, wide_count, *refs):
    sources, (order_ref, label_ref, near_ref), targets, sems = refs[:5], refs[5:8], refs[8:12], refs[12]
    in_tile, counts, out_tile, owner_map = targets
    copies = [
        pltpu.make_async_copy(source, target, sems.at[i])
        for i, (source, target) in enumerate(zip(sources, (*targets, near_ref)))
    ]
    for copy in copies:
        copy.start()
    for copy in copies[:4]:
        copy.wait()
    slot_count, rows, width = near_ref.shape
    column = lax.broadcasted_iota(jnp.int32, (1, slot_count * rows), 1)
    owners = lax.broadcasted_iota(jnp.int32, (wide_count, width), 0)

    def route(h, carry):
        owner_of, labels = carry
        spot = owner_map[out_tile[h]]
        owner = lax.div(spot, own_count)
        label = in_tile[h] * own_count + lax.rem(spot, own_count) + 1
        label = jnp.where(h < counts[0], label, 0)
        owner_of = jnp.where(lax.div(column, rows) == h, owner, owner_of)
        return owner_of, jnp.where(owners == owner, label, labels)

    start = (jnp.zeros_like(column), jnp.zeros((wide_count, width), jnp.int32))
    owner_of, labels = each(slot_count, route, start)
    label_ref[...] = labels.astype(jnp.float32).astype(label_ref.dtype)
    row = lax.broadcasted_iota(jnp.int32, (wide_count * rows, 1), 0)
    hit = row == owner_of * rows + lax.rem(column, rows)
    order_ref[...] = hit.astype(jnp.float32).astype(order_ref.dtype)
    copies[4].wait()


def pack_kernel(wide_count, near_count, order_ref, label_ref, near_ref, far_ref, send_ref, both, ordered):
    slot_count, rows, width = near_ref.shape
    length = send_ref.shape[0] // (wide_count * near_count)
    for side, ref in enumerate((near_ref, far_ref)):
        block = ref[...]
        if rows % 16 != 0:
            block = block.astype(jnp.float32)
        block = block.reshape(slot_count * rows, width).astype(both.dtype)
        both[:, side * width : (side + 1) * width] = block
    ordered[...] = jnp.dot(order_ref[...], both[...], preferred_element_type=jnp.float32)
    labels = label_ref[...].astype(jnp.float32)
    ids = lax.broadcasted_iota(jnp.int32, labels.shape, 0)

    def write(owner, _):
        spot = owner * rows
        if not isinstance(owner, int):
            spot = pl.multiple_of(spot, rows)
        near = ordered[pl.ds(spot, rows), :width]
        far = ordered[pl.ds(spot, rows), width:]
        label = jnp.sum(jnp.where(ids == owner, labels, 0.0), axis=0, keepdims=True)
        label = jnp.broadcast_to(label, (length - 2 * rows, width))
        if length % 16 == 0:
            pieces = [(0, jnp.concatenate([near, far, label], axis=0))]
        else:
            pieces = [(0, near), (rows, far), (2 * rows, label)]
        for z in range(near_count):
            start = message_at(owner, z, wide_count, near_count, length)
            for offset, piece in pieces:
                send_ref[pl.ds(start + offset, piece.shape[0])] = piece.astype(send_ref.dtype)
        return 0

    each(wide_count, write, 0)


def ladder_kernel(
    rows, near_count, own_count, recv_count, amp_ref, got_ref, out_ref, tiles, column, seen
):
    wide_count = seen.shape[0]
    width = got_ref.shape[1]
    length = got_ref.shape[0] // (wide_count * near_count)
    half_size = near_count * rows
    upper = (lax.axis_index("narrow") >= near_count).astype(jnp.int32)
    near_at, far_at = upper * half_size, (1 - upper) * half_size
    tiles[...] = jnp.zeros_like(tiles)
    for u in range(recv_count):
        column[u] = 0

    def message(w, z):
        start = message_at(w, z, wide_count, near_count, length)
        if length % 16 == 0:
            block = got_ref[pl.ds(start, length)].astype(jnp.float32)
            return block[:rows], block[rows : 2 * rows]
        return got_ref[pl.ds(start, rows)], got_ref[pl.ds(start + rows, rows)]

    def read_label(w):
        start = message_at(w, 0, wide_count, near_count, length)
        if length % 16 == 0:
            label = got_ref[pl.ds(start, length)].astype(jnp.float32)[2 * rows :]
        else:
            label = got_ref[pl.ds(start + 2 * rows, length - 2 * rows)].astype(jnp.float32)
        return jnp.max(label).astype(jnp.int32)

    def keep(w, label, found):
        live = jnp.minimum(label, 1)
        at = jnp.where(label > 0, jnp.minimum(found, recv_count), recv_count)
        code = jnp.maximum(label - 1, 0)
        column[at] = lax.div(code, own_count)
        spot = pl.ds(pl.multiple_of(lax.rem(code, own_count) * width, width), width)
        parts = [message(w, z) for z in range(near_count)]
        for side in range(2):
            order = parts if side == 0 else parts[::-1]
            half = jnp.concatenate([part[side] for part in order], axis=0).astype(tiles.dtype)
            start = at * width + (near_at if side == 0 else far_at)
            tiles[pl.ds(pl.multiple_of(start, half_size), half_size), spot] = half
        return found + live

    if wide_count <= UNROLL:
        labels = [read_label(w) for w in range(wide_count)]
        found = jnp.int32(0)
        for w in range(wide_count):
            found = keep(w, labels[w], found)
    else:

        def note(w, _):
            seen[w] = read_label(w)
            return 0

        lax.fori_loop(0, wide_count, note, 0)
        lax.fori_loop(0, wide_count, lambda w, found: keep(w, seen[w], found), jnp.int32(0))
    total = None
    for first in range(0, recv_count, GROUP):
        last = min(first + GROUP, recv_count)
        spots = [pl.multiple_of(column[u] * width, width) for u in range(first, last)]
        picked = jnp.concatenate([amp_ref[:, pl.ds(spot, width)] for spot in spots], axis=1)
        term = jnp.dot(
            picked, tiles[first * width : last * width], preferred_element_type=jnp.float32
        )
        total = term if total is None else total + term
    out_ref[...] = total


def shards(amplitudes, integrals, in_tile, counts, out_tile, owner_map):
    slot_count, rows, width = integrals.shape
    row_count = amplitudes.shape[0]
    wide_count = lax.axis_size("wide")
    depth_count = lax.axis_size("narrow")
    own_count = owner_map.shape[0] // wide_count
    recv_count = slot_count // 2
    near_count = depth_count // 2
    kind = integrals.dtype
    message_count = wide_count * near_count
    length = 2 * rows + PAIR
    if wide_count > UNROLL or length % PAIR != 0 or message_count * length % 16 != 0:
        length = -(-length // 16) * 16
    hbm = pl.BlockSpec(memory_space=pltpu.HBM)
    vmem = pl.BlockSpec(memory_space=pltpu.VMEM)
    limit = pltpu.CompilerParams(vmem_limit_bytes=32 * 2**20)
    across = [(z, depth_count - 1 - z) for z in range(depth_count)]
    far = lax.ppermute(integrals, "narrow", across)
    given = [in_tile, counts, out_tile, owner_map, integrals]
    given = [
        value if value.size == 1 else pltpu.with_memory_space_constraint(value, pltpu.HBM)
        for value in given
    ]
    ordered, sent = wide_count * rows, slot_count * rows
    order, labels, near = pl.pallas_call(
        functools.partial(route_kernel, own_count, wide_count),
        out_shape=[
            jax.ShapeDtypeStruct((ordered, sent), kind),
            jax.ShapeDtypeStruct((wide_count, width), kind),
            jax.ShapeDtypeStruct(integrals.shape, kind),
        ],
        in_specs=[hbm] * len(given),
        out_specs=[vmem] * 3,
        scratch_shapes=[pltpu.SMEM(value.shape, value.dtype) for value in given[:-1]]
        + [pltpu.SemaphoreType.DMA((len(given),))],
        compiler_params=limit,
        cost_estimate=pl.CostEstimate(flops=2**30, bytes_accessed=2**20, transcendentals=0),
        name="route",
    )(*given)
    send = pl.pallas_call(
        functools.partial(pack_kernel, wide_count, near_count),
        out_shape=jax.ShapeDtypeStruct((message_count * length, width), kind),
        in_specs=[vmem] * 4,
        out_specs=vmem,
        scratch_shapes=[
            pltpu.VMEM((sent, 2 * width), kind),
            pltpu.VMEM((ordered, 2 * width), jnp.float32),
        ],
        compiler_params=limit,
        name="pack",
    )(order, labels, near, far)
    places = group_places(wide_count, near_count)
    groups = [
        [w * depth_count + half * near_count + z for w, z in places] for half in range(2)
    ]
    got = lax.all_to_all(
        send.reshape(message_count, length // PAIR, PAIR, width),
        ("wide", "narrow"),
        split_axis=0,
        concat_axis=0,
        tiled=True,
        axis_index_groups=groups,
    ).reshape(message_count * length, width)
    return pl.pallas_call(
        functools.partial(ladder_kernel, rows, near_count, own_count, recv_count),
        out_shape=jax.ShapeDtypeStruct((row_count, own_count * width), jnp.float32),
        in_specs=[vmem] * 2,
        out_specs=vmem,
        scratch_shapes=[
            pltpu.VMEM(((recv_count + 1) * width, own_count * width), kind),
            pltpu.SMEM((recv_count + 1,), jnp.int32),
            pltpu.SMEM((wide_count,), jnp.int32),
        ],
        compiler_params=limit,
        name="ladder",
    )(amplitudes, got)


def solution(mesh):
    return jax.shard_map(
        shards,
        mesh=mesh,
        in_specs=(
            P("narrow", None),
            P("wide", "narrow", None),
            P("wide"),
            P("wide"),
            P("wide"),
            P(),
        ),
        out_specs=P("narrow", "wide"),
        check_vma=False,
    )
```

```python
import functools

import jax
import jax.numpy as jnp
from jax import lax
from jax.experimental import pallas as pl
from jax.experimental.pallas import tpu as pltpu
from jax.sharding import PartitionSpec as P

PAIR = 2
GROUP = 4
UNROLL = 8
CORES = 2


def each(count, body, start):
    if count > UNROLL:
        return lax.fori_loop(0, count, body, start)
    for i in range(count):
        start = body(i, start)
    return start


def chip_order(wide_count):
    chip_count = wide_count // CORES
    if wide_count > UNROLL:
        return list(range(chip_count))
    size = 2 ** (chip_count - 1).bit_length()
    ring = [step ^ (step >> 1) for step in range(1, size)]
    return [chip for chip in ring if chip < chip_count] + [0]


def group_places(wide_count, near_count):
    cores = range(CORES)
    depths = range(near_count)
    return [(chip * CORES + core, z) for chip in chip_order(wide_count) for core in cores for z in depths]


def message_at(w, z, wide_count, near_count, length):
    if isinstance(w, int):
        return group_places(wide_count, near_count).index((w, z)) * length
    place = w * near_count + z
    return pl.multiple_of(place * length, length)


def route_kernel(own_count, wide_count, *refs):
    sources, (order_ref, label_ref, near_ref), targets, sems = refs[:5], refs[5:8], refs[8:12], refs[12]
    in_tile, counts, out_tile, owner_map = targets
    copies = [
        pltpu.make_async_copy(source, target, sems.at[i])
        for i, (source, target) in enumerate(zip(sources, (*targets, near_ref)))
    ]
    for copy in copies:
        copy.start()
    for copy in copies[:4]:
        copy.wait()
    slot_count, rows, width = near_ref.shape
    column = lax.broadcasted_iota(jnp.int32, (1, slot_count * rows), 1)
    owners = lax.broadcasted_iota(jnp.int32, (wide_count, width), 0)

    def route(h, carry):
        owner_of, labels = carry
        spot = owner_map[out_tile[h]]
        owner = lax.div(spot, own_count)
        label = in_tile[h] * own_count + lax.rem(spot, own_count) + 1
        label = jnp.where(h < counts[0], label, 0)
        owner_of = jnp.where(lax.div(column, rows) == h, owner, owner_of)
        return owner_of, jnp.where(owners == owner, label, labels)

    start = (jnp.zeros_like(column), jnp.zeros((wide_count, width), jnp.int32))
    owner_of, labels = each(slot_count, route, start)
    label_ref[...] = labels.astype(jnp.float32).astype(label_ref.dtype)
    row = lax.broadcasted_iota(jnp.int32, (wide_count * rows, 1), 0)
    hit = row == owner_of * rows + lax.rem(column, rows)
    order_ref[...] = hit.astype(jnp.float32).astype(order_ref.dtype)
    copies[4].wait()


def pack_kernel(wide_count, near_count, order_ref, label_ref, near_ref, far_ref, send_ref, both, ordered):
    slot_count, rows, width = near_ref.shape
    length = send_ref.shape[0] // (wide_count * near_count)
    for side, ref in enumerate((near_ref, far_ref)):
        block = ref[...]
        if rows % 16 != 0:
            block = block.astype(jnp.float32)
        block = block.reshape(slot_count * rows, width).astype(both.dtype)
        both[:, side * width : (side + 1) * width] = block
    ordered[...] = jnp.dot(order_ref[...], both[...], preferred_element_type=jnp.float32)
    labels = label_ref[...].astype(jnp.float32)
    ids = lax.broadcasted_iota(jnp.int32, labels.shape, 0)

    def write(owner, _):
        spot = owner * rows
        if not isinstance(owner, int):
            spot = pl.multiple_of(spot, rows)
        near = ordered[pl.ds(spot, rows), :width]
        far = ordered[pl.ds(spot, rows), width:]
        label = jnp.sum(jnp.where(ids == owner, labels, 0.0), axis=0, keepdims=True)
        label = jnp.broadcast_to(label, (length - 2 * rows, width))
        if length % 16 == 0:
            pieces = [(0, jnp.concatenate([near, far, label], axis=0))]
        else:
            pieces = [(0, near), (rows, far), (2 * rows, label)]
        for z in range(near_count):
            start = message_at(owner, z, wide_count, near_count, length)
            for offset, piece in pieces:
                send_ref[pl.ds(start + offset, piece.shape[0])] = piece.astype(send_ref.dtype)
        return 0

    each(wide_count, write, 0)


def ladder_kernel(
    rows, near_count, own_count, recv_count, amp_ref, got_ref, out_ref, tiles, column, seen
):
    wide_count = seen.shape[0]
    width = got_ref.shape[1]
    length = got_ref.shape[0] // (wide_count * near_count)
    half_size = near_count * rows
    upper = (lax.axis_index("narrow") >= near_count).astype(jnp.int32)
    near_at, far_at = upper * half_size, (1 - upper) * half_size
    tiles[...] = jnp.zeros_like(tiles)
    for u in range(recv_count):
        column[u] = 0

    def message(w, z):
        start = message_at(w, z, wide_count, near_count, length)
        if length % 16 == 0:
            block = got_ref[pl.ds(start, length)].astype(jnp.float32)
            return block[:rows], block[rows : 2 * rows]
        return got_ref[pl.ds(start, rows)], got_ref[pl.ds(start + rows, rows)]

    def read_label(w):
        start = message_at(w, 0, wide_count, near_count, length)
        if length % 16 == 0:
            label = got_ref[pl.ds(start, length)].astype(jnp.float32)[2 * rows :]
        else:
            label = got_ref[pl.ds(start + 2 * rows, length - 2 * rows)].astype(jnp.float32)
        return jnp.max(label).astype(jnp.int32)

    def keep(w, label, found):
        live = jnp.minimum(label, 1)
        at = jnp.where(label > 0, jnp.minimum(found, recv_count), recv_count)
        code = jnp.maximum(label - 1, 0)
        column[at] = lax.div(code, own_count)
        spot = pl.ds(pl.multiple_of(lax.rem(code, own_count) * width, width), width)
        parts = [message(w, z) for z in range(near_count)]
        for side in range(2):
            order = parts if side == 0 else parts[::-1]
            half = jnp.concatenate([part[side] for part in order], axis=0).astype(tiles.dtype)
            start = at * width + (near_at if side == 0 else far_at)
            tiles[pl.ds(pl.multiple_of(start, half_size), half_size), spot] = half
        return found + live

    if wide_count <= UNROLL:
        labels = [read_label(w) for w in range(wide_count)]
        found = jnp.int32(0)
        for w in range(wide_count):
            found = keep(w, labels[w], found)
    else:

        def note(w, _):
            seen[w] = read_label(w)
            return 0

        lax.fori_loop(0, wide_count, note, 0)
        lax.fori_loop(0, wide_count, lambda w, found: keep(w, seen[w], found), jnp.int32(0))
    total = None
    for first in range(0, recv_count, GROUP):
        last = min(first + GROUP, recv_count)
        spots = [pl.multiple_of(column[u] * width, width) for u in range(first, last)]
        picked = jnp.concatenate([amp_ref[:, pl.ds(spot, width)] for spot in spots], axis=1)
        term = jnp.dot(
            picked, tiles[first * width : last * width], preferred_element_type=jnp.float32
        )
        total = term if total is None else total + term
    out_ref[...] = total


def shards(amplitudes, integrals, in_tile, counts, out_tile, owner_map):
    slot_count, rows, width = integrals.shape
    row_count = amplitudes.shape[0]
    wide_count = lax.axis_size("wide")
    depth_count = lax.axis_size("narrow")
    own_count = owner_map.shape[0] // wide_count
    recv_count = slot_count // 2
    near_count = depth_count // 2
    kind = integrals.dtype
    message_count = wide_count * near_count
    length = 2 * rows + PAIR
    if wide_count > UNROLL or length % PAIR != 0 or message_count * length % 16 != 0:
        length = -(-length // 16) * 16
    hbm = pl.BlockSpec(memory_space=pltpu.HBM)
    vmem = pl.BlockSpec(memory_space=pltpu.VMEM)
    limit = pltpu.CompilerParams(vmem_limit_bytes=32 * 2**20)
    across = [(z, depth_count - 1 - z) for z in range(depth_count)]
    far = lax.ppermute(integrals, "narrow", across)
    given = [in_tile, counts, out_tile, owner_map, integrals]
    given = [
        value if value.size == 1 else pltpu.with_memory_space_constraint(value, pltpu.HBM)
        for value in given
    ]
    ordered, sent = wide_count * rows, slot_count * rows
    order, labels, near = pl.pallas_call(
        functools.partial(route_kernel, own_count, wide_count),
        out_shape=[
            jax.ShapeDtypeStruct((ordered, sent), kind),
            jax.ShapeDtypeStruct((wide_count, width), kind),
            jax.ShapeDtypeStruct(integrals.shape, kind),
        ],
        in_specs=[hbm] * len(given),
        out_specs=[vmem] * 3,
        scratch_shapes=[pltpu.SMEM(value.shape, value.dtype) for value in given[:-1]]
        + [pltpu.SemaphoreType.DMA((len(given),))],
        compiler_params=limit,
        cost_estimate=pl.CostEstimate(flops=2**30, bytes_accessed=2**20, transcendentals=0),
        name="route",
    )(*given)
    send = pl.pallas_call(
        functools.partial(pack_kernel, wide_count, near_count),
        out_shape=jax.ShapeDtypeStruct((message_count * length, width), kind),
        in_specs=[vmem] * 4,
        out_specs=vmem,
        scratch_shapes=[
            pltpu.VMEM((sent, 2 * width), kind),
            pltpu.VMEM((ordered, 2 * width), jnp.float32),
        ],
        compiler_params=limit,
        name="pack",
    )(order, labels, near, far)
    places = group_places(wide_count, near_count)
    groups = [
        [w * depth_count + half * near_count + z for w, z in places] for half in range(2)
    ]
    got = lax.all_to_all(
        send.reshape(message_count, length // PAIR, PAIR, width),
        ("wide", "narrow"),
        split_axis=0,
        concat_axis=0,
        tiled=True,
        axis_index_groups=groups,
    ).reshape(message_count * length, width)
    return pl.pallas_call(
        functools.partial(ladder_kernel, rows, near_count, own_count, recv_count),
        out_shape=jax.ShapeDtypeStruct((row_count, own_count * width), jnp.float32),
        in_specs=[vmem] * 2,
        out_specs=vmem,
        scratch_shapes=[
            pltpu.VMEM(((recv_count + 1) * width, own_count * width), kind),
            pltpu.SMEM((recv_count + 1,), jnp.int32),
            pltpu.SMEM((wide_count,), jnp.int32),
        ],
        compiler_params=limit,
        name="ladder",
    )(amplitudes, got)


def solution(mesh):
    return jax.shard_map(
        shards,
        mesh=mesh,
        in_specs=(
            P("narrow", None),
            P("wide", "narrow", None),
            P("wide"),
            P("wide"),
            P("wide"),
            P(),
        ),
        out_specs=P("narrow", "wide"),
        check_vma=False,
    )
```

```python
import functools

import jax
import jax.numpy as jnp
from jax import lax
from jax.experimental import pallas as pl
from jax.experimental.pallas import tpu as pltpu
from jax.sharding import PartitionSpec as P

PAIR = 2
GROUP = 4
UNROLL = 8
CORES = 2


def each(count, body, start):
    if count > UNROLL:
        return lax.fori_loop(0, count, body, start)
    for i in range(count):
        start = body(i, start)
    return start


def chip_order(wide_count):
    chip_count = wide_count // CORES
    if wide_count > UNROLL:
        return list(range(chip_count))
    bits = (chip_count - 1).bit_length()
    flipped = [int(format(chip, "b").zfill(bits)[::-1], 2) for chip in range(2**bits)]
    return [chip for chip in flipped[1:] if chip < chip_count] + [0]


def group_places(wide_count, near_count):
    cores = range(CORES)
    depths = range(near_count)
    return [(chip * CORES + core, z) for chip in chip_order(wide_count) for core in cores for z in depths]


def message_at(w, z, wide_count, near_count, length):
    if isinstance(w, int):
        return group_places(wide_count, near_count).index((w, z)) * length
    place = w * near_count + z
    return pl.multiple_of(place * length, length)


def route_kernel(own_count, wide_count, *refs):
    sources, (order_ref, label_ref, near_ref), targets, sems = refs[:5], refs[5:8], refs[8:12], refs[12]
    in_tile, counts, out_tile, owner_map = targets
    copies = [
        pltpu.make_async_copy(source, target, sems.at[i])
        for i, (source, target) in enumerate(zip(sources, (*targets, near_ref)))
    ]
    for copy in copies:
        copy.start()
    for copy in copies[:4]:
        copy.wait()
    slot_count, rows, width = near_ref.shape
    column = lax.broadcasted_iota(jnp.int32, (1, slot_count * rows), 1)
    owners = lax.broadcasted_iota(jnp.int32, (wide_count, width), 0)

    def route(h, carry):
        owner_of, labels = carry
        spot = owner_map[out_tile[h]]
        owner = lax.div(spot, own_count)
        label = in_tile[h] * own_count + lax.rem(spot, own_count) + 1
        label = jnp.where(h < counts[0], label, 0)
        owner_of = jnp.where(lax.div(column, rows) == h, owner, owner_of)
        return owner_of, jnp.where(owners == owner, label, labels)

    start = (jnp.zeros_like(column), jnp.zeros((wide_count, width), jnp.int32))
    owner_of, labels = each(slot_count, route, start)
    label_ref[...] = labels.astype(jnp.float32).astype(label_ref.dtype)
    row = lax.broadcasted_iota(jnp.int32, (wide_count * rows, 1), 0)
    hit = row == owner_of * rows + lax.rem(column, rows)
    order_ref[...] = hit.astype(jnp.float32).astype(order_ref.dtype)
    copies[4].wait()


def pack_kernel(wide_count, near_count, order_ref, label_ref, near_ref, far_ref, send_ref, both, ordered):
    slot_count, rows, width = near_ref.shape
    length = send_ref.shape[0] // (wide_count * near_count)
    for side, ref in enumerate((near_ref, far_ref)):
        block = ref[...]
        if rows % 16 != 0:
            block = block.astype(jnp.float32)
        block = block.reshape(slot_count * rows, width).astype(both.dtype)
        both[:, side * width : (side + 1) * width] = block
    ordered[...] = jnp.dot(order_ref[...], both[...], preferred_element_type=jnp.float32)
    labels = label_ref[...].astype(jnp.float32)
    ids = lax.broadcasted_iota(jnp.int32, labels.shape, 0)

    def write(owner, _):
        spot = owner * rows
        if not isinstance(owner, int):
            spot = pl.multiple_of(spot, rows)
        near = ordered[pl.ds(spot, rows), :width]
        far = ordered[pl.ds(spot, rows), width:]
        label = jnp.sum(jnp.where(ids == owner, labels, 0.0), axis=0, keepdims=True)
        label = jnp.broadcast_to(label, (length - 2 * rows, width))
        if length % 16 == 0:
            pieces = [(0, jnp.concatenate([near, far, label], axis=0))]
        else:
            pieces = [(0, near), (rows, far), (2 * rows, label)]
        for z in range(near_count):
            start = message_at(owner, z, wide_count, near_count, length)
            for offset, piece in pieces:
                send_ref[pl.ds(start + offset, piece.shape[0])] = piece.astype(send_ref.dtype)
        return 0

    each(wide_count, write, 0)


def ladder_kernel(
    rows, near_count, own_count, recv_count, amp_ref, got_ref, out_ref, tiles, column, seen
):
    wide_count = seen.shape[0]
    width = got_ref.shape[1]
    length = got_ref.shape[0] // (wide_count * near_count)
    half_size = near_count * rows
    upper = (lax.axis_index("narrow") >= near_count).astype(jnp.int32)
    near_at, far_at = upper * half_size, (1 - upper) * half_size
    tiles[...] = jnp.zeros_like(tiles)
    for u in range(recv_count):
        column[u] = 0

    def message(w, z):
        start = message_at(w, z, wide_count, near_count, length)
        if length % 16 == 0:
            block = got_ref[pl.ds(start, length)].astype(jnp.float32)
            return block[:rows], block[rows : 2 * rows]
        return got_ref[pl.ds(start, rows)], got_ref[pl.ds(start + rows, rows)]

    def read_label(w):
        start = message_at(w, 0, wide_count, near_count, length)
        if length % 16 == 0:
            label = got_ref[pl.ds(start, length)].astype(jnp.float32)[2 * rows :]
        else:
            label = got_ref[pl.ds(start + 2 * rows, length - 2 * rows)].astype(jnp.float32)
        return label[0, 0].astype(jnp.int32)

    def keep(w, label, found):
        live = jnp.minimum(label, 1)
        at = jnp.where(label > 0, jnp.minimum(found, recv_count), recv_count)
        code = jnp.maximum(label - 1, 0)
        column[at] = lax.div(code, own_count)
        spot = pl.ds(pl.multiple_of(lax.rem(code, own_count) * width, width), width)
        parts = [message(w, z) for z in range(near_count)]
        for side in range(2):
            order = parts if side == 0 else parts[::-1]
            half = jnp.concatenate([part[side] for part in order], axis=0).astype(tiles.dtype)
            start = at * width + (near_at if side == 0 else far_at)
            tiles[pl.ds(pl.multiple_of(start, half_size), half_size), spot] = half
        return found + live

    if wide_count <= UNROLL:
        labels = [read_label(w) for w in range(wide_count)]
        found = jnp.int32(0)
        for w in range(wide_count):
            found = keep(w, labels[w], found)
    else:

        def note(w, _):
            seen[w] = read_label(w)
            return 0

        lax.fori_loop(0, wide_count, note, 0)
        lax.fori_loop(0, wide_count, lambda w, found: keep(w, seen[w], found), jnp.int32(0))
    total = None
    for first in range(0, recv_count, GROUP):
        last = min(first + GROUP, recv_count)
        spots = [pl.multiple_of(column[u] * width, width) for u in range(first, last)]
        picked = jnp.concatenate([amp_ref[:, pl.ds(spot, width)] for spot in spots], axis=1)
        term = jnp.dot(
            picked, tiles[first * width : last * width], preferred_element_type=jnp.float32
        )
        total = term if total is None else total + term
    out_ref[...] = total


def shards(amplitudes, integrals, in_tile, counts, out_tile, owner_map):
    slot_count, rows, width = integrals.shape
    row_count = amplitudes.shape[0]
    wide_count = lax.axis_size("wide")
    depth_count = lax.axis_size("narrow")
    own_count = owner_map.shape[0] // wide_count
    recv_count = slot_count // 2
    near_count = depth_count // 2
    kind = integrals.dtype
    message_count = wide_count * near_count
    length = 2 * rows + PAIR
    if wide_count > UNROLL or length % PAIR != 0 or message_count * length % 16 != 0:
        length = -(-length // 16) * 16
    hbm = pl.BlockSpec(memory_space=pltpu.HBM)
    vmem = pl.BlockSpec(memory_space=pltpu.VMEM)
    limit = pltpu.CompilerParams(vmem_limit_bytes=32 * 2**20)
    across = [(z, depth_count - 1 - z) for z in range(depth_count)]
    far = lax.ppermute(integrals, "narrow", across)
    given = [in_tile, counts, out_tile, owner_map, integrals]
    given = [
        value if value.size == 1 else pltpu.with_memory_space_constraint(value, pltpu.HBM)
        for value in given
    ]
    ordered, sent = wide_count * rows, slot_count * rows
    order, labels, near = pl.pallas_call(
        functools.partial(route_kernel, own_count, wide_count),
        out_shape=[
            jax.ShapeDtypeStruct((ordered, sent), kind),
            jax.ShapeDtypeStruct((wide_count, width), kind),
            jax.ShapeDtypeStruct(integrals.shape, kind),
        ],
        in_specs=[hbm] * len(given),
        out_specs=[vmem] * 3,
        scratch_shapes=[pltpu.SMEM(value.shape, value.dtype) for value in given[:-1]]
        + [pltpu.SemaphoreType.DMA((len(given),))],
        compiler_params=limit,
        cost_estimate=pl.CostEstimate(flops=2**30, bytes_accessed=2**20, transcendentals=0),
        name="route",
    )(*given)
    send = pl.pallas_call(
        functools.partial(pack_kernel, wide_count, near_count),
        out_shape=jax.ShapeDtypeStruct((message_count * length, width), kind),
        in_specs=[vmem] * 4,
        out_specs=vmem,
        scratch_shapes=[
            pltpu.VMEM((sent, 2 * width), kind),
            pltpu.VMEM((ordered, 2 * width), jnp.float32),
        ],
        compiler_params=limit,
        name="pack",
    )(order, labels, near, far)
    places = group_places(wide_count, near_count)
    groups = [
        [w * depth_count + half * near_count + z for w, z in places] for half in range(2)
    ]
    got = lax.all_to_all(
        send.reshape(message_count, length // PAIR, PAIR, width),
        ("wide", "narrow"),
        split_axis=0,
        concat_axis=0,
        tiled=True,
        axis_index_groups=groups,
    ).reshape(message_count * length, width)
    return pl.pallas_call(
        functools.partial(ladder_kernel, rows, near_count, own_count, recv_count),
        out_shape=jax.ShapeDtypeStruct((row_count, own_count * width), jnp.float32),
        in_specs=[vmem] * 2,
        out_specs=vmem,
        scratch_shapes=[
            pltpu.VMEM(((recv_count + 1) * width, own_count * width), kind),
            pltpu.SMEM((recv_count + 1,), jnp.int32),
            pltpu.SMEM((wide_count,), jnp.int32),
        ],
        compiler_params=limit,
        name="ladder",
    )(amplitudes, got)


def solution(mesh):
    return jax.shard_map(
        shards,
        mesh=mesh,
        in_specs=(
            P("narrow", None),
            P("wide", "narrow", None),
            P("wide"),
            P("wide"),
            P("wide"),
            P(),
        ),
        out_specs=P("narrow", "wide"),
        check_vma=False,
    )
```

```python
import functools

import jax
import jax.numpy as jnp
from jax import lax
from jax.experimental import pallas as pl
from jax.experimental.pallas import tpu as pltpu
from jax.sharding import PartitionSpec as P

PAIR = 2
GROUP = 4
UNROLL = 8
CORES = 2


def each(count, body, start):
    if count > UNROLL:
        return lax.fori_loop(0, count, body, start)
    for i in range(count):
        start = body(i, start)
    return start


def chip_order(wide_count):
    chip_count = wide_count // CORES
    if wide_count > UNROLL:
        return list(range(chip_count))
    bits = (chip_count - 1).bit_length()
    flipped = [int(format(chip, "b").zfill(bits)[::-1], 2) for chip in range(2**bits)]
    return [chip for chip in flipped[1:] if chip < chip_count] + [0]


def group_places(wide_count, near_count):
    cores = range(CORES)
    depths = reversed(range(near_count))
    return [(chip * CORES + core, z) for z in depths for chip in chip_order(wide_count) for core in cores]


def message_at(w, z, wide_count, near_count, length):
    if isinstance(w, int):
        return group_places(wide_count, near_count).index((w, z)) * length
    place = (near_count - 1 - z) * wide_count + w
    return pl.multiple_of(place * length, length)


def route_kernel(own_count, wide_count, *refs):
    sources, (order_ref, label_ref, near_ref), targets, sems = refs[:5], refs[5:8], refs[8:12], refs[12]
    in_tile, counts, out_tile, owner_map = targets
    copies = [
        pltpu.make_async_copy(source, target, sems.at[i])
        for i, (source, target) in enumerate(zip(sources, (*targets, near_ref)))
    ]
    for copy in copies:
        copy.start()
    for copy in copies[:4]:
        copy.wait()
    slot_count, rows, width = near_ref.shape
    column = lax.broadcasted_iota(jnp.int32, (1, slot_count * rows), 1)
    owners = lax.broadcasted_iota(jnp.int32, (wide_count, width), 0)

    def route(h, carry):
        owner_of, labels = carry
        spot = owner_map[out_tile[h]]
        owner = lax.div(spot, own_count)
        label = in_tile[h] * own_count + lax.rem(spot, own_count) + 1
        label = jnp.where(h < counts[0], label, 0)
        owner_of = jnp.where(lax.div(column, rows) == h, owner, owner_of)
        return owner_of, jnp.where(owners == owner, label, labels)

    start = (jnp.zeros_like(column), jnp.zeros((wide_count, width), jnp.int32))
    owner_of, labels = each(slot_count, route, start)
    label_ref[...] = labels.astype(jnp.float32).astype(label_ref.dtype)
    row = lax.broadcasted_iota(jnp.int32, (wide_count * rows, 1), 0)
    hit = row == owner_of * rows + lax.rem(column, rows)
    order_ref[...] = hit.astype(jnp.float32).astype(order_ref.dtype)
    copies[4].wait()


def pack_kernel(wide_count, near_count, order_ref, label_ref, near_ref, far_ref, send_ref, both, ordered):
    slot_count, rows, width = near_ref.shape
    length = send_ref.shape[0] // (wide_count * near_count)
    for side, ref in enumerate((near_ref, far_ref)):
        block = ref[...]
        if rows % 16 != 0:
            block = block.astype(jnp.float32)
        block = block.reshape(slot_count * rows, width).astype(both.dtype)
        both[:, side * width : (side + 1) * width] = block
    ordered[...] = jnp.dot(order_ref[...], both[...], preferred_element_type=jnp.float32)
    labels = label_ref[...].astype(jnp.float32)
    ids = lax.broadcasted_iota(jnp.int32, labels.shape, 0)

    def write(owner, _):
        spot = owner * rows
        if not isinstance(owner, int):
            spot = pl.multiple_of(spot, rows)
        near = ordered[pl.ds(spot, rows), :width]
        far = ordered[pl.ds(spot, rows), width:]
        label = jnp.sum(jnp.where(ids == owner, labels, 0.0), axis=0, keepdims=True)
        label = jnp.broadcast_to(label, (length - 2 * rows, width))
        if length % 16 == 0:
            pieces = [(0, jnp.concatenate([near, far, label], axis=0))]
        else:
            pieces = [(0, near), (rows, far), (2 * rows, label)]
        for z in range(near_count):
            start = message_at(owner, z, wide_count, near_count, length)
            for offset, piece in pieces:
                send_ref[pl.ds(start + offset, piece.shape[0])] = piece.astype(send_ref.dtype)
        return 0

    each(wide_count, write, 0)


def ladder_kernel(
    rows, near_count, own_count, recv_count, amp_ref, got_ref, out_ref, tiles, column, seen
):
    wide_count = seen.shape[0]
    width = got_ref.shape[1]
    length = got_ref.shape[0] // (wide_count * near_count)
    half_size = near_count * rows
    upper = (lax.axis_index("narrow") >= near_count).astype(jnp.int32)
    near_at, far_at = upper * half_size, (1 - upper) * half_size
    tiles[...] = jnp.zeros_like(tiles)
    for u in range(recv_count):
        column[u] = 0

    def message(w, z):
        start = message_at(w, z, wide_count, near_count, length)
        if length % 16 == 0:
            block = got_ref[pl.ds(start, length)].astype(jnp.float32)
            return block[:rows], block[rows : 2 * rows]
        return got_ref[pl.ds(start, rows)], got_ref[pl.ds(start + rows, rows)]

    def read_label(w):
        start = message_at(w, 0, wide_count, near_count, length)
        if length % 16 == 0:
            label = got_ref[pl.ds(start, length)].astype(jnp.float32)[2 * rows :]
        else:
            label = got_ref[pl.ds(start + 2 * rows, length - 2 * rows)].astype(jnp.float32)
        return label[0, 0].astype(jnp.int32)

    def keep(w, label, found):
        live = jnp.minimum(label, 1)
        at = jnp.where(label > 0, jnp.minimum(found, recv_count), recv_count)
        code = jnp.maximum(label - 1, 0)
        column[at] = lax.div(code, own_count)
        spot = pl.ds(pl.multiple_of(lax.rem(code, own_count) * width, width), width)
        parts = [message(w, z) for z in range(near_count)]
        for side in range(2):
            order = parts if side == 0 else parts[::-1]
            half = jnp.concatenate([part[side] for part in order], axis=0).astype(tiles.dtype)
            start = at * width + (near_at if side == 0 else far_at)
            tiles[pl.ds(pl.multiple_of(start, half_size), half_size), spot] = half
        return found + live

    if wide_count <= UNROLL:
        labels = [read_label(w) for w in range(wide_count)]
        found = jnp.int32(0)
        for w in range(wide_count):
            found = keep(w, labels[w], found)
    else:

        def note(w, _):
            seen[w] = read_label(w)
            return 0

        lax.fori_loop(0, wide_count, note, 0)
        lax.fori_loop(0, wide_count, lambda w, found: keep(w, seen[w], found), jnp.int32(0))
    total = None
    for first in range(0, recv_count, GROUP):
        last = min(first + GROUP, recv_count)
        spots = [pl.multiple_of(column[u] * width, width) for u in range(first, last)]
        picked = jnp.concatenate([amp_ref[:, pl.ds(spot, width)] for spot in spots], axis=1)
        term = jnp.dot(
            picked, tiles[first * width : last * width], preferred_element_type=jnp.float32
        )
        total = term if total is None else total + term
    out_ref[...] = total


def shards(amplitudes, integrals, in_tile, counts, out_tile, owner_map):
    slot_count, rows, width = integrals.shape
    row_count = amplitudes.shape[0]
    wide_count = lax.axis_size("wide")
    depth_count = lax.axis_size("narrow")
    own_count = owner_map.shape[0] // wide_count
    recv_count = slot_count // 2
    near_count = depth_count // 2
    kind = integrals.dtype
    message_count = wide_count * near_count
    length = 2 * rows + PAIR
    if wide_count > UNROLL or length % PAIR != 0 or message_count * length % 16 != 0:
        length = -(-length // 16) * 16
    hbm = pl.BlockSpec(memory_space=pltpu.HBM)
    vmem = pl.BlockSpec(memory_space=pltpu.VMEM)
    limit = pltpu.CompilerParams(vmem_limit_bytes=32 * 2**20)
    across = [(z, depth_count - 1 - z) for z in range(depth_count)]
    far = lax.ppermute(integrals, "narrow", across)
    given = [in_tile, counts, out_tile, owner_map, integrals]
    given = [
        value if value.size == 1 else pltpu.with_memory_space_constraint(value, pltpu.HBM)
        for value in given
    ]
    ordered, sent = wide_count * rows, slot_count * rows
    order, labels, near = pl.pallas_call(
        functools.partial(route_kernel, own_count, wide_count),
        out_shape=[
            jax.ShapeDtypeStruct((ordered, sent), kind),
            jax.ShapeDtypeStruct((wide_count, width), kind),
            jax.ShapeDtypeStruct(integrals.shape, kind),
        ],
        in_specs=[hbm] * len(given),
        out_specs=[vmem] * 3,
        scratch_shapes=[pltpu.SMEM(value.shape, value.dtype) for value in given[:-1]]
        + [pltpu.SemaphoreType.DMA((len(given),))],
        compiler_params=limit,
        cost_estimate=pl.CostEstimate(flops=2**30, bytes_accessed=2**20, transcendentals=0),
        name="route",
    )(*given)
    send = pl.pallas_call(
        functools.partial(pack_kernel, wide_count, near_count),
        out_shape=jax.ShapeDtypeStruct((message_count * length, width), kind),
        in_specs=[vmem] * 4,
        out_specs=vmem,
        scratch_shapes=[
            pltpu.VMEM((sent, 2 * width), kind),
            pltpu.VMEM((ordered, 2 * width), jnp.float32),
        ],
        compiler_params=limit,
        name="pack",
    )(order, labels, near, far)
    places = group_places(wide_count, near_count)
    groups = [
        [w * depth_count + half * near_count + z for w, z in places] for half in range(2)
    ]
    got = lax.all_to_all(
        send.reshape(message_count, length // PAIR, PAIR, width),
        ("wide", "narrow"),
        split_axis=0,
        concat_axis=0,
        tiled=True,
        axis_index_groups=groups,
    ).reshape(message_count * length, width)
    return pl.pallas_call(
        functools.partial(ladder_kernel, rows, near_count, own_count, recv_count),
        out_shape=jax.ShapeDtypeStruct((row_count, own_count * width), jnp.float32),
        in_specs=[vmem] * 2,
        out_specs=vmem,
        scratch_shapes=[
            pltpu.VMEM(((recv_count + 1) * width, own_count * width), kind),
            pltpu.SMEM((recv_count + 1,), jnp.int32),
            pltpu.SMEM((wide_count,), jnp.int32),
        ],
        compiler_params=limit,
        name="ladder",
    )(amplitudes, got)


def solution(mesh):
    return jax.shard_map(
        shards,
        mesh=mesh,
        in_specs=(
            P("narrow", None),
            P("wide", "narrow", None),
            P("wide"),
            P("wide"),
            P("wide"),
            P(),
        ),
        out_specs=P("narrow", "wide"),
        check_vma=False,
    )
```

```python
import functools

import jax
import jax.numpy as jnp
from jax import lax
from jax.experimental import pallas as pl
from jax.experimental.pallas import tpu as pltpu
from jax.sharding import PartitionSpec as P

PAIR = 2
GROUP = 4
UNROLL = 8
CORES = 2


def each(count, body, start):
    if count > UNROLL:
        return lax.fori_loop(0, count, body, start)
    for i in range(count):
        start = body(i, start)
    return start


def chip_order(wide_count):
    chip_count = wide_count // CORES
    if wide_count > UNROLL:
        return list(range(chip_count))
    first = chip_count // 2
    return [first] + [chip for chip in range(chip_count) if chip != first]


def group_places(wide_count, near_count):
    cores = range(CORES)
    depths = reversed(range(near_count))
    return [(chip * CORES + core, z) for z in depths for chip in chip_order(wide_count) for core in cores]


def message_at(w, z, wide_count, near_count, length):
    if isinstance(w, int):
        return group_places(wide_count, near_count).index((w, z)) * length
    place = (near_count - 1 - z) * wide_count + w
    return pl.multiple_of(place * length, length)


def route_kernel(own_count, wide_count, *refs):
    sources, (order_ref, label_ref, near_ref), targets, sems = refs[:5], refs[5:8], refs[8:12], refs[12]
    in_tile, counts, out_tile, owner_map = targets
    copies = [
        pltpu.make_async_copy(source, target, sems.at[i])
        for i, (source, target) in enumerate(zip(sources, (*targets, near_ref)))
    ]
    for copy in copies:
        copy.start()
    for copy in copies[:4]:
        copy.wait()
    slot_count, rows, width = near_ref.shape
    column = lax.broadcasted_iota(jnp.int32, (1, slot_count * rows), 1)
    owners = lax.broadcasted_iota(jnp.int32, (wide_count, width), 0)

    def route(h, carry):
        owner_of, labels = carry
        spot = owner_map[out_tile[h]]
        owner = lax.div(spot, own_count)
        label = in_tile[h] * own_count + lax.rem(spot, own_count) + 1
        label = jnp.where(h < counts[0], label, 0)
        owner_of = jnp.where(lax.div(column, rows) == h, owner, owner_of)
        return owner_of, jnp.where(owners == owner, label, labels)

    start = (jnp.zeros_like(column), jnp.zeros((wide_count, width), jnp.int32))
    owner_of, labels = each(slot_count, route, start)
    label_ref[...] = labels.astype(jnp.float32).astype(label_ref.dtype)
    row = lax.broadcasted_iota(jnp.int32, (wide_count * rows, 1), 0)
    hit = row == owner_of * rows + lax.rem(column, rows)
    order_ref[...] = hit.astype(jnp.float32).astype(order_ref.dtype)
    copies[4].wait()


def pack_kernel(wide_count, near_count, order_ref, label_ref, near_ref, far_ref, send_ref, both, ordered):
    slot_count, rows, width = near_ref.shape
    length = send_ref.shape[0] // (wide_count * near_count)
    for side, ref in enumerate((near_ref, far_ref)):
        block = ref[...]
        if rows % 16 != 0:
            block = block.astype(jnp.float32)
        block = block.reshape(slot_count * rows, width).astype(both.dtype)
        both[:, side * width : (side + 1) * width] = block
    ordered[...] = jnp.dot(order_ref[...], both[...], preferred_element_type=jnp.float32)
    labels = label_ref[...].astype(jnp.float32)
    ids = lax.broadcasted_iota(jnp.int32, labels.shape, 0)

    def write(owner, _):
        spot = owner * rows
        if not isinstance(owner, int):
            spot = pl.multiple_of(spot, rows)
        near = ordered[pl.ds(spot, rows), :width]
        far = ordered[pl.ds(spot, rows), width:]
        label = jnp.sum(jnp.where(ids == owner, labels, 0.0), axis=0, keepdims=True)
        label = jnp.broadcast_to(label, (length - 2 * rows, width))
        if length % 16 == 0:
            pieces = [(0, jnp.concatenate([near, far, label], axis=0))]
        else:
            pieces = [(0, near), (rows, far), (2 * rows, label)]
        for z in range(near_count):
            start = message_at(owner, z, wide_count, near_count, length)
            for offset, piece in pieces:
                send_ref[pl.ds(start + offset, piece.shape[0])] = piece.astype(send_ref.dtype)
        return 0

    each(wide_count, write, 0)


def ladder_kernel(
    rows, near_count, own_count, recv_count, amp_ref, got_ref, out_ref, tiles, column, seen
):
    wide_count = seen.shape[0]
    width = got_ref.shape[1]
    length = got_ref.shape[0] // (wide_count * near_count)
    half_size = near_count * rows
    upper = (lax.axis_index("narrow") >= near_count).astype(jnp.int32)
    near_at, far_at = upper * half_size, (1 - upper) * half_size
    tiles[...] = jnp.zeros_like(tiles)
    for u in range(recv_count):
        column[u] = 0

    def message(w, z):
        start = message_at(w, z, wide_count, near_count, length)
        if length % 16 == 0:
            block = got_ref[pl.ds(start, length)].astype(jnp.float32)
            return block[:rows], block[rows : 2 * rows]
        return got_ref[pl.ds(start, rows)], got_ref[pl.ds(start + rows, rows)]

    def read_label(w):
        start = message_at(w, 0, wide_count, near_count, length)
        if length % 16 == 0:
            label = got_ref[pl.ds(start, length)].astype(jnp.float32)[2 * rows :]
        else:
            label = got_ref[pl.ds(start + 2 * rows, length - 2 * rows)].astype(jnp.float32)
        return label[0, 0].astype(jnp.int32)

    def keep(w, label, found):
        live = jnp.minimum(label, 1)
        at = jnp.where(label > 0, jnp.minimum(found, recv_count), recv_count)
        code = jnp.maximum(label - 1, 0)
        column[at] = lax.div(code, own_count)
        spot = pl.ds(pl.multiple_of(lax.rem(code, own_count) * width, width), width)
        parts = [message(w, z) for z in range(near_count)]
        for side in range(2):
            order = parts if side == 0 else parts[::-1]
            half = jnp.concatenate([part[side] for part in order], axis=0).astype(tiles.dtype)
            start = at * width + (near_at if side == 0 else far_at)
            tiles[pl.ds(pl.multiple_of(start, half_size), half_size), spot] = half
        return found + live

    if wide_count <= UNROLL:
        labels = [read_label(w) for w in range(wide_count)]
        found = jnp.int32(0)
        for w in range(wide_count):
            found = keep(w, labels[w], found)
    else:

        def note(w, _):
            seen[w] = read_label(w)
            return 0

        lax.fori_loop(0, wide_count, note, 0)
        lax.fori_loop(0, wide_count, lambda w, found: keep(w, seen[w], found), jnp.int32(0))
    total = None
    for first in range(0, recv_count, GROUP):
        last = min(first + GROUP, recv_count)
        spots = [pl.multiple_of(column[u] * width, width) for u in range(first, last)]
        picked = jnp.concatenate([amp_ref[:, pl.ds(spot, width)] for spot in spots], axis=1)
        term = jnp.dot(
            picked, tiles[first * width : last * width], preferred_element_type=jnp.float32
        )
        total = term if total is None else total + term
    out_ref[...] = total


def shards(amplitudes, integrals, in_tile, counts, out_tile, owner_map):
    slot_count, rows, width = integrals.shape
    row_count = amplitudes.shape[0]
    wide_count = lax.axis_size("wide")
    depth_count = lax.axis_size("narrow")
    own_count = owner_map.shape[0] // wide_count
    recv_count = slot_count // 2
    near_count = depth_count // 2
    kind = integrals.dtype
    message_count = wide_count * near_count
    length = 2 * rows + PAIR
    if wide_count > UNROLL or length % PAIR != 0 or message_count * length % 16 != 0:
        length = -(-length // 16) * 16
    hbm = pl.BlockSpec(memory_space=pltpu.HBM)
    vmem = pl.BlockSpec(memory_space=pltpu.VMEM)
    limit = pltpu.CompilerParams(vmem_limit_bytes=32 * 2**20)
    across = [(z, depth_count - 1 - z) for z in range(depth_count)]
    far = lax.ppermute(integrals, "narrow", across)
    given = [in_tile, counts, out_tile, owner_map, integrals]
    given = [
        value if value.size == 1 else pltpu.with_memory_space_constraint(value, pltpu.HBM)
        for value in given
    ]
    ordered, sent = wide_count * rows, slot_count * rows
    order, labels, near = pl.pallas_call(
        functools.partial(route_kernel, own_count, wide_count),
        out_shape=[
            jax.ShapeDtypeStruct((ordered, sent), kind),
            jax.ShapeDtypeStruct((wide_count, width), kind),
            jax.ShapeDtypeStruct(integrals.shape, kind),
        ],
        in_specs=[hbm] * len(given),
        out_specs=[vmem] * 3,
        scratch_shapes=[pltpu.SMEM(value.shape, value.dtype) for value in given[:-1]]
        + [pltpu.SemaphoreType.DMA((len(given),))],
        compiler_params=limit,
        cost_estimate=pl.CostEstimate(flops=2**30, bytes_accessed=2**20, transcendentals=0),
        name="route",
    )(*given)
    send = pl.pallas_call(
        functools.partial(pack_kernel, wide_count, near_count),
        out_shape=jax.ShapeDtypeStruct((message_count * length, width), kind),
        in_specs=[vmem] * 4,
        out_specs=vmem,
        scratch_shapes=[
            pltpu.VMEM((sent, 2 * width), kind),
            pltpu.VMEM((ordered, 2 * width), jnp.float32),
        ],
        compiler_params=limit,
        name="pack",
    )(order, labels, near, far)
    places = group_places(wide_count, near_count)
    groups = [
        [w * depth_count + half * near_count + z for w, z in places] for half in range(2)
    ]
    got = lax.all_to_all(
        send.reshape(message_count, length // PAIR, PAIR, width),
        ("wide", "narrow"),
        split_axis=0,
        concat_axis=0,
        tiled=True,
        axis_index_groups=groups,
    ).reshape(message_count * length, width)
    return pl.pallas_call(
        functools.partial(ladder_kernel, rows, near_count, own_count, recv_count),
        out_shape=jax.ShapeDtypeStruct((row_count, own_count * width), jnp.float32),
        in_specs=[vmem] * 2,
        out_specs=vmem,
        scratch_shapes=[
            pltpu.VMEM(((recv_count + 1) * width, own_count * width), kind),
            pltpu.SMEM((recv_count + 1,), jnp.int32),
            pltpu.SMEM((wide_count,), jnp.int32),
        ],
        compiler_params=limit,
        name="ladder",
    )(amplitudes, got)


def solution(mesh):
    return jax.shard_map(
        shards,
        mesh=mesh,
        in_specs=(
            P("narrow", None),
            P("wide", "narrow", None),
            P("wide"),
            P("wide"),
            P("wide"),
            P(),
        ),
        out_specs=P("narrow", "wide"),
        check_vma=False,
    )
```

```python
import functools

import jax
import jax.numpy as jnp
from jax import lax
from jax.experimental import pallas as pl
from jax.experimental.pallas import tpu as pltpu
from jax.sharding import PartitionSpec as P

PAIR = 2
GROUP = 4
UNROLL = 8
CORES = 2


def each(count, body, start):
    if count > UNROLL:
        return lax.fori_loop(0, count, body, start)
    for i in range(count):
        start = body(i, start)
    return start


def chip_order(wide_count):
    chip_count = wide_count // CORES
    if wide_count > UNROLL:
        return list(range(chip_count))
    bits = (chip_count - 1).bit_length()
    flipped = [int(format(chip, "b").zfill(bits)[::-1], 2) for chip in range(2**bits)]
    return [chip for chip in flipped[1:] if chip < chip_count] + [0]


def group_places(wide_count, near_count):
    cores = range(CORES)
    depths = range(near_count)
    return [(chip * CORES + core, z) for chip in chip_order(wide_count) for z in depths for core in cores]


def message_at(w, z, wide_count, near_count, length):
    if isinstance(w, int):
        return group_places(wide_count, near_count).index((w, z)) * length
    place = (w // CORES * near_count + z) * CORES + w % CORES
    return pl.multiple_of(place * length, length)


def route_kernel(own_count, wide_count, *refs):
    sources, (order_ref, label_ref, near_ref), targets, sems = refs[:5], refs[5:8], refs[8:12], refs[12]
    in_tile, counts, out_tile, owner_map = targets
    copies = [
        pltpu.make_async_copy(source, target, sems.at[i])
        for i, (source, target) in enumerate(zip(sources, (*targets, near_ref)))
    ]
    for copy in copies:
        copy.start()
    for copy in copies[:4]:
        copy.wait()
    slot_count, rows, width = near_ref.shape
    column = lax.broadcasted_iota(jnp.int32, (1, slot_count * rows), 1)
    owners = lax.broadcasted_iota(jnp.int32, (wide_count, width), 0)

    def route(h, carry):
        owner_of, labels = carry
        spot = owner_map[out_tile[h]]
        owner = lax.div(spot, own_count)
        label = in_tile[h] * own_count + lax.rem(spot, own_count) + 1
        label = jnp.where(h < counts[0], label, 0)
        owner_of = jnp.where(lax.div(column, rows) == h, owner, owner_of)
        return owner_of, jnp.where(owners == owner, label, labels)

    start = (jnp.zeros_like(column), jnp.zeros((wide_count, width), jnp.int32))
    owner_of, labels = each(slot_count, route, start)
    label_ref[...] = labels.astype(jnp.float32).astype(label_ref.dtype)
    row = lax.broadcasted_iota(jnp.int32, (wide_count * rows, 1), 0)
    hit = row == owner_of * rows + lax.rem(column, rows)
    order_ref[...] = hit.astype(jnp.float32).astype(order_ref.dtype)
    copies[4].wait()


def pack_kernel(wide_count, near_count, order_ref, label_ref, near_ref, far_ref, send_ref, both, ordered):
    slot_count, rows, width = near_ref.shape
    length = send_ref.shape[0] // (wide_count * near_count)
    for side, ref in enumerate((near_ref, far_ref)):
        block = ref[...]
        if rows % 16 != 0:
            block = block.astype(jnp.float32)
        block = block.reshape(slot_count * rows, width).astype(both.dtype)
        both[:, side * width : (side + 1) * width] = block
    ordered[...] = jnp.dot(order_ref[...], both[...], preferred_element_type=jnp.float32)
    labels = label_ref[...].astype(jnp.float32)
    ids = lax.broadcasted_iota(jnp.int32, labels.shape, 0)

    def write(owner, _):
        spot = owner * rows
        if not isinstance(owner, int):
            spot = pl.multiple_of(spot, rows)
        near = ordered[pl.ds(spot, rows), :width]
        far = ordered[pl.ds(spot, rows), width:]
        label = jnp.sum(jnp.where(ids == owner, labels, 0.0), axis=0, keepdims=True)
        label = jnp.broadcast_to(label, (length - 2 * rows, width))
        if length % 16 == 0:
            pieces = [(0, jnp.concatenate([near, far, label], axis=0))]
        else:
            pieces = [(0, near), (rows, far), (2 * rows, label)]
        for z in range(near_count):
            start = message_at(owner, z, wide_count, near_count, length)
            for offset, piece in pieces:
                send_ref[pl.ds(start + offset, piece.shape[0])] = piece.astype(send_ref.dtype)
        return 0

    each(wide_count, write, 0)


def ladder_kernel(
    rows, near_count, own_count, recv_count, amp_ref, got_ref, out_ref, tiles, column, seen
):
    wide_count = seen.shape[0]
    width = got_ref.shape[1]
    length = got_ref.shape[0] // (wide_count * near_count)
    half_size = near_count * rows
    upper = (lax.axis_index("narrow") >= near_count).astype(jnp.int32)
    near_at, far_at = upper * half_size, (1 - upper) * half_size
    tiles[...] = jnp.zeros_like(tiles)
    for u in range(recv_count):
        column[u] = 0

    def message(w, z):
        start = message_at(w, z, wide_count, near_count, length)
        if length % 16 == 0:
            block = got_ref[pl.ds(start, length)].astype(jnp.float32)
            return block[:rows], block[rows : 2 * rows]
        return got_ref[pl.ds(start, rows)], got_ref[pl.ds(start + rows, rows)]

    def read_label(w):
        start = message_at(w, 0, wide_count, near_count, length)
        if length % 16 == 0:
            label = got_ref[pl.ds(start, length)].astype(jnp.float32)[2 * rows :]
        else:
            label = got_ref[pl.ds(start + 2 * rows, length - 2 * rows)].astype(jnp.float32)
        return label[0, 0].astype(jnp.int32)

    def keep(w, label, found):
        live = jnp.minimum(label, 1)
        at = jnp.where(label > 0, jnp.minimum(found, recv_count), recv_count)
        code = jnp.maximum(label - 1, 0)
        column[at] = lax.div(code, own_count)
        spot = pl.ds(pl.multiple_of(lax.rem(code, own_count) * width, width), width)
        parts = [message(w, z) for z in range(near_count)]
        for side in range(2):
            order = parts if side == 0 else parts[::-1]
            half = jnp.concatenate([part[side] for part in order], axis=0).astype(tiles.dtype)
            start = at * width + (near_at if side == 0 else far_at)
            tiles[pl.ds(pl.multiple_of(start, half_size), half_size), spot] = half
        return found + live

    if wide_count <= UNROLL:
        labels = [read_label(w) for w in range(wide_count)]
        found = jnp.int32(0)
        for w in range(wide_count):
            found = keep(w, labels[w], found)
    else:

        def note(w, _):
            seen[w] = read_label(w)
            return 0

        lax.fori_loop(0, wide_count, note, 0)
        lax.fori_loop(0, wide_count, lambda w, found: keep(w, seen[w], found), jnp.int32(0))
    total = None
    for first in range(0, recv_count, GROUP):
        last = min(first + GROUP, recv_count)
        spots = [pl.multiple_of(column[u] * width, width) for u in range(first, last)]
        picked = jnp.concatenate([amp_ref[:, pl.ds(spot, width)] for spot in spots], axis=1)
        term = jnp.dot(
            picked, tiles[first * width : last * width], preferred_element_type=jnp.float32
        )
        total = term if total is None else total + term
    out_ref[...] = total


def shards(amplitudes, integrals, in_tile, counts, out_tile, owner_map):
    slot_count, rows, width = integrals.shape
    row_count = amplitudes.shape[0]
    wide_count = lax.axis_size("wide")
    depth_count = lax.axis_size("narrow")
    own_count = owner_map.shape[0] // wide_count
    recv_count = slot_count // 2
    near_count = depth_count // 2
    kind = integrals.dtype
    message_count = wide_count * near_count
    length = 2 * rows + PAIR
    if wide_count > UNROLL or length % PAIR != 0 or message_count * length % 16 != 0:
        length = -(-length // 16) * 16
    hbm = pl.BlockSpec(memory_space=pltpu.HBM)
    vmem = pl.BlockSpec(memory_space=pltpu.VMEM)
    limit = pltpu.CompilerParams(vmem_limit_bytes=32 * 2**20)
    across = [(z, depth_count - 1 - z) for z in range(depth_count)]
    far = lax.ppermute(integrals, "narrow", across)
    given = [in_tile, counts, out_tile, owner_map, integrals]
    given = [
        value if value.size == 1 else pltpu.with_memory_space_constraint(value, pltpu.HBM)
        for value in given
    ]
    ordered, sent = wide_count * rows, slot_count * rows
    order, labels, near = pl.pallas_call(
        functools.partial(route_kernel, own_count, wide_count),
        out_shape=[
            jax.ShapeDtypeStruct((ordered, sent), kind),
            jax.ShapeDtypeStruct((wide_count, width), kind),
            jax.ShapeDtypeStruct(integrals.shape, kind),
        ],
        in_specs=[hbm] * len(given),
        out_specs=[vmem] * 3,
        scratch_shapes=[pltpu.SMEM(value.shape, value.dtype) for value in given[:-1]]
        + [pltpu.SemaphoreType.DMA((len(given),))],
        compiler_params=limit,
        cost_estimate=pl.CostEstimate(flops=2**30, bytes_accessed=2**20, transcendentals=0),
        name="route",
    )(*given)
    send = pl.pallas_call(
        functools.partial(pack_kernel, wide_count, near_count),
        out_shape=jax.ShapeDtypeStruct((message_count * length, width), kind),
        in_specs=[vmem] * 4,
        out_specs=vmem,
        scratch_shapes=[
            pltpu.VMEM((sent, 2 * width), kind),
            pltpu.VMEM((ordered, 2 * width), jnp.float32),
        ],
        compiler_params=limit,
        name="pack",
    )(order, labels, near, far)
    places = group_places(wide_count, near_count)
    groups = [
        [w * depth_count + half * near_count + z for w, z in places] for half in range(2)
    ]
    got = lax.all_to_all(
        send.reshape(message_count, length // PAIR, PAIR, width),
        ("wide", "narrow"),
        split_axis=0,
        concat_axis=0,
        tiled=True,
        axis_index_groups=groups,
    ).reshape(message_count * length, width)
    return pl.pallas_call(
        functools.partial(ladder_kernel, rows, near_count, own_count, recv_count),
        out_shape=jax.ShapeDtypeStruct((row_count, own_count * width), jnp.float32),
        in_specs=[vmem] * 2,
        out_specs=vmem,
        scratch_shapes=[
            pltpu.VMEM(((recv_count + 1) * width, own_count * width), kind),
            pltpu.SMEM((recv_count + 1,), jnp.int32),
            pltpu.SMEM((wide_count,), jnp.int32),
        ],
        compiler_params=limit,
        name="ladder",
    )(amplitudes, got)


def solution(mesh):
    return jax.shard_map(
        shards,
        mesh=mesh,
        in_specs=(
            P("narrow", None),
            P("wide", "narrow", None),
            P("wide"),
            P("wide"),
            P("wide"),
            P(),
        ),
        out_specs=P("narrow", "wide"),
        check_vma=False,
    )
```

```python
import functools

import jax
import jax.numpy as jnp
from jax import lax
from jax.experimental import pallas as pl
from jax.experimental.pallas import tpu as pltpu
from jax.sharding import PartitionSpec as P

PAIR = 2
GROUP = 4
UNROLL = 8
CORES = 2


def each(count, body, start):
    if count > UNROLL:
        return lax.fori_loop(0, count, body, start)
    for i in range(count):
        start = body(i, start)
    return start


def chip_order(wide_count):
    chip_count = wide_count // CORES
    if wide_count > UNROLL:
        return list(range(chip_count))
    bits = (chip_count - 1).bit_length()
    flipped = [int(format(chip, "b").zfill(bits)[::-1], 2) for chip in range(2**bits)]
    return [chip for chip in flipped[1:] if chip < chip_count] + [0]


def group_places(wide_count, near_count):
    cores = range(CORES)
    depths = list(reversed(range(near_count)))
    return [(chip * CORES + core, z) for chip in chip_order(wide_count) for z in depths for core in cores]


def message_at(w, z, wide_count, near_count, length):
    if isinstance(w, int):
        return group_places(wide_count, near_count).index((w, z)) * length
    place = (w // CORES * near_count + near_count - 1 - z) * CORES + w % CORES
    return pl.multiple_of(place * length, length)


def route_kernel(own_count, wide_count, *refs):
    sources, (order_ref, label_ref, near_ref), targets, sems = refs[:5], refs[5:8], refs[8:12], refs[12]
    in_tile, counts, out_tile, owner_map = targets
    copies = [
        pltpu.make_async_copy(source, target, sems.at[i])
        for i, (source, target) in enumerate(zip(sources, (*targets, near_ref)))
    ]
    for copy in copies:
        copy.start()
    for copy in copies[:4]:
        copy.wait()
    slot_count, rows, width = near_ref.shape
    column = lax.broadcasted_iota(jnp.int32, (1, slot_count * rows), 1)
    owners = lax.broadcasted_iota(jnp.int32, (wide_count, width), 0)

    def route(h, carry):
        owner_of, labels = carry
        spot = owner_map[out_tile[h]]
        owner = lax.div(spot, own_count)
        label = in_tile[h] * own_count + lax.rem(spot, own_count) + 1
        label = jnp.where(h < counts[0], label, 0)
        owner_of = jnp.where(lax.div(column, rows) == h, owner, owner_of)
        return owner_of, jnp.where(owners == owner, label, labels)

    start = (jnp.zeros_like(column), jnp.zeros((wide_count, width), jnp.int32))
    owner_of, labels = each(slot_count, route, start)
    label_ref[...] = labels.astype(jnp.float32).astype(label_ref.dtype)
    row = lax.broadcasted_iota(jnp.int32, (wide_count * rows, 1), 0)
    hit = row == owner_of * rows + lax.rem(column, rows)
    order_ref[...] = hit.astype(jnp.float32).astype(order_ref.dtype)
    copies[4].wait()


def pack_kernel(wide_count, near_count, order_ref, label_ref, near_ref, far_ref, send_ref, both, ordered):
    slot_count, rows, width = near_ref.shape
    length = send_ref.shape[0] // (wide_count * near_count)
    for side, ref in enumerate((near_ref, far_ref)):
        block = ref[...]
        if rows % 16 != 0:
            block = block.astype(jnp.float32)
        block = block.reshape(slot_count * rows, width).astype(both.dtype)
        both[:, side * width : (side + 1) * width] = block
    ordered[...] = jnp.dot(order_ref[...], both[...], preferred_element_type=jnp.float32)
    labels = label_ref[...].astype(jnp.float32)
    ids = lax.broadcasted_iota(jnp.int32, labels.shape, 0)

    def write(owner, _):
        spot = owner * rows
        if not isinstance(owner, int):
            spot = pl.multiple_of(spot, rows)
        near = ordered[pl.ds(spot, rows), :width]
        far = ordered[pl.ds(spot, rows), width:]
        label = jnp.sum(jnp.where(ids == owner, labels, 0.0), axis=0, keepdims=True)
        label = jnp.broadcast_to(label, (length - 2 * rows, width))
        if length % 16 == 0:
            pieces = [(0, jnp.concatenate([near, far, label], axis=0))]
        else:
            pieces = [(0, near), (rows, far), (2 * rows, label)]
        for z in range(near_count):
            start = message_at(owner, z, wide_count, near_count, length)
            for offset, piece in pieces:
                send_ref[pl.ds(start + offset, piece.shape[0])] = piece.astype(send_ref.dtype)
        return 0

    each(wide_count, write, 0)


def ladder_kernel(
    rows, near_count, own_count, recv_count, amp_ref, got_ref, out_ref, tiles, column, seen
):
    wide_count = seen.shape[0]
    width = got_ref.shape[1]
    length = got_ref.shape[0] // (wide_count * near_count)
    half_size = near_count * rows
    upper = (lax.axis_index("narrow") >= near_count).astype(jnp.int32)
    near_at, far_at = upper * half_size, (1 - upper) * half_size
    tiles[...] = jnp.zeros_like(tiles)
    for u in range(recv_count):
        column[u] = 0

    def message(w, z):
        start = message_at(w, z, wide_count, near_count, length)
        if length % 16 == 0:
            block = got_ref[pl.ds(start, length)].astype(jnp.float32)
            return block[:rows], block[rows : 2 * rows]
        return got_ref[pl.ds(start, rows)], got_ref[pl.ds(start + rows, rows)]

    def read_label(w):
        start = message_at(w, 0, wide_count, near_count, length)
        if length % 16 == 0:
            label = got_ref[pl.ds(start, length)].astype(jnp.float32)[2 * rows :]
        else:
            label = got_ref[pl.ds(start + 2 * rows, length - 2 * rows)].astype(jnp.float32)
        return label[0, 0].astype(jnp.int32)

    def keep(w, label, found):
        live = jnp.minimum(label, 1)
        at = jnp.where(label > 0, jnp.minimum(found, recv_count), recv_count)
        code = jnp.maximum(label - 1, 0)
        column[at] = lax.div(code, own_count)
        spot = pl.ds(pl.multiple_of(lax.rem(code, own_count) * width, width), width)
        parts = [message(w, z) for z in range(near_count)]
        for side in range(2):
            order = parts if side == 0 else parts[::-1]
            half = jnp.concatenate([part[side] for part in order], axis=0).astype(tiles.dtype)
            start = at * width + (near_at if side == 0 else far_at)
            tiles[pl.ds(pl.multiple_of(start, half_size), half_size), spot] = half
        return found + live

    if wide_count <= UNROLL:
        labels = [read_label(w) for w in range(wide_count)]
        found = jnp.int32(0)
        for w in range(wide_count):
            found = keep(w, labels[w], found)
    else:

        def note(w, _):
            seen[w] = read_label(w)
            return 0

        lax.fori_loop(0, wide_count, note, 0)
        lax.fori_loop(0, wide_count, lambda w, found: keep(w, seen[w], found), jnp.int32(0))
    total = None
    for first in range(0, recv_count, GROUP):
        last = min(first + GROUP, recv_count)
        spots = [pl.multiple_of(column[u] * width, width) for u in range(first, last)]
        picked = jnp.concatenate([amp_ref[:, pl.ds(spot, width)] for spot in spots], axis=1)
        term = jnp.dot(
            picked, tiles[first * width : last * width], preferred_element_type=jnp.float32
        )
        total = term if total is None else total + term
    out_ref[...] = total


def shards(amplitudes, integrals, in_tile, counts, out_tile, owner_map):
    slot_count, rows, width = integrals.shape
    row_count = amplitudes.shape[0]
    wide_count = lax.axis_size("wide")
    depth_count = lax.axis_size("narrow")
    own_count = owner_map.shape[0] // wide_count
    recv_count = slot_count // 2
    near_count = depth_count // 2
    kind = integrals.dtype
    message_count = wide_count * near_count
    length = 2 * rows + PAIR
    if wide_count > UNROLL or length % PAIR != 0 or message_count * length % 16 != 0:
        length = -(-length // 16) * 16
    hbm = pl.BlockSpec(memory_space=pltpu.HBM)
    vmem = pl.BlockSpec(memory_space=pltpu.VMEM)
    limit = pltpu.CompilerParams(vmem_limit_bytes=32 * 2**20)
    across = [(z, depth_count - 1 - z) for z in range(depth_count)]
    far = lax.ppermute(integrals, "narrow", across)
    given = [in_tile, counts, out_tile, owner_map, integrals]
    given = [
        value if value.size == 1 else pltpu.with_memory_space_constraint(value, pltpu.HBM)
        for value in given
    ]
    ordered, sent = wide_count * rows, slot_count * rows
    order, labels, near = pl.pallas_call(
        functools.partial(route_kernel, own_count, wide_count),
        out_shape=[
            jax.ShapeDtypeStruct((ordered, sent), kind),
            jax.ShapeDtypeStruct((wide_count, width), kind),
            jax.ShapeDtypeStruct(integrals.shape, kind),
        ],
        in_specs=[hbm] * len(given),
        out_specs=[vmem] * 3,
        scratch_shapes=[pltpu.SMEM(value.shape, value.dtype) for value in given[:-1]]
        + [pltpu.SemaphoreType.DMA((len(given),))],
        compiler_params=limit,
        cost_estimate=pl.CostEstimate(flops=2**30, bytes_accessed=2**20, transcendentals=0),
        name="route",
    )(*given)
    send = pl.pallas_call(
        functools.partial(pack_kernel, wide_count, near_count),
        out_shape=jax.ShapeDtypeStruct((message_count * length, width), kind),
        in_specs=[vmem] * 4,
        out_specs=vmem,
        scratch_shapes=[
            pltpu.VMEM((sent, 2 * width), kind),
            pltpu.VMEM((ordered, 2 * width), jnp.float32),
        ],
        compiler_params=limit,
        name="pack",
    )(order, labels, near, far)
    places = group_places(wide_count, near_count)
    groups = [
        [w * depth_count + half * near_count + z for w, z in places] for half in range(2)
    ]
    got = lax.all_to_all(
        send.reshape(message_count, length // PAIR, PAIR, width),
        ("wide", "narrow"),
        split_axis=0,
        concat_axis=0,
        tiled=True,
        axis_index_groups=groups,
    ).reshape(message_count * length, width)
    return pl.pallas_call(
        functools.partial(ladder_kernel, rows, near_count, own_count, recv_count),
        out_shape=jax.ShapeDtypeStruct((row_count, own_count * width), jnp.float32),
        in_specs=[vmem] * 2,
        out_specs=vmem,
        scratch_shapes=[
            pltpu.VMEM(((recv_count + 1) * width, own_count * width), kind),
            pltpu.SMEM((recv_count + 1,), jnp.int32),
            pltpu.SMEM((wide_count,), jnp.int32),
        ],
        compiler_params=limit,
        name="ladder",
    )(amplitudes, got)


def solution(mesh):
    return jax.shard_map(
        shards,
        mesh=mesh,
        in_specs=(
            P("narrow", None),
            P("wide", "narrow", None),
            P("wide"),
            P("wide"),
            P("wide"),
            P(),
        ),
        out_specs=P("narrow", "wide"),
        check_vma=False,
    )
```

```python
import functools

import jax
import jax.numpy as jnp
from jax import lax
from jax.experimental import pallas as pl
from jax.experimental.pallas import tpu as pltpu
from jax.sharding import PartitionSpec as P

PAIR = 2
GROUP = 4
UNROLL = 8
CORES = 2


def each(count, body, start):
    if count > UNROLL:
        return lax.fori_loop(0, count, body, start)
    for i in range(count):
        start = body(i, start)
    return start


def chip_order(wide_count):
    chip_count = wide_count // CORES
    if wide_count > UNROLL:
        return list(range(chip_count))
    size = 2 ** (chip_count - 1).bit_length()
    ring = [step ^ (step >> 1) for step in range(1, size)]
    return [chip for chip in ring if chip < chip_count] + [0]


def group_places(wide_count, near_count):
    cores = range(CORES)
    depths = list(reversed(range(near_count)))
    return [(chip * CORES + core, z) for chip in chip_order(wide_count) for z in depths for core in cores]


def message_at(w, z, wide_count, near_count, length):
    if isinstance(w, int):
        return group_places(wide_count, near_count).index((w, z)) * length
    place = (w // CORES * near_count + near_count - 1 - z) * CORES + w % CORES
    return pl.multiple_of(place * length, length)


def route_kernel(own_count, wide_count, *refs):
    sources, (order_ref, label_ref, near_ref), targets, sems = refs[:5], refs[5:8], refs[8:12], refs[12]
    in_tile, counts, out_tile, owner_map = targets
    copies = [
        pltpu.make_async_copy(source, target, sems.at[i])
        for i, (source, target) in enumerate(zip(sources, (*targets, near_ref)))
    ]
    for copy in copies:
        copy.start()
    for copy in copies[:4]:
        copy.wait()
    slot_count, rows, width = near_ref.shape
    column = lax.broadcasted_iota(jnp.int32, (1, slot_count * rows), 1)
    owners = lax.broadcasted_iota(jnp.int32, (wide_count, width), 0)

    def route(h, carry):
        owner_of, labels = carry
        spot = owner_map[out_tile[h]]
        owner = lax.div(spot, own_count)
        label = in_tile[h] * own_count + lax.rem(spot, own_count) + 1
        label = jnp.where(h < counts[0], label, 0)
        owner_of = jnp.where(lax.div(column, rows) == h, owner, owner_of)
        return owner_of, jnp.where(owners == owner, label, labels)

    start = (jnp.zeros_like(column), jnp.zeros((wide_count, width), jnp.int32))
    owner_of, labels = each(slot_count, route, start)
    label_ref[...] = labels.astype(jnp.float32).astype(label_ref.dtype)
    row = lax.broadcasted_iota(jnp.int32, (wide_count * rows, 1), 0)
    hit = row == owner_of * rows + lax.rem(column, rows)
    order_ref[...] = hit.astype(jnp.float32).astype(order_ref.dtype)
    copies[4].wait()


def pack_kernel(wide_count, near_count, order_ref, label_ref, near_ref, far_ref, send_ref, both, ordered):
    slot_count, rows, width = near_ref.shape
    length = send_ref.shape[0] // (wide_count * near_count)
    for side, ref in enumerate((near_ref, far_ref)):
        block = ref[...]
        if rows % 16 != 0:
            block = block.astype(jnp.float32)
        block = block.reshape(slot_count * rows, width).astype(both.dtype)
        both[:, side * width : (side + 1) * width] = block
    ordered[...] = jnp.dot(order_ref[...], both[...], preferred_element_type=jnp.float32)
    labels = label_ref[...].astype(jnp.float32)
    ids = lax.broadcasted_iota(jnp.int32, labels.shape, 0)

    def write(owner, _):
        spot = owner * rows
        if not isinstance(owner, int):
            spot = pl.multiple_of(spot, rows)
        near = ordered[pl.ds(spot, rows), :width]
        far = ordered[pl.ds(spot, rows), width:]
        label = jnp.sum(jnp.where(ids == owner, labels, 0.0), axis=0, keepdims=True)
        label = jnp.broadcast_to(label, (length - 2 * rows, width))
        if length % 16 == 0:
            pieces = [(0, jnp.concatenate([near, far, label], axis=0))]
        else:
            pieces = [(0, near), (rows, far), (2 * rows, label)]
        for z in range(near_count):
            start = message_at(owner, z, wide_count, near_count, length)
            for offset, piece in pieces:
                send_ref[pl.ds(start + offset, piece.shape[0])] = piece.astype(send_ref.dtype)
        return 0

    each(wide_count, write, 0)


def ladder_kernel(
    rows, near_count, own_count, recv_count, amp_ref, got_ref, out_ref, tiles, column, seen
):
    wide_count = seen.shape[0]
    width = got_ref.shape[1]
    length = got_ref.shape[0] // (wide_count * near_count)
    half_size = near_count * rows
    upper = (lax.axis_index("narrow") >= near_count).astype(jnp.int32)
    near_at, far_at = upper * half_size, (1 - upper) * half_size
    tiles[...] = jnp.zeros_like(tiles)
    for u in range(recv_count):
        column[u] = 0

    def message(w, z):
        start = message_at(w, z, wide_count, near_count, length)
        if length % 16 == 0:
            block = got_ref[pl.ds(start, length)].astype(jnp.float32)
            return block[:rows], block[rows : 2 * rows]
        return got_ref[pl.ds(start, rows)], got_ref[pl.ds(start + rows, rows)]

    def read_label(w):
        start = message_at(w, 0, wide_count, near_count, length)
        if length % 16 == 0:
            label = got_ref[pl.ds(start, length)].astype(jnp.float32)[2 * rows :]
        else:
            label = got_ref[pl.ds(start + 2 * rows, length - 2 * rows)].astype(jnp.float32)
        return label[0, 0].astype(jnp.int32)

    def keep(w, label, found):
        live = jnp.minimum(label, 1)
        at = jnp.where(label > 0, jnp.minimum(found, recv_count), recv_count)
        code = jnp.maximum(label - 1, 0)
        column[at] = lax.div(code, own_count)
        spot = pl.ds(pl.multiple_of(lax.rem(code, own_count) * width, width), width)
        parts = [message(w, z) for z in range(near_count)]
        for side in range(2):
            order = parts if side == 0 else parts[::-1]
            half = jnp.concatenate([part[side] for part in order], axis=0).astype(tiles.dtype)
            start = at * width + (near_at if side == 0 else far_at)
            tiles[pl.ds(pl.multiple_of(start, half_size), half_size), spot] = half
        return found + live

    if wide_count <= UNROLL:
        labels = [read_label(w) for w in range(wide_count)]
        found = jnp.int32(0)
        for w in range(wide_count):
            found = keep(w, labels[w], found)
    else:

        def note(w, _):
            seen[w] = read_label(w)
            return 0

        lax.fori_loop(0, wide_count, note, 0)
        lax.fori_loop(0, wide_count, lambda w, found: keep(w, seen[w], found), jnp.int32(0))
    total = None
    for first in range(0, recv_count, GROUP):
        last = min(first + GROUP, recv_count)
        spots = [pl.multiple_of(column[u] * width, width) for u in range(first, last)]
        picked = jnp.concatenate([amp_ref[:, pl.ds(spot, width)] for spot in spots], axis=1)
        term = jnp.dot(
            picked, tiles[first * width : last * width], preferred_element_type=jnp.float32
        )
        total = term if total is None else total + term
    out_ref[...] = total


def shards(amplitudes, integrals, in_tile, counts, out_tile, owner_map):
    slot_count, rows, width = integrals.shape
    row_count = amplitudes.shape[0]
    wide_count = lax.axis_size("wide")
    depth_count = lax.axis_size("narrow")
    own_count = owner_map.shape[0] // wide_count
    recv_count = slot_count // 2
    near_count = depth_count // 2
    kind = integrals.dtype
    message_count = wide_count * near_count
    length = 2 * rows + PAIR
    if wide_count > UNROLL or length % PAIR != 0 or message_count * length % 16 != 0:
        length = -(-length // 16) * 16
    hbm = pl.BlockSpec(memory_space=pltpu.HBM)
    vmem = pl.BlockSpec(memory_space=pltpu.VMEM)
    limit = pltpu.CompilerParams(vmem_limit_bytes=32 * 2**20)
    across = [(z, depth_count - 1 - z) for z in range(depth_count)]
    far = lax.ppermute(integrals, "narrow", across)
    given = [in_tile, counts, out_tile, owner_map, integrals]
    given = [
        value if value.size == 1 else pltpu.with_memory_space_constraint(value, pltpu.HBM)
        for value in given
    ]
    ordered, sent = wide_count * rows, slot_count * rows
    order, labels, near = pl.pallas_call(
        functools.partial(route_kernel, own_count, wide_count),
        out_shape=[
            jax.ShapeDtypeStruct((ordered, sent), kind),
            jax.ShapeDtypeStruct((wide_count, width), kind),
            jax.ShapeDtypeStruct(integrals.shape, kind),
        ],
        in_specs=[hbm] * len(given),
        out_specs=[vmem] * 3,
        scratch_shapes=[pltpu.SMEM(value.shape, value.dtype) for value in given[:-1]]
        + [pltpu.SemaphoreType.DMA((len(given),))],
        compiler_params=limit,
        cost_estimate=pl.CostEstimate(flops=2**30, bytes_accessed=2**20, transcendentals=0),
        name="route",
    )(*given)
    send = pl.pallas_call(
        functools.partial(pack_kernel, wide_count, near_count),
        out_shape=jax.ShapeDtypeStruct((message_count * length, width), kind),
        in_specs=[vmem] * 4,
        out_specs=vmem,
        scratch_shapes=[
            pltpu.VMEM((sent, 2 * width), kind),
            pltpu.VMEM((ordered, 2 * width), jnp.float32),
        ],
        compiler_params=limit,
        name="pack",
    )(order, labels, near, far)
    places = group_places(wide_count, near_count)
    groups = [
        [w * depth_count + half * near_count + z for w, z in places] for half in range(2)
    ]
    got = lax.all_to_all(
        send.reshape(message_count, length // PAIR, PAIR, width),
        ("wide", "narrow"),
        split_axis=0,
        concat_axis=0,
        tiled=True,
        axis_index_groups=groups,
    ).reshape(message_count * length, width)
    return pl.pallas_call(
        functools.partial(ladder_kernel, rows, near_count, own_count, recv_count),
        out_shape=jax.ShapeDtypeStruct((row_count, own_count * width), jnp.float32),
        in_specs=[vmem] * 2,
        out_specs=vmem,
        scratch_shapes=[
            pltpu.VMEM(((recv_count + 1) * width, own_count * width), kind),
            pltpu.SMEM((recv_count + 1,), jnp.int32),
            pltpu.SMEM((wide_count,), jnp.int32),
        ],
        compiler_params=limit,
        name="ladder",
    )(amplitudes, got)


def solution(mesh):
    return jax.shard_map(
        shards,
        mesh=mesh,
        in_specs=(
            P("narrow", None),
            P("wide", "narrow", None),
            P("wide"),
            P("wide"),
            P("wide"),
            P(),
        ),
        out_specs=P("narrow", "wide"),
        check_vma=False,
    )
```

```python
import functools

import jax
import jax.numpy as jnp
from jax import lax
from jax.experimental import pallas as pl
from jax.experimental.pallas import tpu as pltpu
from jax.sharding import PartitionSpec as P

PAIR = 2
GROUP = 4
UNROLL = 8
CORES = 2


def each(count, body, start):
    if count > UNROLL:
        return lax.fori_loop(0, count, body, start)
    for i in range(count):
        start = body(i, start)
    return start


def chip_order(wide_count):
    chip_count = wide_count // CORES
    if wide_count > UNROLL:
        return list(range(chip_count))
    return list(range(1, chip_count)) + [0]


def group_places(wide_count, near_count):
    cores = range(CORES)
    depths = list(reversed(range(near_count)))
    return [(chip * CORES + core, z) for chip in chip_order(wide_count) for z in depths for core in cores]


def message_at(w, z, wide_count, near_count, length):
    if isinstance(w, int):
        return group_places(wide_count, near_count).index((w, z)) * length
    place = (w // CORES * near_count + near_count - 1 - z) * CORES + w % CORES
    return pl.multiple_of(place * length, length)


def route_kernel(own_count, wide_count, *refs):
    sources, (order_ref, label_ref, near_ref), targets, sems = refs[:5], refs[5:8], refs[8:12], refs[12]
    in_tile, counts, out_tile, owner_map = targets
    copies = [
        pltpu.make_async_copy(source, target, sems.at[i])
        for i, (source, target) in enumerate(zip(sources, (*targets, near_ref)))
    ]
    for copy in copies:
        copy.start()
    for copy in copies[:4]:
        copy.wait()
    slot_count, rows, width = near_ref.shape
    column = lax.broadcasted_iota(jnp.int32, (1, slot_count * rows), 1)
    owners = lax.broadcasted_iota(jnp.int32, (wide_count, width), 0)

    def route(h, carry):
        owner_of, labels = carry
        spot = owner_map[out_tile[h]]
        owner = lax.div(spot, own_count)
        label = in_tile[h] * own_count + lax.rem(spot, own_count) + 1
        label = jnp.where(h < counts[0], label, 0)
        owner_of = jnp.where(lax.div(column, rows) == h, owner, owner_of)
        return owner_of, jnp.where(owners == owner, label, labels)

    start = (jnp.zeros_like(column), jnp.zeros((wide_count, width), jnp.int32))
    owner_of, labels = each(slot_count, route, start)
    label_ref[...] = labels.astype(jnp.float32).astype(label_ref.dtype)
    row = lax.broadcasted_iota(jnp.int32, (wide_count * rows, 1), 0)
    hit = row == owner_of * rows + lax.rem(column, rows)
    order_ref[...] = hit.astype(jnp.float32).astype(order_ref.dtype)
    copies[4].wait()


def pack_kernel(wide_count, near_count, order_ref, label_ref, near_ref, far_ref, send_ref, both, ordered):
    slot_count, rows, width = near_ref.shape
    length = send_ref.shape[0] // (wide_count * near_count)
    for side, ref in enumerate((near_ref, far_ref)):
        block = ref[...]
        if rows % 16 != 0:
            block = block.astype(jnp.float32)
        block = block.reshape(slot_count * rows, width).astype(both.dtype)
        both[:, side * width : (side + 1) * width] = block
    ordered[...] = jnp.dot(order_ref[...], both[...], preferred_element_type=jnp.float32)
    labels = label_ref[...].astype(jnp.float32)
    ids = lax.broadcasted_iota(jnp.int32, labels.shape, 0)

    def write(owner, _):
        spot = owner * rows
        if not isinstance(owner, int):
            spot = pl.multiple_of(spot, rows)
        near = ordered[pl.ds(spot, rows), :width]
        far = ordered[pl.ds(spot, rows), width:]
        label = jnp.sum(jnp.where(ids == owner, labels, 0.0), axis=0, keepdims=True)
        label = jnp.broadcast_to(label, (length - 2 * rows, width))
        if length % 16 == 0:
            pieces = [(0, jnp.concatenate([near, far, label], axis=0))]
        else:
            pieces = [(0, near), (rows, far), (2 * rows, label)]
        for z in range(near_count):
            start = message_at(owner, z, wide_count, near_count, length)
            for offset, piece in pieces:
                send_ref[pl.ds(start + offset, piece.shape[0])] = piece.astype(send_ref.dtype)
        return 0

    each(wide_count, write, 0)


def ladder_kernel(
    rows, near_count, own_count, recv_count, amp_ref, got_ref, out_ref, tiles, column, seen
):
    wide_count = seen.shape[0]
    width = got_ref.shape[1]
    length = got_ref.shape[0] // (wide_count * near_count)
    half_size = near_count * rows
    upper = (lax.axis_index("narrow") >= near_count).astype(jnp.int32)
    near_at, far_at = upper * half_size, (1 - upper) * half_size
    tiles[...] = jnp.zeros_like(tiles)
    for u in range(recv_count):
        column[u] = 0

    def message(w, z):
        start = message_at(w, z, wide_count, near_count, length)
        if length % 16 == 0:
            block = got_ref[pl.ds(start, length)].astype(jnp.float32)
            return block[:rows], block[rows : 2 * rows]
        return got_ref[pl.ds(start, rows)], got_ref[pl.ds(start + rows, rows)]

    def read_label(w):
        start = message_at(w, 0, wide_count, near_count, length)
        if length % 16 == 0:
            label = got_ref[pl.ds(start, length)].astype(jnp.float32)[2 * rows :]
        else:
            label = got_ref[pl.ds(start + 2 * rows, length - 2 * rows)].astype(jnp.float32)
        return label[0, 0].astype(jnp.int32)

    def keep(w, label, found):
        live = jnp.minimum(label, 1)
        at = jnp.where(label > 0, jnp.minimum(found, recv_count), recv_count)
        code = jnp.maximum(label - 1, 0)
        column[at] = lax.div(code, own_count)
        spot = pl.ds(pl.multiple_of(lax.rem(code, own_count) * width, width), width)
        parts = [message(w, z) for z in range(near_count)]
        for side in range(2):
            order = parts if side == 0 else parts[::-1]
            half = jnp.concatenate([part[side] for part in order], axis=0).astype(tiles.dtype)
            start = at * width + (near_at if side == 0 else far_at)
            tiles[pl.ds(pl.multiple_of(start, half_size), half_size), spot] = half
        return found + live

    if wide_count <= UNROLL:
        labels = [read_label(w) for w in range(wide_count)]
        found = jnp.int32(0)
        for w in range(wide_count):
            found = keep(w, labels[w], found)
    else:

        def note(w, _):
            seen[w] = read_label(w)
            return 0

        lax.fori_loop(0, wide_count, note, 0)
        lax.fori_loop(0, wide_count, lambda w, found: keep(w, seen[w], found), jnp.int32(0))
    total = None
    for first in range(0, recv_count, GROUP):
        last = min(first + GROUP, recv_count)
        spots = [pl.multiple_of(column[u] * width, width) for u in range(first, last)]
        picked = jnp.concatenate([amp_ref[:, pl.ds(spot, width)] for spot in spots], axis=1)
        term = jnp.dot(
            picked, tiles[first * width : last * width], preferred_element_type=jnp.float32
        )
        total = term if total is None else total + term
    out_ref[...] = total


def shards(amplitudes, integrals, in_tile, counts, out_tile, owner_map):
    slot_count, rows, width = integrals.shape
    row_count = amplitudes.shape[0]
    wide_count = lax.axis_size("wide")
    depth_count = lax.axis_size("narrow")
    own_count = owner_map.shape[0] // wide_count
    recv_count = slot_count // 2
    near_count = depth_count // 2
    kind = integrals.dtype
    message_count = wide_count * near_count
    length = 2 * rows + PAIR
    if wide_count > UNROLL or length % PAIR != 0 or message_count * length % 16 != 0:
        length = -(-length // 16) * 16
    hbm = pl.BlockSpec(memory_space=pltpu.HBM)
    vmem = pl.BlockSpec(memory_space=pltpu.VMEM)
    limit = pltpu.CompilerParams(vmem_limit_bytes=32 * 2**20)
    across = [(z, depth_count - 1 - z) for z in range(depth_count)]
    far = lax.ppermute(integrals, "narrow", across)
    given = [in_tile, counts, out_tile, owner_map, integrals]
    given = [
        value if value.size == 1 else pltpu.with_memory_space_constraint(value, pltpu.HBM)
        for value in given
    ]
    ordered, sent = wide_count * rows, slot_count * rows
    order, labels, near = pl.pallas_call(
        functools.partial(route_kernel, own_count, wide_count),
        out_shape=[
            jax.ShapeDtypeStruct((ordered, sent), kind),
            jax.ShapeDtypeStruct((wide_count, width), kind),
            jax.ShapeDtypeStruct(integrals.shape, kind),
        ],
        in_specs=[hbm] * len(given),
        out_specs=[vmem] * 3,
        scratch_shapes=[pltpu.SMEM(value.shape, value.dtype) for value in given[:-1]]
        + [pltpu.SemaphoreType.DMA((len(given),))],
        compiler_params=limit,
        cost_estimate=pl.CostEstimate(flops=2**30, bytes_accessed=2**20, transcendentals=0),
        name="route",
    )(*given)
    send = pl.pallas_call(
        functools.partial(pack_kernel, wide_count, near_count),
        out_shape=jax.ShapeDtypeStruct((message_count * length, width), kind),
        in_specs=[vmem] * 4,
        out_specs=vmem,
        scratch_shapes=[
            pltpu.VMEM((sent, 2 * width), kind),
            pltpu.VMEM((ordered, 2 * width), jnp.float32),
        ],
        compiler_params=limit,
        name="pack",
    )(order, labels, near, far)
    places = group_places(wide_count, near_count)
    groups = [
        [w * depth_count + half * near_count + z for w, z in places] for half in range(2)
    ]
    got = lax.all_to_all(
        send.reshape(message_count, length // PAIR, PAIR, width),
        ("wide", "narrow"),
        split_axis=0,
        concat_axis=0,
        tiled=True,
        axis_index_groups=groups,
    ).reshape(message_count * length, width)
    return pl.pallas_call(
        functools.partial(ladder_kernel, rows, near_count, own_count, recv_count),
        out_shape=jax.ShapeDtypeStruct((row_count, own_count * width), jnp.float32),
        in_specs=[vmem] * 2,
        out_specs=vmem,
        scratch_shapes=[
            pltpu.VMEM(((recv_count + 1) * width, own_count * width), kind),
            pltpu.SMEM((recv_count + 1,), jnp.int32),
            pltpu.SMEM((wide_count,), jnp.int32),
        ],
        compiler_params=limit,
        name="ladder",
    )(amplitudes, got)


def solution(mesh):
    return jax.shard_map(
        shards,
        mesh=mesh,
        in_specs=(
            P("narrow", None),
            P("wide", "narrow", None),
            P("wide"),
            P("wide"),
            P("wide"),
            P(),
        ),
        out_specs=P("narrow", "wide"),
        check_vma=False,
    )
```

```python
import functools

import jax
import jax.numpy as jnp
from jax import lax
from jax.experimental import pallas as pl
from jax.experimental.pallas import tpu as pltpu
from jax.sharding import PartitionSpec as P

PAIR = 2
GROUP = 4
UNROLL = 8
CORES = 2


def each(count, body, start):
    if count > UNROLL:
        return lax.fori_loop(0, count, body, start)
    for i in range(count):
        start = body(i, start)
    return start


def chip_order(wide_count):
    chip_count = wide_count // CORES
    if wide_count > UNROLL:
        return list(range(chip_count))
    bits = (chip_count - 1).bit_length()
    flipped = [int(format(chip, "b").zfill(bits)[::-1], 2) for chip in range(2**bits)]
    return [chip for chip in flipped[1:] if chip < chip_count] + [0]


def group_places(wide_count, near_count):
    cores = list(reversed(range(CORES)))
    depths = list(reversed(range(near_count)))
    return [(chip * CORES + core, z) for chip in chip_order(wide_count) for z in depths for core in cores]


def message_at(w, z, wide_count, near_count, length):
    if isinstance(w, int):
        return group_places(wide_count, near_count).index((w, z)) * length
    place = (w // CORES * near_count + near_count - 1 - z) * CORES + CORES - 1 - w % CORES
    return pl.multiple_of(place * length, length)


def route_kernel(own_count, wide_count, *refs):
    sources, (order_ref, label_ref, near_ref), targets, sems = refs[:5], refs[5:8], refs[8:12], refs[12]
    in_tile, counts, out_tile, owner_map = targets
    copies = [
        pltpu.make_async_copy(source, target, sems.at[i])
        for i, (source, target) in enumerate(zip(sources, (*targets, near_ref)))
    ]
    for copy in copies:
        copy.start()
    for copy in copies[:4]:
        copy.wait()
    slot_count, rows, width = near_ref.shape
    column = lax.broadcasted_iota(jnp.int32, (1, slot_count * rows), 1)
    owners = lax.broadcasted_iota(jnp.int32, (wide_count, width), 0)

    def route(h, carry):
        owner_of, labels = carry
        spot = owner_map[out_tile[h]]
        owner = lax.div(spot, own_count)
        label = in_tile[h] * own_count + lax.rem(spot, own_count) + 1
        label = jnp.where(h < counts[0], label, 0)
        owner_of = jnp.where(lax.div(column, rows) == h, owner, owner_of)
        return owner_of, jnp.where(owners == owner, label, labels)

    start = (jnp.zeros_like(column), jnp.zeros((wide_count, width), jnp.int32))
    owner_of, labels = each(slot_count, route, start)
    label_ref[...] = labels.astype(jnp.float32).astype(label_ref.dtype)
    row = lax.broadcasted_iota(jnp.int32, (wide_count * rows, 1), 0)
    hit = row == owner_of * rows + lax.rem(column, rows)
    order_ref[...] = hit.astype(jnp.float32).astype(order_ref.dtype)
    copies[4].wait()


def pack_kernel(wide_count, near_count, order_ref, label_ref, near_ref, far_ref, send_ref, both, ordered):
    slot_count, rows, width = near_ref.shape
    length = send_ref.shape[0] // (wide_count * near_count)
    for side, ref in enumerate((near_ref, far_ref)):
        block = ref[...]
        if rows % 16 != 0:
            block = block.astype(jnp.float32)
        block = block.reshape(slot_count * rows, width).astype(both.dtype)
        both[:, side * width : (side + 1) * width] = block
    ordered[...] = jnp.dot(order_ref[...], both[...], preferred_element_type=jnp.float32)
    labels = label_ref[...].astype(jnp.float32)
    ids = lax.broadcasted_iota(jnp.int32, labels.shape, 0)

    def write(owner, _):
        spot = owner * rows
        if not isinstance(owner, int):
            spot = pl.multiple_of(spot, rows)
        near = ordered[pl.ds(spot, rows), :width]
        far = ordered[pl.ds(spot, rows), width:]
        label = jnp.sum(jnp.where(ids == owner, labels, 0.0), axis=0, keepdims=True)
        label = jnp.broadcast_to(label, (length - 2 * rows, width))
        if length % 16 == 0:
            pieces = [(0, jnp.concatenate([near, far, label], axis=0))]
        else:
            pieces = [(0, near), (rows, far), (2 * rows, label)]
        for z in range(near_count):
            start = message_at(owner, z, wide_count, near_count, length)
            for offset, piece in pieces:
                send_ref[pl.ds(start + offset, piece.shape[0])] = piece.astype(send_ref.dtype)
        return 0

    each(wide_count, write, 0)


def ladder_kernel(
    rows, near_count, own_count, recv_count, amp_ref, got_ref, out_ref, tiles, column, seen
):
    wide_count = seen.shape[0]
    width = got_ref.shape[1]
    length = got_ref.shape[0] // (wide_count * near_count)
    half_size = near_count * rows
    upper = (lax.axis_index("narrow") >= near_count).astype(jnp.int32)
    near_at, far_at = upper * half_size, (1 - upper) * half_size
    tiles[...] = jnp.zeros_like(tiles)
    for u in range(recv_count):
        column[u] = 0

    def message(w, z):
        start = message_at(w, z, wide_count, near_count, length)
        if length % 16 == 0:
            block = got_ref[pl.ds(start, length)].astype(jnp.float32)
            return block[:rows], block[rows : 2 * rows]
        return got_ref[pl.ds(start, rows)], got_ref[pl.ds(start + rows, rows)]

    def read_label(w):
        start = message_at(w, 0, wide_count, near_count, length)
        if length % 16 == 0:
            label = got_ref[pl.ds(start, length)].astype(jnp.float32)[2 * rows :]
        else:
            label = got_ref[pl.ds(start + 2 * rows, length - 2 * rows)].astype(jnp.float32)
        return label[0, 0].astype(jnp.int32)

    def keep(w, label, found):
        live = jnp.minimum(label, 1)
        at = jnp.where(label > 0, jnp.minimum(found, recv_count), recv_count)
        code = jnp.maximum(label - 1, 0)
        column[at] = lax.div(code, own_count)
        spot = pl.ds(pl.multiple_of(lax.rem(code, own_count) * width, width), width)
        parts = [message(w, z) for z in range(near_count)]
        for side in range(2):
            order = parts if side == 0 else parts[::-1]
            half = jnp.concatenate([part[side] for part in order], axis=0).astype(tiles.dtype)
            start = at * width + (near_at if side == 0 else far_at)
            tiles[pl.ds(pl.multiple_of(start, half_size), half_size), spot] = half
        return found + live

    if wide_count <= UNROLL:
        labels = [read_label(w) for w in range(wide_count)]
        found = jnp.int32(0)
        for w in range(wide_count):
            found = keep(w, labels[w], found)
    else:

        def note(w, _):
            seen[w] = read_label(w)
            return 0

        lax.fori_loop(0, wide_count, note, 0)
        lax.fori_loop(0, wide_count, lambda w, found: keep(w, seen[w], found), jnp.int32(0))
    total = None
    for first in range(0, recv_count, GROUP):
        last = min(first + GROUP, recv_count)
        spots = [pl.multiple_of(column[u] * width, width) for u in range(first, last)]
        picked = jnp.concatenate([amp_ref[:, pl.ds(spot, width)] for spot in spots], axis=1)
        term = jnp.dot(
            picked, tiles[first * width : last * width], preferred_element_type=jnp.float32
        )
        total = term if total is None else total + term
    out_ref[...] = total


def shards(amplitudes, integrals, in_tile, counts, out_tile, owner_map):
    slot_count, rows, width = integrals.shape
    row_count = amplitudes.shape[0]
    wide_count = lax.axis_size("wide")
    depth_count = lax.axis_size("narrow")
    own_count = owner_map.shape[0] // wide_count
    recv_count = slot_count // 2
    near_count = depth_count // 2
    kind = integrals.dtype
    message_count = wide_count * near_count
    length = 2 * rows + PAIR
    if wide_count > UNROLL or length % PAIR != 0 or message_count * length % 16 != 0:
        length = -(-length // 16) * 16
    hbm = pl.BlockSpec(memory_space=pltpu.HBM)
    vmem = pl.BlockSpec(memory_space=pltpu.VMEM)
    limit = pltpu.CompilerParams(vmem_limit_bytes=32 * 2**20)
    across = [(z, depth_count - 1 - z) for z in range(depth_count)]
    far = lax.ppermute(integrals, "narrow", across)
    given = [in_tile, counts, out_tile, owner_map, integrals]
    given = [
        value if value.size == 1 else pltpu.with_memory_space_constraint(value, pltpu.HBM)
        for value in given
    ]
    ordered, sent = wide_count * rows, slot_count * rows
    order, labels, near = pl.pallas_call(
        functools.partial(route_kernel, own_count, wide_count),
        out_shape=[
            jax.ShapeDtypeStruct((ordered, sent), kind),
            jax.ShapeDtypeStruct((wide_count, width), kind),
            jax.ShapeDtypeStruct(integrals.shape, kind),
        ],
        in_specs=[hbm] * len(given),
        out_specs=[vmem] * 3,
        scratch_shapes=[pltpu.SMEM(value.shape, value.dtype) for value in given[:-1]]
        + [pltpu.SemaphoreType.DMA((len(given),))],
        compiler_params=limit,
        cost_estimate=pl.CostEstimate(flops=2**30, bytes_accessed=2**20, transcendentals=0),
        name="route",
    )(*given)
    send = pl.pallas_call(
        functools.partial(pack_kernel, wide_count, near_count),
        out_shape=jax.ShapeDtypeStruct((message_count * length, width), kind),
        in_specs=[vmem] * 4,
        out_specs=vmem,
        scratch_shapes=[
            pltpu.VMEM((sent, 2 * width), kind),
            pltpu.VMEM((ordered, 2 * width), jnp.float32),
        ],
        compiler_params=limit,
        name="pack",
    )(order, labels, near, far)
    places = group_places(wide_count, near_count)
    groups = [
        [w * depth_count + half * near_count + z for w, z in places] for half in range(2)
    ]
    got = lax.all_to_all(
        send.reshape(message_count, length // PAIR, PAIR, width),
        ("wide", "narrow"),
        split_axis=0,
        concat_axis=0,
        tiled=True,
        axis_index_groups=groups,
    ).reshape(message_count * length, width)
    return pl.pallas_call(
        functools.partial(ladder_kernel, rows, near_count, own_count, recv_count),
        out_shape=jax.ShapeDtypeStruct((row_count, own_count * width), jnp.float32),
        in_specs=[vmem] * 2,
        out_specs=vmem,
        scratch_shapes=[
            pltpu.VMEM(((recv_count + 1) * width, own_count * width), kind),
            pltpu.SMEM((recv_count + 1,), jnp.int32),
            pltpu.SMEM((wide_count,), jnp.int32),
        ],
        compiler_params=limit,
        name="ladder",
    )(amplitudes, got)


def solution(mesh):
    return jax.shard_map(
        shards,
        mesh=mesh,
        in_specs=(
            P("narrow", None),
            P("wide", "narrow", None),
            P("wide"),
            P("wide"),
            P("wide"),
            P(),
        ),
        out_specs=P("narrow", "wide"),
        check_vma=False,
    )
```
